32 devices in a mesh: grp: 4 (over y, x), feat: 8 (over z, core).
Axes of the slice: x: 2, y: 2, z: 4, core: 2. Of those that a mesh axis runs over, the one named last changes fastest.
Arguments:
- resid: bfloat16 [4, 512, 2304], P(None, 'grp'), may hold values from -6 to 6
- w_enc: bfloat16 [4, 2304, 8192], P(None, None, 'feat'), may hold values from -0.125 to 0.125
- b_enc: float32 [4, 8192], P(None, 'feat'), may hold values from -3 to 3
- w_dec: bfloat16 [4, 4, 8192, 2304], P(None, 'grp', 'feat'), may hold values from -0.0625 to 0.0625
- targets: bfloat16 [4, 512, 2304], P('grp'), may hold values from -6 to 6
- start_layer: int32 [4, 8], P(None, 'feat'), may hold values from 0 to 3, as said below
Outputs:
- active: bfloat16 [512, 4, 8192], P('grp', None, 'feat')
- recon: bfloat16 [4, 512, 2304], P('grp', 'feat')
- recon_loss: float32 [], replicated
- feat_grad: float32 [512, 4, 8192], P('grp', None, 'feat')
The draws below stay inside these ranges and needn't reach their ends.
Inputs may be any that keep to these rules, and one draw needn't show every extreme that they name: `start_layer`: each column is nondecreasing over source layers; in every column the first source feeds from target 0 and the last source feeds only target 4 - 1.
All inputs are finite; a program needn't handle non-finite values.
Results may differ from the reference program's by a relative error of at most 0.0049.
Values may be sent and summed in bfloat16 or wider, within the bound.
No kernel may reach another device: no remote copies, remote signals or barrier semaphores. Data moves between devices by JAX's collectives and lax.ppermute only.
A program may use at most 128 MiB of HBM per device.

```python
import jax
import jax.numpy as jnp
from jax import lax

D = 2304
F = 8192
L_SRC = 4
TOK = 512
L_TGT = 4
N_FEAT = 8


def draw_start_layer(key, part):
    middle = jnp.sort(jax.random.randint(key, (L_SRC - 2, N_FEAT), 0, L_TGT), axis=0).astype(jnp.int32)
    first_row = jnp.zeros((1, N_FEAT), jnp.int32)
    last_row = jnp.full((1, N_FEAT), L_TGT - 1, jnp.int32)
    return jnp.concatenate([first_row, middle, last_row], axis=0)


def levels(rng, dims, shards, smallest, largest):
    level = 1.0
    for dim, parts in shards:
        steps = jax.random.uniform(jax.random.fold_in(jax.random.fold_in(rng, 6), dim), (parts,), jnp.float32, smallest / len(shards), largest / len(shards))
        level = level * jnp.repeat(jnp.exp(steps), dims[dim] // parts).reshape((-1,) + (1,) * (len(dims) - 1 - dim))
    return level


def bell_draw(key, extent, width, bound, shards=(), kind=jnp.bfloat16):
    result = jax.random.normal(key, extent, jnp.float32) * width
    if len(shards) > 0:
        result = levels(key, extent, shards, -0.22, 0.18) * result
    return jnp.clip(result, min=-bound, max=bound).astype(kind)


def setup_inputs(seed: int = 0) -> dict:
    keys = jax.random.split(jax.random.key(seed), 7)
    return {
        "resid": bell_draw(keys[0], (L_SRC, TOK, D), 1.0, 6.0, ((1, 4),)),
        "w_enc": bell_draw(keys[1], (L_SRC, D, F), D ** -0.5, 0.125, ((2, 8),)),
        "b_enc": bell_draw(keys[2], (L_SRC, F), 0.5, 3.0, ((1, 8),), jnp.float32),
        "w_dec": bell_draw(keys[3], (L_SRC, L_TGT, F, D), F ** -0.5, 0.0625, ((1, 4), (2, 8))),
        "targets": bell_draw(keys[4], (L_TGT, TOK, D), 1.0, 6.0, ((0, 4),)),
        "start_layer": draw_start_layer(jax.random.fold_in(keys[6], 71), 0),
    }


def feeding(start_layer):
    target_ids = jnp.arange(L_TGT, dtype=jnp.int32)
    return (target_ids[None, :, None] >= start_layer[:, None, :]).astype(jnp.float32)


def reference(resid, w_enc, b_enc, w_dec, targets, start_layer):
    feeds_mask = feeding(start_layer)
    encoded = []
    for source in range(L_SRC):
        pre_act = jnp.dot(resid[source], w_enc[source], preferred_element_type=jnp.float32) + b_enc[source]
        encoded.append(jnp.maximum(pre_act, 0.0).astype(jnp.bfloat16))
    active = jnp.stack(encoded, axis=1)
    block_width = F // N_FEAT
    recon_list = []
    for target in range(L_TGT):
        def add_block(index, summed):
            first_col = (index * block_width).astype(jnp.int32)
            columns = lax.dynamic_slice_in_dim(active, first_col, block_width, 2)
            weights = lax.dynamic_slice_in_dim(w_dec[:, target], first_col, block_width, 1)
            block_mask = lax.dynamic_index_in_dim(feeds_mask[:, target, :], index, 1, False)
            term = jnp.zeros((TOK, D), jnp.float32)
            for source in range(L_SRC):
                term = term + block_mask[source] * jnp.dot(columns[:, source], weights[source], preferred_element_type=jnp.float32)
            return summed + term
        recon_list.append(lax.fori_loop(0, N_FEAT, add_block, jnp.zeros((TOK, D), jnp.float32)))
    recon_full = jnp.stack(recon_list, axis=0)
    difference = recon_full - targets.astype(jnp.float32)
    error_rows = difference.astype(jnp.bfloat16)
    recon_loss = jnp.sum(difference * difference) / (L_TGT * TOK * D)
    gradients = []
    for source in range(L_SRC):
        summed = jnp.zeros((TOK, F), jnp.float32)
        for target in range(L_TGT):
            column_mask = jnp.repeat(feeds_mask[source, target], block_width)
            summed = summed + column_mask[None, :] * lax.dot_general(error_rows[target], w_dec[source, target], (((1,), (1,)), ((), ())), preferred_element_type=jnp.float32)
        gradients.append(summed)
    feat_grad = jnp.stack(gradients, axis=1)
    return active, recon_full.astype(jnp.bfloat16), recon_loss, feat_grad
```

```python
from functools import partial

import jax
import jax.numpy as jnp
from jax import lax
from jax.experimental import pallas as pl
from jax.experimental.pallas import tpu as pltpu
from jax.sharding import PartitionSpec as P

BF16 = jnp.bfloat16
F32 = jnp.float32
WANTED_CHUNKS = 2
ROW_TILE = 16


def pick_tile(size, wanted):
    if size % wanted:
        return size
    return wanted


def swap(x, axis, size, offset):
    return lax.ppermute(x, axis, [(i, i ^ offset) for i in range(size)])


class Plan:
    def __init__(self, resid, w_dec):
        self.sources, self.rows, self.model = resid.shape
        self.width = w_dec.shape[2]
        self.groups = lax.axis_size("grp")
        self.feats = lax.axis_size("feat")
        self.depth = self.feats // 2
        self.tokens = self.rows * self.groups
        self.rows_feat = self.tokens // self.feats
        self.per_group = self.rows // self.rows_feat
        self.pairs = self.per_group // 2
        self.chunks = WANTED_CHUNKS
        while self.rows_feat % (self.chunks * ROW_TILE):
            self.chunks -= 1
        self.piece = self.rows_feat // self.chunks
        self.block = self.per_group * self.piece
        bits = [1 << i for i in range(self.groups.bit_length() - 1)]
        self.lanes = [bits[i:] + bits[:i] for i in range(len(bits))]
        starts = [i * self.sources // len(bits) for i in range(len(bits) + 1)]
        self.lane_sources = list(zip(starts[:-1], starts[1:]))


def encode_kernel(plan, resid_ref, w_ref, b_ref, *outs):
    product = jnp.dot(resid_ref[0], w_ref[0], preferred_element_type=F32)
    value = jnp.maximum(product + b_ref[0], 0.0).astype(BF16)
    outs[-1][0] = value
    for c in range(plan.chunks):
        for b in range(plan.per_group):
            first = (b * plan.chunks + c) * plan.piece
            outs[c][0, b * plan.piece:(b + 1) * plan.piece, :] = value[first:first + plan.piece]


def encode(plan, lane, resid, w_enc, b_enc):
    lo, hi = plan.lane_sources[lane]
    n = hi - lo
    tile = pick_tile(plan.width, 256)
    out_shape = [jax.ShapeDtypeStruct((n, plan.block, plan.width), BF16)] * plan.chunks
    out_shape.append(jax.ShapeDtypeStruct((n, plan.rows, plan.width), BF16))
    out_specs = [pl.BlockSpec((1, plan.block, tile), lambda s, j: (s, 0, j))] * plan.chunks
    out_specs.append(pl.BlockSpec((1, plan.rows, tile), lambda s, j: (s, 0, j)))
    return pl.pallas_call(
        partial(encode_kernel, plan),
        grid=(n, plan.width // tile),
        in_specs=[
            pl.BlockSpec((1, plan.rows, plan.model), lambda s, j: (s + lo, 0, 0)),
            pl.BlockSpec((1, plan.model, tile), lambda s, j: (s + lo, 0, j)),
            pl.BlockSpec((1, 1, tile), lambda s, j: (s + lo, 0, j)),
        ],
        out_specs=out_specs,
        out_shape=out_shape,
        cost_estimate=pl.CostEstimate(
            flops=2 * n * plan.rows * plan.model * plan.width,
            bytes_accessed=2 * n * plan.model * plan.width,
            transcendentals=0,
        ),
        compiler_params=pltpu.CompilerParams(vmem_limit_bytes=32 << 20),
        name="encode",
    )(resid, w_enc, b_enc[:, None, :])


def decode_kernel(plan, index_ref, *refs):
    n_in = plan.groups * len(plan.lanes)
    pieces, w_ref, send_ref, keep_ref, x_ref = refs[:n_in], refs[n_in], *refs[n_in + 1:]
    half = plan.groups * plan.pairs * plan.piece
    core = index_ref[0]

    @pl.when(pl.program_id(0) == 0)
    def _():
        for lane, (lo, hi) in enumerate(plan.lane_sources):
            for s in range(lo, hi):
                feeds = index_ref[1 + s] > 0
                for j in range(plan.groups):
                    ref = pieces[lane * plan.groups + j]
                    for b in range(plan.pairs):
                        for h in range(2):
                            owner = 1 - core if h == 0 else core
                            first = pl.multiple_of((2 * b + owner) * plan.piece, ROW_TILE)
                            rows = ref[s - lo, pl.ds(first, plan.piece), :]
                            to = h * half + (j * plan.pairs + b) * plan.piece
                            x_ref[to:to + plan.piece, s * plan.width:(s + 1) * plan.width] = (
                                jnp.where(feeds, rows, jnp.zeros_like(rows))
                            )

    w = w_ref[:, 0].reshape(plan.sources * plan.width, w_ref.shape[3])
    product = jnp.dot(x_ref[...], w, preferred_element_type=F32)
    send_ref[...] = product[:half].astype(BF16)
    keep_ref[...] = product[half:]


def decode(plan, index, pieces, w_dec):
    tile = pick_tile(plan.model, 256)
    half = plan.groups * plan.pairs * plan.piece
    whole = pl.BlockSpec(memory_space=pltpu.VMEM)
    depth = plan.sources * plan.width
    return pl.pallas_call(
        partial(decode_kernel, plan),
        grid=(plan.model // tile,),
        in_specs=[pl.BlockSpec(memory_space=pltpu.SMEM)]
        + [whole] * len(pieces)
        + [pl.BlockSpec((plan.sources, 1, plan.width, tile), lambda j: (0, 0, 0, j))],
        out_specs=[pl.BlockSpec((half, tile), lambda j: (0, j))] * 2,
        out_shape=[
            jax.ShapeDtypeStruct((half, plan.model), BF16),
            jax.ShapeDtypeStruct((half, plan.model), F32),
        ],
        scratch_shapes=[pltpu.VMEM((2 * half, depth), BF16)],
        cost_estimate=pl.CostEstimate(
            flops=4 * half * depth * plan.model,
            bytes_accessed=2 * depth * plan.model,
            transcendentals=0,
        ),
        compiler_params=pltpu.CompilerParams(vmem_limit_bytes=32 << 20),
        name="decode",
    )(index, *pieces, w_dec)


def lane_order(plan, lane):
    first, rest = plan.lanes[lane][0], plan.lanes[lane][1:]
    kept = [0]
    for bit in reversed(rest):
        kept = [j | bit for j in kept] + kept
    return first, kept


def gradient_kernel(plan, lane, index_ref, *refs):
    n_in = 2 * plan.depth
    errors, w_ref, outs, e_ref = refs[:n_in], refs[n_in], refs[n_in + 1:-1], refs[-1]
    lo, hi = plan.lane_sources[lane]
    first, kept = lane_order(plan, lane)

    @pl.when((pl.program_id(0) == 0) & (pl.program_id(1) == 0))
    def _():
        for i in range(n_in):
            at = pl.multiple_of(index_ref[1 + plan.sources + i] * plan.piece, ROW_TILE)
            e_ref[pl.ds(at, plan.piece), :] = errors[i][...]

    product = lax.dot_general(
        e_ref[...], w_ref[0, 0], (((1,), (1,)), ((), ())), preferred_element_type=F32
    )
    feeds = index_ref[1 + lo + pl.program_id(0)] > 0
    product = jnp.where(feeds, product, 0.0)
    n = len(kept)
    for p, j in enumerate(kept):
        away = (j ^ first) * plan.block
        outs[p][0] = product[away:away + plan.block].astype(BF16)
        outs[n + p][0] = product[j * plan.block:(j + 1) * plan.block]


def gradient(plan, lane, index, errors, w_dec):
    lo, hi = plan.lane_sources[lane]
    n = hi - lo
    tile = pick_tile(plan.width, 256)
    half = plan.groups // 2
    shape = (n, plan.block, plan.width)
    whole = pl.BlockSpec(memory_space=pltpu.VMEM)
    rows = plan.groups * plan.block
    outs = pl.pallas_call(
        partial(gradient_kernel, plan, lane),
        grid=(n, plan.width // tile),
        in_specs=[pl.BlockSpec(memory_space=pltpu.SMEM)]
        + [whole] * len(errors)
        + [pl.BlockSpec((1, 1, tile, plan.model), lambda s, j: (s + lo, 0, j, 0))],
        out_specs=[pl.BlockSpec((1, plan.block, tile), lambda s, j: (s, 0, j))] * (2 * half),
        out_shape=[jax.ShapeDtypeStruct(shape, BF16)] * half
        + [jax.ShapeDtypeStruct(shape, F32)] * half,
        scratch_shapes=[pltpu.VMEM((rows, plan.model), BF16)],
        cost_estimate=pl.CostEstimate(
            flops=2 * n * rows * plan.model * plan.width,
            bytes_accessed=2 * n * plan.model * plan.width,
            transcendentals=0,
        ),
        compiler_params=pltpu.CompilerParams(vmem_limit_bytes=32 << 20),
        name="gradient",
    )(index, *errors, w_dec)
    return outs[:half], outs[half:]


def per_device(resid, w_enc, b_enc, w_dec, targets, start_layer):
    plan = Plan(resid, w_dec)
    group = lax.axis_index("grp").astype(jnp.int32)
    feat = lax.axis_index("feat").astype(jnp.int32)
    core, level = feat % 2, feat // 2
    groups, feats = plan.groups, plan.feats

    def block_of(level_to):
        return ((level_to // plan.pairs) ^ group) * plan.pairs + level_to % plan.pairs

    feeds = (group >= start_layer[:, 0]).astype(jnp.int32)
    places = [block_of(level ^ d) * 2 + core for d in range(plan.depth)]
    places += [block_of(level ^ d) * 2 + 1 - core for d in range(plan.depth)]
    index = jnp.concatenate([core[None], feeds, jnp.stack(places)])

    encoded = [encode(plan, i, resid, w_enc, b_enc) for i in range(len(plan.lanes))]
    active = jnp.stack(
        [e[-1][s] for e in encoded for s in range(e[-1].shape[0])], axis=1
    )

    gathered = []
    for c in range(plan.chunks):
        pieces = []
        for lane, bits in enumerate(plan.lanes):
            held = {0: encoded[lane][c]}
            for bit in bits:
                held.update(
                    {j | bit: swap(x, "grp", groups, bit) for j, x in list(held.items())}
                )
            pieces += [held[j] for j in range(groups)]
        gathered.append(pieces)

    recon_parts, squares = [], 0.0
    lane_results = [[] for _ in plan.lanes]
    for c in range(plan.chunks):
        send, keep = decode(plan, index, gathered[c], w_dec)
        other = swap(send, "feat", feats, 1)

        def part(level_to):
            first = block_of(level_to) * plan.piece
            mine = lax.dynamic_slice_in_dim(keep, first, plan.piece, 0)
            theirs = lax.dynamic_slice_in_dim(other, first, plan.piece, 0)
            return mine + theirs.astype(F32)

        arrived = [
            swap(part(level ^ d).astype(BF16), "feat", feats, 2 * d)
            for d in range(plan.depth - 1, 0, -1)
        ]
        recon_rows = part(level)
        for rows in arrived:
            recon_rows = recon_rows + rows.astype(F32)
        first = feat * plan.rows_feat + c * plan.piece
        own_targets = lax.dynamic_slice_in_dim(targets[0], first, plan.piece, 0)
        difference = recon_rows - own_targets.astype(F32)
        recon_parts.append(recon_rows.astype(BF16))
        squares = squares + jnp.sum(difference * difference)

        error = difference.astype(BF16)
        errors = [error] + [
            swap(error, "feat", feats, 2 * d) for d in range(1, plan.depth)
        ]
        errors += [swap(e, "feat", feats, 1) for e in errors]

        for lane, bits in enumerate(plan.lanes):
            away, kept = gradient(plan, lane, index, errors, w_dec)
            for step, bit in enumerate(bits):
                got = [swap(x, "grp", groups, bit) for x in away]
                total = [x + y.astype(F32) for x, y in zip(kept, got)]
                cut = len(total) // 2
                away = [x.astype(BF16) for x in total[:cut]]
                kept = total[cut:]
            lane_results[lane].append(total[0])

    loss = jnp.full((8, 128), squares, F32)
    for bit in (1 << i for i in range(feats.bit_length() - 1)):
        loss = loss + swap(loss, "feat", feats, bit)
    for bit in (1 << i for i in range(groups.bit_length() - 1)):
        loss = loss + swap(loss, "grp", groups, bit)
    entries = targets.shape[0] * groups * plan.tokens * plan.model
    recon_loss = loss[0, 0] / entries

    recon = jnp.concatenate(recon_parts, axis=0)[None]
    per_source = []
    for lane, (lo, hi) in enumerate(plan.lane_sources):
        parts = [
            r.reshape(hi - lo, plan.per_group, 1, plan.piece, plan.width)
            for r in lane_results[lane]
        ]
        per_source.append(
            jnp.concatenate(parts, axis=2).reshape(hi - lo, plan.rows, plan.width)
        )
    feat_grad = jnp.concatenate(per_source, axis=0).transpose(1, 0, 2)
    return active, recon, recon_loss, feat_grad


def solution(mesh):
    in_specs = (
        P(None, "grp", None),
        P(None, None, "feat"),
        P(None, "feat"),
        P(None, "grp", "feat", None),
        P("grp", None, None),
        P(None, "feat"),
    )
    out_specs = (P("grp", None, "feat"), P("grp", "feat", None), P(), P("grp", None, "feat"))
    return jax.shard_map(
        per_device, mesh=mesh, in_specs=in_specs, out_specs=out_specs, check_vma=False
    )
```

```python
from functools import partial

import jax
import jax.numpy as jnp
from jax import lax
from jax.experimental import pallas as pl
from jax.experimental.pallas import tpu as pltpu
from jax.sharding import PartitionSpec as P

BF16 = jnp.bfloat16
F32 = jnp.float32
WANTED_CHUNKS = 2
ROW_TILE = 16
VMEM_BYTES = 46 << 20
SMALL_COST = pl.CostEstimate(flops=1 << 20, bytes_accessed=1 << 10, transcendentals=0)


def pick_tile(size, wanted):
    if size % wanted:
        return size
    return wanted


def swap(x, axis, size, offset):
    return lax.ppermute(x, axis, [(i, i ^ offset) for i in range(size)])


def after(values, earlier):
    if not earlier:
        return list(values)
    return list(lax.optimization_barrier(list(values) + list(earlier)))[:len(values)]


class Plan:
    def __init__(self, resid, w_dec):
        self.sources, self.rows, self.model = resid.shape
        self.width = w_dec.shape[2]
        self.groups = lax.axis_size("grp")
        self.feats = lax.axis_size("feat")
        self.depth = self.feats // 2
        self.tokens = self.rows * self.groups
        self.rows_feat = self.tokens // self.feats
        self.per_group = self.rows // self.rows_feat
        self.pairs = self.per_group // 2
        self.chunks = WANTED_CHUNKS
        while self.rows_feat % (self.chunks * ROW_TILE):
            self.chunks -= 1
        self.piece = self.rows_feat // self.chunks
        self.block = self.per_group * self.piece
        bits = [1 << i for i in range(self.groups.bit_length() - 1)]
        self.lanes = [bits[i:] + bits[:i] for i in range(len(bits))]
        starts = [i * self.sources // len(bits) for i in range(len(bits) + 1)]
        self.lane_sources = list(zip(starts[:-1], starts[1:]))


def encode_kernel(plan, first_source, resid_ref, w_ref, b_ref, *outs):
    product = jnp.dot(resid_ref[0], w_ref[0], preferred_element_type=F32)
    bias = b_ref[pl.ds(first_source + pl.program_id(0), 1), :]
    value = jnp.maximum(product + bias, 0.0).astype(BF16)
    outs[-1][0] = value
    for c in range(plan.chunks):
        for b in range(plan.per_group):
            first = (b * plan.chunks + c) * plan.piece
            outs[c][0, b * plan.piece:(b + 1) * plan.piece, :] = value[first:first + plan.piece]


def encode(plan, lane, resid, w_enc, b_enc):
    lo, hi = plan.lane_sources[lane]
    n = hi - lo
    tile = pick_tile(plan.width, 256)
    out_shape = [jax.ShapeDtypeStruct((n, plan.block, plan.width), BF16)] * plan.chunks
    out_shape.append(jax.ShapeDtypeStruct((n, plan.rows, plan.width), BF16))
    out_specs = [pl.BlockSpec((1, plan.block, tile), lambda s, j: (s, 0, j))] * plan.chunks
    out_specs.append(pl.BlockSpec((1, plan.rows, tile), lambda s, j: (s, 0, j)))
    return pl.pallas_call(
        partial(encode_kernel, plan, lo),
        grid=(n, plan.width // tile),
        in_specs=[
            pl.BlockSpec((1, plan.rows, plan.model), lambda s, j: (s + lo, 0, 0)),
            pl.BlockSpec((1, plan.model, tile), lambda s, j: (s + lo, 0, j)),
            pl.BlockSpec((plan.sources, tile), lambda s, j: (0, j)),
        ],
        out_specs=out_specs,
        out_shape=out_shape,
        cost_estimate=SMALL_COST,
        compiler_params=pltpu.CompilerParams(vmem_limit_bytes=VMEM_BYTES),
        name="encode",
    )(resid, w_enc, b_enc)


def decode_kernel(plan, index_ref, *refs):
    n_in = plan.groups * len(plan.lanes)
    pieces, w_ref, send_ref, keep_ref, x_ref = refs[:n_in], refs[n_in], *refs[n_in + 1:]
    half = plan.groups * plan.pairs * plan.piece
    core = index_ref[0]

    @pl.when(pl.program_id(0) == 0)
    def _():
        for lane, (lo, hi) in enumerate(plan.lane_sources):
            for s in range(lo, hi):
                feeds = index_ref[1 + s] > 0
                for j in range(plan.groups):
                    ref = pieces[lane * plan.groups + j]
                    for b in range(plan.pairs):
                        for h in range(2):
                            owner = 1 - core if h == 0 else core
                            first = pl.multiple_of((2 * b + owner) * plan.piece, ROW_TILE)
                            rows = ref[s - lo, pl.ds(first, plan.piece), :]
                            to = h * half + (j * plan.pairs + b) * plan.piece
                            x_ref[to:to + plan.piece, s * plan.width:(s + 1) * plan.width] = (
                                jnp.where(feeds, rows, jnp.zeros_like(rows))
                            )

    w = w_ref[:, 0].reshape(plan.sources * plan.width, w_ref.shape[3])
    product = jnp.dot(x_ref[...], w, preferred_element_type=F32)
    send_ref[...] = product[:half].astype(BF16)
    keep_ref[...] = product[half:]


def decode(plan, index, pieces, w_dec):
    tile = pick_tile(plan.model, 256)
    half = plan.groups * plan.pairs * plan.piece
    whole = pl.BlockSpec(memory_space=pltpu.VMEM)
    depth = plan.sources * plan.width
    return pl.pallas_call(
        partial(decode_kernel, plan),
        grid=(plan.model // tile,),
        in_specs=[pl.BlockSpec(memory_space=pltpu.SMEM)]
        + [whole] * len(pieces)
        + [pl.BlockSpec((plan.sources, 1, plan.width, tile), lambda j: (0, 0, 0, j))],
        out_specs=[pl.BlockSpec((half, tile), lambda j: (0, j))] * 2,
        out_shape=[
            jax.ShapeDtypeStruct((half, plan.model), BF16),
            jax.ShapeDtypeStruct((half, plan.model), F32),
        ],
        scratch_shapes=[pltpu.VMEM((2 * half, depth), BF16)],
        cost_estimate=SMALL_COST,
        compiler_params=pltpu.CompilerParams(vmem_limit_bytes=VMEM_BYTES),
        name="decode",
    )(index, *pieces, w_dec)


def lane_order(plan, lane):
    first, rest = plan.lanes[lane][0], plan.lanes[lane][1:]
    kept = [0]
    for bit in reversed(rest):
        kept = [j | bit for j in kept] + kept
    return first, kept


def gradient_kernel(plan, lane, index_ref, *refs):
    n_in = 2 * plan.depth
    errors, w_ref, outs, e_ref = refs[:n_in], refs[n_in], refs[n_in + 1:-1], refs[-1]
    if lane == 0:
        squares_ref, outs = outs[-1], outs[:-1]
    lo, hi = plan.lane_sources[lane]
    first, kept = lane_order(plan, lane)

    @pl.when((pl.program_id(0) == 0) & (pl.program_id(1) == 0))
    def _():
        for i in range(n_in):
            at = pl.multiple_of(index_ref[1 + plan.sources + i] * plan.piece, ROW_TILE)
            e_ref[pl.ds(at, plan.piece), :] = errors[i][...]
        if lane == 0:
            total = jnp.zeros((8, 128), F32)
            for row in range(0, e_ref.shape[0], ROW_TILE):
                value = e_ref[row:row + ROW_TILE, :].astype(F32)
                value = value * value
                value = value[:8] + value[8:]
                for col in range(0, plan.model, 128):
                    total = total + value[:, col:col + 128]
            squares_ref[...] = total

    product = lax.dot_general(
        w_ref[0, 0], e_ref[...], (((1,), (1,)), ((), ())), preferred_element_type=F32
    ).T
    feeds = index_ref[1 + lo + pl.program_id(0)] > 0
    product = jnp.where(feeds, product, 0.0)
    n = len(kept)
    for p, j in enumerate(kept):
        away = (j ^ first) * plan.block
        outs[p][0] = product[away:away + plan.block].astype(BF16)
        outs[n + p][0] = product[j * plan.block:(j + 1) * plan.block]


def gradient(plan, lane, index, errors, w_dec):
    lo, hi = plan.lane_sources[lane]
    n = hi - lo
    tile = pick_tile(plan.width, 512)
    half = plan.groups // 2
    shape = (n, plan.block, plan.width)
    whole = pl.BlockSpec(memory_space=pltpu.VMEM)
    rows = plan.groups * plan.block
    extra_specs = [pl.BlockSpec((8, 128), lambda s, j: (0, 0))] if lane == 0 else []
    extra_shape = [jax.ShapeDtypeStruct((8, 128), F32)] if lane == 0 else []
    outs = pl.pallas_call(
        partial(gradient_kernel, plan, lane),
        grid=(n, plan.width // tile),
        in_specs=[pl.BlockSpec(memory_space=pltpu.SMEM)]
        + [whole] * len(errors)
        + [pl.BlockSpec((1, 1, tile, plan.model), lambda s, j: (s + lo, 0, j, 0))],
        out_specs=[pl.BlockSpec((1, plan.block, tile), lambda s, j: (s, 0, j))] * (2 * half)
        + extra_specs,
        out_shape=[jax.ShapeDtypeStruct(shape, BF16)] * half
        + [jax.ShapeDtypeStruct(shape, F32)] * half
        + extra_shape,
        scratch_shapes=[pltpu.VMEM((rows, plan.model), BF16)],
        cost_estimate=SMALL_COST,
        compiler_params=pltpu.CompilerParams(vmem_limit_bytes=VMEM_BYTES),
        name="gradient",
    )(index, *errors, w_dec)
    return outs[:half], outs[half:2 * half], outs[2 * half:]


def per_device(resid, w_enc, b_enc, w_dec, targets, start_layer):
    plan = Plan(resid, w_dec)
    group = lax.axis_index("grp").astype(jnp.int32)
    feat = lax.axis_index("feat").astype(jnp.int32)
    core, level = feat % 2, feat // 2
    groups, feats = plan.groups, plan.feats

    def block_of(level_to):
        return ((level_to // plan.pairs) ^ group) * plan.pairs + level_to % plan.pairs

    feeds = (group >= start_layer[:, 0]).astype(jnp.int32)
    places = [block_of(level ^ d) * 2 + core for d in range(plan.depth)]
    places += [block_of(level ^ d) * 2 + 1 - core for d in range(plan.depth)]
    index = jnp.concatenate([core[None], feeds, jnp.stack(places)])

    encoded = [encode(plan, i, resid, w_enc, b_enc) for i in range(len(plan.lanes))]
    active = jnp.stack(
        [e[-1][s] for e in encoded for s in range(e[-1].shape[0])], axis=1
    )

    gathered = []
    earlier = []
    for c in range(plan.chunks):
        own = after([e[c] for e in encoded], earlier)
        pieces = []
        for lane, bits in enumerate(plan.lanes):
            held = {0: own[lane]}
            for bit in bits:
                held.update(
                    {j | bit: swap(x, "grp", groups, bit) for j, x in list(held.items())}
                )
            pieces += [held[j] for j in range(groups)]
        gathered.append(pieces)
        earlier = [pieces[groups - 1]]

    level_bits = [1 << i for i in range(plan.depth.bit_length() - 1)]
    recon_parts = []
    squares = jnp.zeros((8, 128), F32)
    lane_results = [[] for _ in plan.lanes]
    behind, before_parts, before_recon, before_gradient = [], [], [], []
    for c in range(plan.chunks):
        pieces = after(gathered[c], behind)
        send, keep = decode(plan, index, pieces, w_dec)
        keep, = after([keep], before_parts)
        other = swap(send, "feat", feats, 1)

        def part(level_to):
            first = block_of(level_to) * plan.piece
            mine = lax.dynamic_slice_in_dim(keep, first, plan.piece, 0)
            theirs = lax.dynamic_slice_in_dim(other, first, plan.piece, 0)
            return mine + theirs.astype(F32)

        held = {d: part(level ^ d) for d in range(plan.depth)}
        for bit in level_bits:
            sends = {d: held.pop(d).astype(BF16) for d in sorted(held) if d & bit}
            behind = list(sends.values())
            for d in sorted(sends, reverse=True):
                arrived = swap(sends[d], "feat", feats, 2 * bit)
                held[d ^ bit] = held[d ^ bit] + arrived.astype(F32)
        recon_rows, = after([held[0]], before_recon)
        first = feat * plan.rows_feat + c * plan.piece
        own_targets = lax.dynamic_slice_in_dim(targets[0], first, plan.piece, 0)
        difference = recon_rows - own_targets.astype(F32)
        recon_parts.append(recon_rows.astype(BF16))

        held = {0: difference.astype(BF16)}
        before_parts = [held[0]]
        for bit in reversed(level_bits):
            held.update(
                {d | bit: swap(x, "feat", feats, 2 * bit) for d, x in list(held.items())}
            )
        errors = [held[d] for d in range(plan.depth)]
        errors += [swap(e, "feat", feats, 1) for e in errors]
        errors = after(errors, before_gradient)

        before_recon, before_gradient = [], []
        for lane, bits in enumerate(plan.lanes):
            away, kept, extra = gradient(plan, lane, index, errors, w_dec)
            before_recon += away
            if extra:
                squares = squares + extra[0]
            for step, bit in enumerate(bits):
                got = [swap(x, "grp", groups, bit) for x in away]
                total = [x + y.astype(F32) for x, y in zip(kept, got)]
                cut = len(total) // 2
                away = [x.astype(BF16) for x in total[:cut]]
                before_gradient += away
                kept = total[cut:]
            lane_results[lane].append(total[0])

    loss = jnp.full((8, 128), jnp.sum(squares), F32)
    for bit in (1 << i for i in range(groups.bit_length() - 1)):
        loss = loss + swap(loss, "grp", groups, bit)
    entries = targets.shape[0] * groups * plan.tokens * plan.model
    recon_loss = loss[0, 0] / entries

    recon = jnp.concatenate(recon_parts, axis=0)[None]
    per_source = []
    for lane, (lo, hi) in enumerate(plan.lane_sources):
        parts = [
            r.reshape(hi - lo, plan.per_group, 1, plan.piece, plan.width)
            for r in lane_results[lane]
        ]
        per_source.append(
            jnp.concatenate(parts, axis=2).reshape(hi - lo, plan.rows, plan.width)
        )
    feat_grad = jnp.concatenate(per_source, axis=0).transpose(1, 0, 2)
    return active, recon, recon_loss, feat_grad


def solution(mesh):
    in_specs = (
        P(None, "grp", None),
        P(None, None, "feat"),
        P(None, "feat"),
        P(None, "grp", "feat", None),
        P("grp", None, None),
        P(None, "feat"),
    )
    out_specs = (P("grp", None, "feat"), P("grp", "feat", None), P(), P("grp", None, "feat"))
    return jax.shard_map(
        per_device, mesh=mesh, in_specs=in_specs, out_specs=out_specs, check_vma=False
    )
```

```python
from functools import partial

import jax
import jax.numpy as jnp
from jax import lax
from jax.experimental import pallas as pl
from jax.experimental.pallas import tpu as pltpu
from jax.sharding import PartitionSpec as P

BF16 = jnp.bfloat16
F32 = jnp.float32
WANTED_CHUNKS = 2
ROW_TILE = 16
IN_FLIGHT = 4
VMEM_BYTES = 44 << 20
ENCODE_VMEM_BYTES = 59 << 20
SMALL_COST = pl.CostEstimate(flops=1 << 20, bytes_accessed=1 << 10, transcendentals=0)
FAR = pl.BlockSpec(memory_space=pltpu.HBM)
ANYWHERE = pl.BlockSpec(memory_space=pl.ANY)
SCALARS = pl.BlockSpec(memory_space=pltpu.SMEM)
NEAR = pl.BlockSpec(memory_space=pltpu.VMEM)


def pick_tile(size, wanted):
    return wanted if size % wanted == 0 else size


def swap(x, axis, size, offset):
    return lax.ppermute(x, axis, [(i, i ^ offset) for i in range(size)])


def after(values, earlier):
    if not earlier:
        return list(values)
    return list(lax.optimization_barrier(list(values) + list(earlier)))[:len(values)]


class Plan:
    def __init__(self, resid, w_dec):
        self.sources, self.rows, self.model = resid.shape
        self.width = w_dec.shape[2]
        self.groups = lax.axis_size("grp")
        self.feats = lax.axis_size("feat")
        self.depth = self.feats // 2
        self.tokens = self.rows * self.groups
        self.rows_feat = self.tokens // self.feats
        self.per_group = self.rows // self.rows_feat
        self.pairs = self.per_group // 2
        self.chunks = WANTED_CHUNKS
        while self.rows_feat % (self.chunks * ROW_TILE):
            self.chunks -= 1
        self.piece = self.rows_feat // self.chunks
        self.block = self.per_group * self.piece
        self.chunk_rows = self.groups * self.block
        bits = [1 << i for i in range(self.groups.bit_length() - 1)]
        self.lanes = [bits[i:] + bits[:i] for i in range(len(bits))]
        starts = [i * self.sources // len(bits) for i in range(len(bits) + 1)]
        self.lane_sources = list(zip(starts[:-1], starts[1:]))
        self.level_bits = [1 << i for i in range(self.depth.bit_length() - 1)]

    def kept_order(self, lane):
        kept = [0]
        for bit in reversed(self.lanes[lane][1:]):
            kept = [j | bit for j in kept] + kept
        return kept


class Stream:
    def __init__(self, copies):
        self.copies = copies
        self.started = 0
        self.more(IN_FLIGHT)

    def more(self, count):
        for copy in self.copies[self.started:self.started + count]:
            copy.start()
        self.started += count

    def wait(self, i):
        self.copies[i].wait()
        self.more(1)


def call(kernel, name, in_specs, out_shape, scratch, args, vmem=VMEM_BYTES, **options):
    return pl.pallas_call(
        kernel,
        in_specs=in_specs,
        out_shape=out_shape,
        scratch_shapes=scratch,
        cost_estimate=SMALL_COST,
        compiler_params=pltpu.CompilerParams(vmem_limit_bytes=vmem),
        name=name,
        **options,
    )(*args)


def encode_kernel(plan, lane, resid_ref, w_ref, b_ref, *refs):
    outs, (x_buf, w_buf, b_buf, total, x_sem, w_sem) = refs[:-6], refs[-6:]
    lo, hi = plan.lane_sources[lane]
    depth = w_buf.shape[1] // (w_sem.shape[0] // (hi - lo))
    steps = plan.model // depth
    near = [
        pltpu.make_async_copy(resid_ref.at[pl.ds(lo, hi - lo)], x_buf, x_sem.at[0]),
        pltpu.make_async_copy(b_ref, b_buf, x_sem.at[1]),
    ]
    near[0].start()
    stream = Stream([
        pltpu.make_async_copy(
            w_ref.at[lo + s, pl.ds(i * depth, depth)],
            w_buf.at[s, pl.ds(i * depth, depth)],
            w_sem.at[s * steps + i],
        )
        for s in range(hi - lo)
        for i in range(steps)
    ])
    near[1].start()
    near[0].wait()
    for s in range(hi - lo):
        for i in range(steps):
            stream.wait(s * steps + i)
            part = slice(i * depth, (i + 1) * depth)
            product = jnp.dot(
                x_buf[s, :, part], w_buf[s, part, :], preferred_element_type=F32
            )
            if i:
                product = total[...] + product
            if i < steps - 1:
                total[...] = product
        if s == 0:
            near[1].wait()
        value = jnp.maximum(product + b_buf[lo + s:lo + s + 1, :], 0.0).astype(BF16)
        outs[-1][s] = value
        for c in range(plan.chunks):
            for b in range(plan.per_group):
                first = (b * plan.chunks + c) * plan.piece
                outs[c][s, b * plan.piece:(b + 1) * plan.piece, :] = (
                    value[first:first + plan.piece]
                )


def encode(plan, lane, resid, w_enc, b_enc):
    lo, hi = plan.lane_sources[lane]
    n = hi - lo
    steps = plan.model // pick_tile(plan.model, 768)
    out_shape = [jax.ShapeDtypeStruct((n, plan.block, plan.width), BF16)] * plan.chunks
    out_shape.append(jax.ShapeDtypeStruct((n, plan.rows, plan.width), BF16))
    return call(
        partial(encode_kernel, plan, lane),
        "encode",
        [FAR, FAR, FAR],
        out_shape,
        [
            pltpu.VMEM((n, plan.rows, plan.model), BF16),
            pltpu.VMEM((n, plan.model, plan.width), BF16),
            pltpu.VMEM((plan.sources, plan.width), F32),
            pltpu.VMEM((plan.rows, plan.width), F32),
            pltpu.SemaphoreType.DMA((2,)),
            pltpu.SemaphoreType.DMA((n * steps,)),
        ],
        (resid, w_enc, b_enc),
        vmem=ENCODE_VMEM_BYTES,
    )


def decode_kernel(plan, index_ref, *refs):
    n_in = plan.groups * len(plan.lanes)
    pieces, w_ref = refs[:n_in], refs[n_in]
    send_ref, keeps = refs[n_in + 1], refs[n_in + 2:-5]
    x_buf, w_buf, total, x_sem, w_sem = refs[-5:]
    half = plan.chunk_rows // 2
    core = index_ref[0]
    depth = pick_tile(plan.width, 256)
    steps = plan.width // depth

    placing = []
    for lane, (lo, hi) in enumerate(plan.lane_sources):
        for j in range(plan.groups):
            for b in range(plan.pairs):
                place = index_ref[1 + plan.sources + j * plan.pairs + b] * plan.piece
                for owner in range(2):
                    to = pl.multiple_of(place + jnp.where(core == owner, half, 0), ROW_TILE)
                    placing.append(pltpu.make_async_copy(
                        pieces[lane * plan.groups + j].at[
                            :, pl.ds((2 * b + owner) * plan.piece, plan.piece)
                        ],
                        x_buf.at[pl.ds(lo, hi - lo), pl.ds(to, plan.piece)],
                        x_sem.at[len(placing)],
                    ))
    for copy in placing:
        copy.start()
    stream = Stream([
        pltpu.make_async_copy(
            w_ref.at[s, 0, pl.ds(i * depth, depth)],
            w_buf.at[s, pl.ds(i * depth, depth)],
            w_sem.at[s * steps + i],
        )
        for s in range(plan.sources)
        for i in range(steps)
    ])
    for copy in placing:
        copy.wait()
    for s in range(plan.sources):
        @pl.when(index_ref[1 + s] == 0)
        def _(s=s):
            x_buf[s] = jnp.zeros(x_buf.shape[1:], BF16)

    for s in range(plan.sources):
        for i in range(steps):
            stream.wait(s * steps + i)
            part = slice(i * depth, (i + 1) * depth)
            product = jnp.dot(
                x_buf[s, :, part], w_buf[s, part, :], preferred_element_type=F32
            )
            if s + i:
                product = total[...] + product
            if s * steps + i < plan.sources * steps - 1:
                total[...] = product
    send_ref[...] = product[:half].astype(BF16)
    for d in range(plan.depth):
        keeps[d][...] = product[half + d * plan.piece:half + (d + 1) * plan.piece]


def decode(plan, index, pieces, w_dec):
    half = plan.chunk_rows // 2
    steps = plan.width // pick_tile(plan.width, 256)
    outs = call(
        partial(decode_kernel, plan),
        "decode",
        [SCALARS] + [ANYWHERE] * len(pieces) + [FAR],
        [jax.ShapeDtypeStruct((half, plan.model), BF16)]
        + [jax.ShapeDtypeStruct((plan.piece, plan.model), F32)] * plan.depth,
        [
            pltpu.VMEM((plan.sources, plan.chunk_rows, plan.width), BF16),
            pltpu.VMEM((plan.sources, plan.width, plan.model), BF16),
            pltpu.VMEM((plan.chunk_rows, plan.model), F32),
            pltpu.SemaphoreType.DMA((len(pieces) * plan.per_group,)),
            pltpu.SemaphoreType.DMA((plan.sources * steps,)),
        ],
        (index, *pieces, w_dec),
    )
    return outs[0], outs[1:]


def gradient_kernel(plan, lane, index_ref, *refs):
    n_in = 2 * plan.depth
    errors, w_ref, outs = refs[:n_in], refs[n_in], refs[n_in + 1:-4]
    e_buf, w_buf, e_sem, w_sem = refs[-4:]
    lo, hi = plan.lane_sources[lane]
    first, kept = plan.lanes[lane][0], plan.kept_order(lane)
    base = 1 + plan.sources + plan.groups * plan.pairs
    depth = pick_tile(plan.width, 512)
    steps = plan.width // depth

    placing = [
        pltpu.make_async_copy(
            errors[i],
            e_buf.at[
                pl.ds(pl.multiple_of(index_ref[base + i] * plan.piece, ROW_TILE), plan.piece)
            ],
            e_sem.at[i],
        )
        for i in range(n_in)
    ]
    for copy in placing:
        copy.start()
    stream = Stream([
        pltpu.make_async_copy(
            w_ref.at[lo + s, 0, pl.ds(i * depth, depth)],
            w_buf.at[s, pl.ds(i * depth, depth)],
            w_sem.at[s * steps + i],
        )
        for s in range(hi - lo)
        for i in range(steps)
    ])
    for copy in placing:
        copy.wait()
    if lane == 0:
        total = jnp.zeros((8, 128), F32)
        for row in range(0, plan.chunk_rows, ROW_TILE):
            value = e_buf[row:row + ROW_TILE, :].astype(F32)
            value = value * value
            value = value[:8] + value[8:]
            for col in range(0, plan.model, 128):
                total = total + value[:, col:col + 128]
        outs[-1][...] = total

    n = len(kept)
    for s in range(hi - lo):
        feeds = index_ref[1 + lo + s] > 0
        for i in range(steps):
            stream.wait(s * steps + i)
            part = slice(i * depth, (i + 1) * depth)
            product = lax.dot_general(
                w_buf[s, part, :], e_buf[...], (((1,), (1,)), ((), ())),
                preferred_element_type=F32,
            ).T
            product = jnp.where(feeds, product, 0.0)
            for p, j in enumerate(kept):
                away = (j ^ first) * plan.block
                outs[p][s, :, part] = product[away:away + plan.block].astype(BF16)
                outs[n + p][s, :, part] = product[j * plan.block:(j + 1) * plan.block]


def gradient(plan, lane, index, errors, w_dec):
    lo, hi = plan.lane_sources[lane]
    n = hi - lo
    steps = plan.width // pick_tile(plan.width, 512)
    half = plan.groups // 2
    shape = (n, plan.block, plan.width)
    out_shape = [jax.ShapeDtypeStruct(shape, BF16)] * half
    out_shape += [jax.ShapeDtypeStruct(shape, F32)] * half
    if lane == 0:
        out_shape.append(jax.ShapeDtypeStruct((8, 128), F32))
    outs = call(
        partial(gradient_kernel, plan, lane),
        "gradient",
        [SCALARS] + [ANYWHERE] * len(errors) + [FAR],
        out_shape,
        [
            pltpu.VMEM((plan.chunk_rows, plan.model), BF16),
            pltpu.VMEM((n, plan.width, plan.model), BF16),
            pltpu.SemaphoreType.DMA((len(errors),)),
            pltpu.SemaphoreType.DMA((n * steps,)),
        ],
        (index, *errors, w_dec),
    )
    return outs[:half], outs[half:2 * half], outs[2 * half:]


def finish_kernel(plan, chunk, with_previous, *refs):
    lanes = len(plan.lanes)
    kept, got = refs[:lanes], refs[lanes:2 * lanes]
    out_ref, stage, sem = refs[-3:]
    for lane, (lo, hi) in enumerate(plan.lane_sources):
        for s in range(lo, hi):
            stage[:, s, :] = kept[lane][s - lo] + got[lane][s - lo].astype(F32)
    copies = [
        pltpu.make_async_copy(
            stage.at[pl.ds(b * plan.piece, plan.piece)],
            out_ref.at[pl.ds((b * plan.chunks + chunk) * plan.piece, plan.piece)],
            sem.at[b],
        )
        for b in range(plan.per_group)
    ]
    for copy in copies:
        copy.start()
    for copy in copies:
        copy.wait()


def finish(plan, chunk, kept, got, previous):
    options = {}
    if previous is not None:
        options["input_output_aliases"] = {2 * len(kept): 0}
    previous = [] if previous is None else [previous]
    return call(
        partial(finish_kernel, plan, chunk, bool(previous)),
        "finish",
        [NEAR] * (2 * len(kept)) + [FAR] * len(previous),
        jax.ShapeDtypeStruct((plan.rows, plan.sources, plan.width), F32),
        [
            pltpu.VMEM((plan.block, plan.sources, plan.width), F32),
            pltpu.SemaphoreType.DMA((plan.per_group,)),
        ],
        (*kept, *got, *previous),
        out_specs=FAR,
        **options,
    )


def per_device(resid, w_enc, b_enc, w_dec, targets, start_layer):
    plan = Plan(resid, w_dec)
    group = lax.axis_index("grp").astype(jnp.int32)
    feat = lax.axis_index("feat").astype(jnp.int32)
    core, level = feat % 2, feat // 2
    groups, feats, chunks = plan.groups, plan.feats, plan.chunks

    feeds = (group >= start_layer[:, 0]).astype(jnp.int32)
    offsets = [
        ((group ^ j) * plan.pairs + b) ^ level
        for j in range(groups)
        for b in range(plan.pairs)
    ]
    places = []
    for other in range(2):
        for d in range(plan.depth):
            owner = level ^ d
            place = ((owner // plan.pairs) ^ group) * plan.pairs + owner % plan.pairs
            places.append(place * 2 + (core ^ other))
    index = jnp.concatenate([core[None], feeds, jnp.stack(offsets), jnp.stack(places)])

    encoded = [encode(plan, i, resid, w_enc, b_enc) for i in range(len(plan.lanes))]
    active = jnp.stack(
        [e[-1][s] for e in encoded for s in range(e[-1].shape[0])], axis=1
    )

    gathered, arrivals = [], []
    earlier = []
    for c in range(chunks):
        own = after([e[c] for e in encoded], earlier)
        pieces, first_arrivals = [], []
        for lane, bits in enumerate(plan.lanes):
            held = {0: own[lane]}
            for bit in bits:
                held.update(
                    {j | bit: swap(x, "grp", groups, bit) for j, x in list(held.items())}
                )
            pieces += [held[j] for j in range(groups)]
            first_arrivals += [held[bit] for bit in bits]
        gathered.append(pieces)
        arrivals.append(first_arrivals)
        earlier = [first_arrivals[0]]

    recon_parts = []
    squares = jnp.zeros((8, 128), F32)
    before_decode, before_gradient, after_gradient = [], [], []
    unfinished = []
    pending = None

    def exchange_errors(state, earlier):
        c, recon_rows = state
        recon_rows, = after([recon_rows], earlier)
        first = feat * plan.rows_feat + c * plan.piece
        own_targets = lax.dynamic_slice_in_dim(targets[0], first, plan.piece, 0)
        difference = recon_rows - own_targets.astype(F32)
        recon_parts.append(recon_rows.astype(BF16))
        error = difference.astype(BF16)
        held = {0: error}
        for bit in reversed(plan.level_bits):
            held.update(
                {d | bit: swap(x, "feat", feats, 2 * bit) for d, x in list(held.items())}
            )
        errors = [held[d] for d in range(plan.depth)]
        return error, errors + [swap(e, "feat", feats, 1) for e in errors]

    def exchange_gradients(errors):
        nonlocal squares, before_gradient, after_gradient
        errors = after(errors, before_gradient)
        before_gradient, after_gradient = [], []
        kept_all, got_all = [], []
        for lane, bits in enumerate(plan.lanes):
            away, kept, extra = gradient(plan, lane, index, errors, w_dec)
            after_gradient += away
            if extra:
                squares = squares + extra[0]
            for step, bit in enumerate(bits):
                got = [swap(x, "grp", groups, bit) for x in away]
                cut = len(got) // 2
                if cut:
                    total = [x + y.astype(F32) for x, y in zip(kept, got)]
                    away = [x.astype(BF16) for x in total[:cut]]
                    before_gradient += away
                    kept = total[cut:]
            kept_all.append(kept[0])
            got_all.append(got[0])
        unfinished.append((kept_all, got_all))

    for c in range(chunks):
        pieces = after(gathered[c], before_decode)
        send, keeps = decode(plan, index, pieces, w_dec)
        ready = []
        if c + 1 < chunks:
            send, = after([send], arrivals[c + 1])
        if pending is not None:
            error, errors = exchange_errors(pending, [send])
            ready = [error]
        other = swap(send, "feat", feats, 1)
        other, = after([other], ready)
        held = {
            d: keeps[d] + other[d * plan.piece:(d + 1) * plan.piece].astype(F32)
            for d in range(plan.depth)
        }
        for bit in plan.level_bits:
            sends = {d: held.pop(d).astype(BF16) for d in sorted(held) if d & bit}
            before_decode = list(sends.values())
            for d in sorted(sends, reverse=True):
                arrived = swap(sends[d], "feat", feats, 2 * bit)
                held[d ^ bit] = held[d ^ bit] + arrived.astype(F32)
        if pending is not None:
            exchange_gradients(errors)
        pending = (c, held[0])
    error, errors = exchange_errors(pending, after_gradient)
    exchange_gradients(errors)

    feat_grad = None
    for c, (kept, got) in enumerate(unfinished):
        if c + 1 < chunks:
            tied = after(kept + got, after_gradient)
            kept, got = tied[:len(kept)], tied[len(kept):]
        feat_grad = finish(plan, c, kept, got, feat_grad)

    loss = jnp.full((8, 128), jnp.sum(squares), F32)
    for bit in (1 << i for i in range(groups.bit_length() - 1)):
        loss = loss + swap(loss, "grp", groups, bit)
    entries = targets.shape[0] * groups * plan.tokens * plan.model
    recon_loss = loss[0, 0] / entries
    recon = jnp.concatenate(recon_parts, axis=0)[None]
    return active, recon, recon_loss, feat_grad


def solution(mesh):
    in_specs = (
        P(None, "grp", None),
        P(None, None, "feat"),
        P(None, "feat"),
        P(None, "grp", "feat", None),
        P("grp", None, None),
        P(None, "feat"),
    )
    out_specs = (P("grp", None, "feat"), P("grp", "feat", None), P(), P("grp", None, "feat"))
    return jax.shard_map(
        per_device, mesh=mesh, in_specs=in_specs, out_specs=out_specs, check_vma=False
    )
```

```python
from functools import partial

import jax
import jax.numpy as jnp
from jax import lax
from jax.experimental import pallas as pl
from jax.experimental.layout import Layout, with_layout_constraint
from jax.experimental.pallas import tpu as pltpu
from jax.sharding import PartitionSpec as P

BF16 = jnp.bfloat16
F32 = jnp.float32
WANTED_CHUNKS = 2
ROW_TILE = 16
IN_FLIGHT = 4
VMEM_BYTES = 44 << 20
MOST_VMEM_BYTES = 59 << 20
SMALL_COST = pl.CostEstimate(flops=1 << 20, bytes_accessed=1 << 10, transcendentals=0)
FAR = pl.BlockSpec(memory_space=pltpu.HBM)
ANYWHERE = pl.BlockSpec(memory_space=pl.ANY)
SCALARS = pl.BlockSpec(memory_space=pltpu.SMEM)
NEAR = pl.BlockSpec(memory_space=pltpu.VMEM)


def pick_tile(size, wanted):
    return wanted if size % wanted == 0 else size


def swap(x, axis, size, offset):
    return lax.ppermute(x, axis, [(i, i ^ offset) for i in range(size)])


def after(values, earlier):
    if not earlier:
        return list(values)
    return list(lax.optimization_barrier(list(values) + list(earlier)))[:len(values)]


class Plan:
    def __init__(self, resid, w_dec):
        self.sources, self.rows, self.model = resid.shape
        self.width = w_dec.shape[2]
        self.groups = lax.axis_size("grp")
        self.feats = lax.axis_size("feat")
        self.depth = self.feats // 2
        self.tokens = self.rows * self.groups
        self.rows_feat = self.tokens // self.feats
        self.per_group = self.rows // self.rows_feat
        self.pairs = self.per_group // 2
        self.chunks = WANTED_CHUNKS
        while self.rows_feat % (self.chunks * ROW_TILE):
            self.chunks -= 1
        self.piece = self.rows_feat // self.chunks
        self.block = self.per_group * self.piece
        self.chunk_rows = self.groups * self.block
        bits = [1 << i for i in range(self.groups.bit_length() - 1)]
        self.lanes = [bits[i:] + bits[:i] for i in range(len(bits))]
        starts = [i * self.sources // len(bits) for i in range(len(bits) + 1)]
        self.lane_sources = list(zip(starts[:-1], starts[1:]))
        self.level_bits = [1 << i for i in range(self.depth.bit_length() - 1)]

    def kept_order(self, lane):
        kept = [0]
        for bit in reversed(self.lanes[lane][1:]):
            kept = [j | bit for j in kept] + kept
        return kept


class Stream:
    def __init__(self, copies):
        self.copies = copies
        self.started = 0
        self.more(IN_FLIGHT)

    def more(self, count):
        for copy in self.copies[self.started:self.started + count]:
            copy.start()
        self.started += count

    def wait(self, i):
        self.copies[i].wait()
        self.more(1)


def call(kernel, name, in_specs, out_shape, scratch, args, vmem=VMEM_BYTES, **options):
    return pl.pallas_call(
        kernel,
        in_specs=in_specs,
        out_shape=out_shape,
        scratch_shapes=scratch,
        cost_estimate=SMALL_COST,
        compiler_params=pltpu.CompilerParams(vmem_limit_bytes=vmem),
        name=name,
        **options,
    )(*args)


def encode_kernel(plan, lane, resid_ref, w_ref, b_ref, *refs):
    outs, (x_buf, w_buf, b_buf, total, x_sem, w_sem) = refs[:-6], refs[-6:]
    lo, hi = plan.lane_sources[lane]
    depth = w_buf.shape[1] // (w_sem.shape[0] // (hi - lo))
    steps = plan.model // depth
    near = [
        pltpu.make_async_copy(resid_ref.at[pl.ds(lo, hi - lo)], x_buf, x_sem.at[0]),
        pltpu.make_async_copy(b_ref, b_buf, x_sem.at[1]),
    ]
    near[0].start()
    stream = Stream([
        pltpu.make_async_copy(
            w_ref.at[lo + s, pl.ds(i * depth, depth)],
            w_buf.at[s, pl.ds(i * depth, depth)],
            w_sem.at[s * steps + i],
        )
        for s in range(hi - lo)
        for i in range(steps)
    ])
    near[1].start()
    near[0].wait()
    for s in range(hi - lo):
        for i in range(steps):
            stream.wait(s * steps + i)
            part = slice(i * depth, (i + 1) * depth)
            product = jnp.dot(
                x_buf[s, :, part], w_buf[s, part, :], preferred_element_type=F32
            )
            if i:
                product = total[...] + product
            if i < steps - 1:
                total[...] = product
        if s == 0:
            near[1].wait()
        value = jnp.maximum(product + b_buf[lo + s:lo + s + 1, :], 0.0).astype(BF16)
        outs[-1][s] = value
        for c in range(plan.chunks):
            for b in range(plan.per_group):
                first = (b * plan.chunks + c) * plan.piece
                outs[c][s, b * plan.piece:(b + 1) * plan.piece, :] = (
                    value[first:first + plan.piece]
                )


def encode(plan, lane, resid, w_enc, b_enc):
    lo, hi = plan.lane_sources[lane]
    n = hi - lo
    steps = plan.model // pick_tile(plan.model, 768)
    out_shape = [jax.ShapeDtypeStruct((n, plan.block, plan.width), BF16)] * plan.chunks
    out_shape.append(jax.ShapeDtypeStruct((n, plan.rows, plan.width), BF16))
    return call(
        partial(encode_kernel, plan, lane),
        "encode",
        [FAR, FAR, FAR],
        out_shape,
        [
            pltpu.VMEM((n, plan.rows, plan.model), BF16),
            pltpu.VMEM((n, plan.model, plan.width), BF16),
            pltpu.VMEM((plan.sources, plan.width), F32),
            pltpu.VMEM((plan.rows, plan.width), F32),
            pltpu.SemaphoreType.DMA((2,)),
            pltpu.SemaphoreType.DMA((n * steps,)),
        ],
        (resid, w_enc, b_enc),
        vmem=MOST_VMEM_BYTES,
    )


def decode_kernel(plan, index_ref, *refs):
    n_in = plan.groups * len(plan.lanes)
    pieces, w_ref = refs[:n_in], refs[n_in]
    send_ref, keeps = refs[n_in + 1], refs[n_in + 2:-5]
    x_buf, w_buf, total, x_sem, w_sem = refs[-5:]
    half = plan.chunk_rows // 2
    core = index_ref[0]
    depth = pick_tile(plan.width, 256)
    steps = plan.width // depth

    placing = []
    for lane, (lo, hi) in enumerate(plan.lane_sources):
        for j in range(plan.groups):
            for b in range(plan.pairs):
                place = index_ref[1 + plan.sources + j * plan.pairs + b] * plan.piece
                for owner in range(2):
                    to = pl.multiple_of(place + jnp.where(core == owner, half, 0), ROW_TILE)
                    placing.append(pltpu.make_async_copy(
                        pieces[lane * plan.groups + j].at[
                            :, pl.ds((2 * b + owner) * plan.piece, plan.piece)
                        ],
                        x_buf.at[pl.ds(lo, hi - lo), pl.ds(to, plan.piece)],
                        x_sem.at[len(placing)],
                    ))
    for copy in placing:
        copy.start()
    stream = Stream([
        pltpu.make_async_copy(
            w_ref.at[s, 0, pl.ds(i * depth, depth)],
            w_buf.at[s, pl.ds(i * depth, depth)],
            w_sem.at[s * steps + i],
        )
        for s in range(plan.sources)
        for i in range(steps)
    ])
    for copy in placing:
        copy.wait()
    for s in range(plan.sources):
        @pl.when(index_ref[1 + s] == 0)
        def _(s=s):
            x_buf[s] = jnp.zeros(x_buf.shape[1:], BF16)

    for s in range(plan.sources):
        for i in range(steps):
            stream.wait(s * steps + i)
            part = slice(i * depth, (i + 1) * depth)
            product = jnp.dot(
                x_buf[s, :, part], w_buf[s, part, :], preferred_element_type=F32
            )
            if s + i:
                product = total[...] + product
            if s * steps + i < plan.sources * steps - 1:
                total[...] = product
    send_ref[...] = product[:half].astype(BF16)
    for d in range(plan.depth):
        keeps[d][...] = product[half + d * plan.piece:half + (d + 1) * plan.piece]


def decode(plan, index, pieces, w_dec):
    half = plan.chunk_rows // 2
    steps = plan.width // pick_tile(plan.width, 256)
    outs = call(
        partial(decode_kernel, plan),
        "decode",
        [SCALARS] + [ANYWHERE] * len(pieces) + [FAR],
        [jax.ShapeDtypeStruct((half, plan.model), BF16)]
        + [jax.ShapeDtypeStruct((plan.piece, plan.model), F32)] * plan.depth,
        [
            pltpu.VMEM((plan.sources, plan.chunk_rows, plan.width), BF16),
            pltpu.VMEM((plan.sources, plan.width, plan.model), BF16),
            pltpu.VMEM((plan.chunk_rows, plan.model), F32),
            pltpu.SemaphoreType.DMA((len(pieces) * plan.per_group,)),
            pltpu.SemaphoreType.DMA((plan.sources * steps,)),
        ],
        (index, *pieces, w_dec),
        vmem=MOST_VMEM_BYTES,
    )
    return outs[0], outs[1:]


def gradient_kernel(plan, lane, index_ref, errors_ref, w_ref, *refs):
    outs, (e_buf, w_buf, e_sem, w_sem) = refs[:-4], refs[-4:]
    lo, hi = plan.lane_sources[lane]
    first, kept = plan.lanes[lane][0], plan.kept_order(lane)
    depth = pick_tile(plan.width, 256)
    steps = plan.width // depth
    group = index_ref[1 + plan.sources + plan.groups * plan.pairs]

    placing = []
    for j in range(plan.groups):
        rows = pl.multiple_of((group ^ j) * plan.block, ROW_TILE)
        placing.append(pltpu.make_async_copy(
            errors_ref.at[pl.ds(rows, plan.block)],
            e_buf.at[pl.ds(j * plan.block, plan.block)],
            e_sem.at[j],
        ))
    for copy in placing:
        copy.start()
    stream = Stream([
        pltpu.make_async_copy(
            w_ref.at[lo + s, 0, pl.ds(i * depth, depth)],
            w_buf.at[s, pl.ds(i * depth, depth)],
            w_sem.at[s * steps + i],
        )
        for s in range(hi - lo)
        for i in range(steps)
    ])
    for copy in placing:
        copy.wait()
    if lane == 0:
        total = jnp.zeros((8, 128), F32)
        for row in range(0, plan.chunk_rows, ROW_TILE):
            value = e_buf[row:row + ROW_TILE, :].astype(F32)
            value = value * value
            value = value[:8] + value[8:]
            for col in range(0, plan.model, 128):
                total = total + value[:, col:col + 128]
        outs[-1][...] = total

    n = len(kept)
    for s in range(hi - lo):
        feeds = index_ref[1 + lo + s] > 0
        for i in range(steps):
            stream.wait(s * steps + i)
            part = slice(i * depth, (i + 1) * depth)
            product = lax.dot_general(
                e_buf[...], w_buf[s, part, :], (((1,), (1,)), ((), ())),
                preferred_element_type=F32,
            )
            product = jnp.where(feeds, product, 0.0)
            for p, j in enumerate(kept):
                away = (j ^ first) * plan.block
                outs[p][s, :, part] = product[away:away + plan.block].astype(BF16)
                outs[n + p][s, :, part] = product[j * plan.block:(j + 1) * plan.block]


def gradient(plan, lane, index, errors, w_dec):
    lo, hi = plan.lane_sources[lane]
    n = hi - lo
    steps = plan.width // pick_tile(plan.width, 256)
    half = plan.groups // 2
    shape = (n, plan.block, plan.width)
    out_shape = [jax.ShapeDtypeStruct(shape, BF16)] * half
    out_shape += [jax.ShapeDtypeStruct(shape, F32)] * half
    if lane == 0:
        out_shape.append(jax.ShapeDtypeStruct((8, 128), F32))
    outs = call(
        partial(gradient_kernel, plan, lane),
        "gradient",
        [SCALARS, ANYWHERE, FAR],
        out_shape,
        [
            pltpu.VMEM((plan.chunk_rows, plan.model), BF16),
            pltpu.VMEM((n, plan.width, plan.model), BF16),
            pltpu.SemaphoreType.DMA((plan.groups,)),
            pltpu.SemaphoreType.DMA((n * steps,)),
        ],
        (index, errors, w_dec),
    )
    return outs[:half], outs[half:2 * half], outs[2 * half:]


def finish_kernel(plan, chunk, with_previous, *refs):
    lanes = len(plan.lanes)
    kept, got = refs[:lanes], refs[lanes:2 * lanes]
    out_ref, stage, sem = refs[-3:]
    for lane, (lo, hi) in enumerate(plan.lane_sources):
        for s in range(lo, hi):
            stage[:, s, :] = kept[lane][s - lo] + got[lane][s - lo].astype(F32)
    copies = [
        pltpu.make_async_copy(
            stage.at[pl.ds(b * plan.piece, plan.piece)],
            out_ref.at[pl.ds((b * plan.chunks + chunk) * plan.piece, plan.piece)],
            sem.at[b],
        )
        for b in range(plan.per_group)
    ]
    for copy in copies:
        copy.start()
    for copy in copies:
        copy.wait()


def finish(plan, chunk, kept, got, previous):
    options = {}
    if previous is not None:
        options["input_output_aliases"] = {2 * len(kept): 0}
    previous = [] if previous is None else [previous]
    return call(
        partial(finish_kernel, plan, chunk, bool(previous)),
        "finish",
        [NEAR] * (2 * len(kept)) + [FAR] * len(previous),
        jax.ShapeDtypeStruct((plan.rows, plan.sources, plan.width), F32),
        [
            pltpu.VMEM((plan.block, plan.sources, plan.width), F32),
            pltpu.SemaphoreType.DMA((plan.per_group,)),
        ],
        (*kept, *got, *previous),
        out_specs=FAR,
        **options,
    )


def per_device(resid, w_enc, b_enc, w_dec, targets, start_layer):
    plan = Plan(resid, w_dec)
    group = lax.axis_index("grp").astype(jnp.int32)
    feat = lax.axis_index("feat").astype(jnp.int32)
    core, level = feat % 2, feat // 2
    groups, feats, chunks = plan.groups, plan.feats, plan.chunks

    feeds = (group >= start_layer[:, 0]).astype(jnp.int32)
    offsets = [
        ((group ^ j) * plan.pairs + b) ^ level
        for j in range(groups)
        for b in range(plan.pairs)
    ]
    index = jnp.concatenate([core[None], feeds, jnp.stack(offsets), group[None]])

    encoded = [encode(plan, i, resid, w_enc, b_enc) for i in range(len(plan.lanes))]
    active = jnp.stack(
        [e[-1][s] for e in encoded for s in range(e[-1].shape[0])], axis=1
    )
    active = with_layout_constraint(active, Layout((0, 1, 2)))

    gathered, arrivals = [], []
    earlier = []
    for c in range(chunks):
        own = after([e[c] for e in encoded], earlier)
        pieces, first_arrivals = [], []
        for lane, bits in enumerate(plan.lanes):
            mine = own[lane]
            if not c:
                mine, = after([mine], first_arrivals[-len(bits):])
            held = {0: mine}
            for bit in bits:
                held.update(
                    {j | bit: swap(x, "grp", groups, bit) for j, x in list(held.items())}
                )
            pieces += [held[j] for j in range(groups)]
            first_arrivals += [held[bit] for bit in bits]
        gathered.append(pieces)
        arrivals.append(first_arrivals)
        earlier = first_arrivals

    recon_parts = []
    squares = jnp.zeros((8, 128), F32)
    before_decode, before_gradient, after_gradient = [active], [], []
    unfinished = []
    pending = None

    def exchange_errors(state, earlier):
        c, recon_rows = state
        recon_rows, = after([recon_rows], earlier)
        first = feat * plan.rows_feat + c * plan.piece
        own_targets = lax.dynamic_slice_in_dim(targets[0], first, plan.piece, 0)
        difference = recon_rows - own_targets.astype(F32)
        recon_parts.append(recon_rows.astype(BF16))
        error = difference.astype(BF16)
        return error, lax.all_gather(error, "feat", axis=0, tiled=True)

    def exchange_gradients(errors):
        nonlocal squares, before_gradient, after_gradient
        errors, = after([errors], before_gradient)
        before_gradient, after_gradient = [], []
        kept_all, got_all = [], []
        for lane, bits in enumerate(plan.lanes):
            away, kept, extra = gradient(plan, lane, index, errors, w_dec)
            after_gradient += away
            if got_all:
                away = after(away, first_got)
            if extra:
                squares = squares + extra[0]
            for step, bit in enumerate(bits):
                got = [swap(x, "grp", groups, bit) for x in away]
                if not step:
                    first_got = got[:1]
                cut = len(got) // 2
                if cut:
                    total = [x + y.astype(F32) for x, y in zip(kept, got)]
                    away = [x.astype(BF16) for x in total[:cut]]
                    before_gradient += away
                    kept = total[cut:]
            kept_all.append(kept[0])
            got_all.append(got[0])
        unfinished.append((kept_all, got_all))

    for c in range(chunks):
        pieces = after(gathered[c], before_decode)
        send, keeps = decode(plan, index, pieces, w_dec)
        ready = []
        if c + 1 < chunks:
            send, = after([send], arrivals[c + 1])
        if pending is not None:
            error, errors = exchange_errors(pending, [send])
            ready = [error]
        other = swap(send, "feat", feats, 1)
        other, = after([other], ready)
        held = {
            d: keeps[d] + other[d * plan.piece:(d + 1) * plan.piece].astype(F32)
            for d in range(plan.depth)
        }
        for bit in plan.level_bits:
            sends = {d: held.pop(d).astype(BF16) for d in sorted(held) if d & bit}
            before_decode = list(sends.values())
            for d in sorted(sends, reverse=True):
                arrived = swap(sends[d], "feat", feats, 2 * bit)
                held[d ^ bit] = held[d ^ bit] + arrived.astype(F32)
        if pending is not None:
            exchange_gradients(errors)
        pending = (c, held[0])
    error, errors = exchange_errors(pending, after_gradient)
    exchange_gradients(errors)

    feat_grad = None
    for c, (kept, got) in enumerate(unfinished):
        if c + 1 < chunks:
            tied = after(kept + got, after_gradient)
            kept, got = tied[:len(kept)], tied[len(kept):]
        feat_grad = finish(plan, c, kept, got, feat_grad)

    loss = jnp.full((8, 128), jnp.sum(squares), F32)
    for bit in (1 << i for i in range(groups.bit_length() - 1)):
        loss = loss + swap(loss, "grp", groups, bit)
    entries = targets.shape[0] * groups * plan.tokens * plan.model
    recon_loss = loss[0, 0] / entries
    recon = jnp.concatenate(recon_parts, axis=0)[None]
    return active, recon, recon_loss, feat_grad


def solution(mesh):
    in_specs = (
        P(None, "grp", None),
        P(None, None, "feat"),
        P(None, "feat"),
        P(None, "grp", "feat", None),
        P("grp", None, None),
        P(None, "feat"),
    )
    out_specs = (P("grp", None, "feat"), P("grp", "feat", None), P(), P("grp", None, "feat"))
    return jax.shard_map(
        per_device, mesh=mesh, in_specs=in_specs, out_specs=out_specs, check_vma=False
    )
```

```python
from functools import partial

import jax
import jax.numpy as jnp
from jax import lax
from jax.experimental import pallas as pl
from jax.experimental.layout import Layout, with_layout_constraint
from jax.experimental.pallas import tpu as pltpu
from jax.sharding import PartitionSpec as P

BF16 = jnp.bfloat16
F32 = jnp.float32
WANTED_CHUNKS = 2
ROW_TILE = 16
IN_FLIGHT = 3
WEIGHT_SLOTS = 5
VMEM_BYTES = 44 << 20
MOST_VMEM_BYTES = 59 << 20
SMALL_COST = pl.CostEstimate(flops=1 << 20, bytes_accessed=1 << 10, transcendentals=0)
FAR = pl.BlockSpec(memory_space=pltpu.HBM)
ANYWHERE = pl.BlockSpec(memory_space=pl.ANY)
SCALARS = pl.BlockSpec(memory_space=pltpu.SMEM)
NEAR = pl.BlockSpec(memory_space=pltpu.VMEM)


def pick_tile(size, wanted):
    return wanted if size % wanted == 0 else size


def swap(x, axis, size, offset):
    return lax.ppermute(x, axis, [(i, i ^ offset) for i in range(size)])


def after(values, earlier):
    if not earlier:
        return list(values)
    return list(lax.optimization_barrier(list(values) + list(earlier)))[:len(values)]


class Plan:
    def __init__(self, resid, w_dec):
        self.sources, self.rows, self.model = resid.shape
        self.width = w_dec.shape[2]
        self.groups = lax.axis_size("grp")
        self.feats = lax.axis_size("feat")
        self.depth = self.feats // 2
        self.tokens = self.rows * self.groups
        self.rows_feat = self.tokens // self.feats
        self.per_group = self.rows // self.rows_feat
        self.pairs = self.per_group // 2
        self.chunks = WANTED_CHUNKS
        while self.rows_feat % (self.chunks * ROW_TILE):
            self.chunks -= 1
        self.piece = self.rows_feat // self.chunks
        self.block = self.per_group * self.piece
        self.chunk_rows = self.groups * self.block
        bits = [1 << i for i in range(self.groups.bit_length() - 1)]
        self.lanes = [bits[i:] + bits[:i] for i in range(len(bits))]
        starts = [i * self.sources // len(bits) for i in range(len(bits) + 1)]
        self.lane_sources = list(zip(starts[:-1], starts[1:]))
        self.level_bits = [1 << i for i in range(self.depth.bit_length() - 1)]

    def kept_order(self, lane):
        kept = [0]
        for bit in reversed(self.lanes[lane][1:]):
            kept = [j | bit for j in kept] + kept
        return kept


class Stream:
    def __init__(self, copies):
        self.copies = copies
        self.started = 0
        self.more(IN_FLIGHT)

    def more(self, count):
        for copy in self.copies[self.started:self.started + count]:
            copy.start()
        self.started += count

    def wait(self, i):
        self.copies[i].wait()
        self.more(1)


def call(kernel, name, in_specs, out_shape, scratch, args, vmem=VMEM_BYTES, **options):
    return pl.pallas_call(
        kernel,
        in_specs=in_specs,
        out_shape=out_shape,
        scratch_shapes=scratch,
        cost_estimate=SMALL_COST,
        compiler_params=pltpu.CompilerParams(vmem_limit_bytes=vmem),
        name=name,
        **options,
    )(*args)


def encode_kernel(plan, lane, resid_ref, w_ref, b_ref, *refs):
    outs, (x_buf, w_buf, b_buf, total, x_sem, w_sem) = refs[:-6], refs[-6:]
    lo, hi = plan.lane_sources[lane]
    depth = w_buf.shape[1] // (w_sem.shape[0] // (hi - lo))
    steps = plan.model // depth
    near = [
        pltpu.make_async_copy(resid_ref.at[pl.ds(lo, hi - lo)], x_buf, x_sem.at[0]),
        pltpu.make_async_copy(b_ref, b_buf, x_sem.at[1]),
    ]
    near[0].start()
    stream = Stream([
        pltpu.make_async_copy(
            w_ref.at[lo + s, pl.ds(i * depth, depth)],
            w_buf.at[s, pl.ds(i * depth, depth)],
            w_sem.at[s * steps + i],
        )
        for s in range(hi - lo)
        for i in range(steps)
    ])
    near[1].start()
    near[0].wait()
    for s in range(hi - lo):
        for i in range(steps):
            stream.wait(s * steps + i)
            part = slice(i * depth, (i + 1) * depth)
            product = jnp.dot(
                x_buf[s, :, part], w_buf[s, part, :], preferred_element_type=F32
            )
            if i:
                product = total[...] + product
            if i < steps - 1:
                total[...] = product
        if s == 0:
            near[1].wait()
        outs[0][s] = jnp.maximum(product + b_buf[lo + s:lo + s + 1, :], 0.0).astype(BF16)


def encode(plan, lane, resid, w_enc, b_enc):
    lo, hi = plan.lane_sources[lane]
    n = hi - lo
    steps = plan.model // pick_tile(plan.model, 768)
    return call(
        partial(encode_kernel, plan, lane),
        "encode",
        [FAR, FAR, FAR],
        jax.ShapeDtypeStruct((n, plan.rows, plan.width), BF16),
        [
            pltpu.VMEM((n, plan.rows, plan.model), BF16),
            pltpu.VMEM((n, plan.model, plan.width), BF16),
            pltpu.VMEM((plan.sources, plan.width), F32),
            pltpu.VMEM((plan.rows, plan.width), F32),
            pltpu.SemaphoreType.DMA((2,)),
            pltpu.SemaphoreType.DMA((n * steps,)),
        ],
        (resid, w_enc, b_enc),
        vmem=MOST_VMEM_BYTES,
    )


def decode_kernel(plan, index_ref, *refs):
    n_in = plan.groups * len(plan.lanes)
    pieces, w_ref, outs = refs[:n_in], refs[n_in], refs[n_in + 1:-5]
    x_buf, w_buf, total, x_sem, w_sem = refs[-5:]
    half = plan.tokens // 2
    core = index_ref[0]
    depth = w_buf.shape[1]
    steps = plan.width // depth

    placing = []
    for lane, (lo, hi) in enumerate(plan.lane_sources):
        for j in range(plan.groups):
            for b in range(plan.pairs):
                place = index_ref[1 + plan.sources + j * plan.pairs + b] * plan.rows_feat
                for owner in range(2):
                    to = pl.multiple_of(place + jnp.where(core == owner, half, 0), ROW_TILE)
                    placing.append(pltpu.make_async_copy(
                        pieces[lane * plan.groups + j].at[
                            :, pl.ds((2 * b + owner) * plan.rows_feat, plan.rows_feat)
                        ],
                        x_buf.at[pl.ds(lo, hi - lo), pl.ds(to, plan.rows_feat)],
                        x_sem.at[len(placing)],
                    ))
    for copy in placing:
        copy.start()
    stream = Stream([
        pltpu.make_async_copy(
            w_ref.at[s, 0, pl.ds(i * depth, depth)],
            w_buf.at[(s * steps + i) % w_buf.shape[0]],
            w_sem.at[s * steps + i],
        )
        for s in range(plan.sources)
        for i in range(steps)
    ])
    for copy in placing:
        copy.wait()
    for s in range(plan.sources):
        @pl.when(index_ref[1 + s] == 0)
        def _(s=s):
            x_buf[s] = jnp.zeros(x_buf.shape[1:], BF16)

    tile = pick_tile(plan.model, 768)
    for s in range(plan.sources):
        for i in range(steps):
            stream.wait(s * steps + i)
            w_ref = w_buf.at[(s * steps + i) % w_buf.shape[0]]
            part = slice(i * depth, (i + 1) * depth)
            last = s * steps + i == plan.sources * steps - 1
            for n in range(0, plan.model, tile):
                cols = slice(n, n + tile)
                product = jnp.dot(
                    x_buf[s, :, part], w_ref[:, cols], preferred_element_type=F32
                )
                if s + i:
                    product = total[:, cols] + product
                if not last:
                    total[:, cols] = product
                    continue
                for c in range(plan.chunks):
                    for d in range(plan.depth):
                        first = d * plan.rows_feat + c * plan.piece
                        outs[c][d * plan.piece:(d + 1) * plan.piece, cols] = (
                            product[first:first + plan.piece].astype(BF16)
                        )
                        outs[plan.chunks + c * plan.depth + d][:, cols] = (
                            product[half + first:half + first + plan.piece]
                        )


def decode(plan, index, pieces, w_dec):
    step = pick_tile(plan.width, 512)
    steps = plan.width // step
    chunks, depth = plan.chunks, plan.depth
    outs = call(
        partial(decode_kernel, plan),
        "decode",
        [SCALARS] + [ANYWHERE] * len(pieces) + [FAR],
        [jax.ShapeDtypeStruct((depth * plan.piece, plan.model), BF16)] * chunks
        + [jax.ShapeDtypeStruct((plan.piece, plan.model), F32)] * (chunks * depth),
        [
            pltpu.VMEM((plan.sources, plan.tokens, plan.width), BF16),
            pltpu.VMEM((WEIGHT_SLOTS, step, plan.model), BF16),
            pltpu.VMEM((plan.tokens, plan.model), F32),
            pltpu.SemaphoreType.DMA((len(pieces) * plan.per_group,)),
            pltpu.SemaphoreType.DMA((plan.sources * steps,)),
        ],
        (index, *pieces, w_dec),
    )
    sends, keeps = outs[:chunks], outs[chunks:]
    return sends, [keeps[c * depth:(c + 1) * depth] for c in range(chunks)]


def gradient_kernel(plan, index_ref, *refs):
    n_in = 2 * plan.depth
    errors, w_ref, outs = refs[:n_in], refs[n_in], refs[n_in + 1:-4]
    e_buf, w_buf, e_sem, w_sem = refs[-4:]
    depth = pick_tile(plan.width, 256)
    steps = plan.width // depth
    base = 1 + plan.sources + plan.groups * plan.pairs

    placing = [
        pltpu.make_async_copy(
            errors[i],
            e_buf.at[
                pl.ds(pl.multiple_of(index_ref[base + i] * plan.piece, ROW_TILE), plan.piece)
            ],
            e_sem.at[i],
        )
        for i in range(n_in)
    ]
    for copy in placing:
        copy.start()
    stream = Stream([
        pltpu.make_async_copy(
            w_ref.at[s, 0, pl.ds(i * depth, depth)],
            w_buf.at[s, pl.ds(i * depth, depth)],
            w_sem.at[s * steps + i],
        )
        for s in range(plan.sources)
        for i in range(steps)
    ])
    for copy in placing:
        copy.wait()

    half = plan.groups // 2
    for lane, (lo, hi) in enumerate(plan.lane_sources):
        first, kept = plan.lanes[lane][0], plan.kept_order(lane)
        away, keep = outs[2 * lane * half:][:half], outs[(2 * lane + 1) * half:][:half]
        for s in range(lo, hi):
            feeds = index_ref[1 + s] > 0
            for i in range(steps):
                stream.wait(s * steps + i)
                part = slice(i * depth, (i + 1) * depth)
                product = lax.dot_general(
                    e_buf[...], w_buf[s, part, :], (((1,), (1,)), ((), ())),
                    preferred_element_type=F32,
                )
                product = jnp.where(feeds, product, 0.0)
                for p, j in enumerate(kept):
                    far = (j ^ first) * plan.block
                    away[p][s - lo, :, part] = product[far:far + plan.block].astype(BF16)
                    keep[p][s - lo, :, part] = product[j * plan.block:(j + 1) * plan.block]

    total = jnp.zeros((8, 128), F32)
    for row in range(0, plan.chunk_rows, ROW_TILE):
        value = e_buf[row:row + ROW_TILE, :].astype(F32)
        value = value * value
        value = value[:8] + value[8:]
        for col in range(0, plan.model, 128):
            total = total + value[:, col:col + 128]
    outs[-1][...] = total


def gradient(plan, index, errors, w_dec):
    steps = plan.width // pick_tile(plan.width, 256)
    half = plan.groups // 2
    out_shape = []
    for lo, hi in plan.lane_sources:
        shape = (hi - lo, plan.block, plan.width)
        out_shape += [jax.ShapeDtypeStruct(shape, BF16)] * half
        out_shape += [jax.ShapeDtypeStruct(shape, F32)] * half
    outs = call(
        partial(gradient_kernel, plan),
        "gradient",
        [SCALARS] + [ANYWHERE] * len(errors) + [FAR],
        out_shape + [jax.ShapeDtypeStruct((8, 128), F32)],
        [
            pltpu.VMEM((plan.chunk_rows, plan.model), BF16),
            pltpu.VMEM((plan.sources, plan.width, plan.model), BF16),
            pltpu.SemaphoreType.DMA((len(errors),)),
            pltpu.SemaphoreType.DMA((plan.sources * steps,)),
        ],
        (index, *errors, w_dec),
    )
    lanes = [outs[2 * i * half:2 * (i + 1) * half] for i in range(len(plan.lanes))]
    return [(lane[:half], lane[half:]) for lane in lanes], outs[-1]


def finish_kernel(plan, chunk, with_previous, *refs):
    lanes = len(plan.lanes)
    kept, got = refs[:lanes], refs[lanes:2 * lanes]
    out_ref, stage, sem = refs[-3:]
    for lane, (lo, hi) in enumerate(plan.lane_sources):
        for s in range(lo, hi):
            stage[:, s, :] = kept[lane][s - lo] + got[lane][s - lo].astype(F32)
    copies = [
        pltpu.make_async_copy(
            stage.at[pl.ds(b * plan.piece, plan.piece)],
            out_ref.at[pl.ds((b * plan.chunks + chunk) * plan.piece, plan.piece)],
            sem.at[b],
        )
        for b in range(plan.per_group)
    ]
    for copy in copies:
        copy.start()
    for copy in copies:
        copy.wait()


def finish(plan, chunk, kept, got, previous):
    options = {}
    if previous is not None:
        options["input_output_aliases"] = {2 * len(kept): 0}
    previous = [] if previous is None else [previous]
    return call(
        partial(finish_kernel, plan, chunk, bool(previous)),
        "finish",
        [NEAR] * (2 * len(kept)) + [FAR] * len(previous),
        jax.ShapeDtypeStruct((plan.rows, plan.sources, plan.width), F32),
        [
            pltpu.VMEM((plan.block, plan.sources, plan.width), F32),
            pltpu.SemaphoreType.DMA((plan.per_group,)),
        ],
        (*kept, *got, *previous),
        out_specs=FAR,
        **options,
    )


def per_device(resid, w_enc, b_enc, w_dec, targets, start_layer):
    plan = Plan(resid, w_dec)
    group = lax.axis_index("grp").astype(jnp.int32)
    feat = lax.axis_index("feat").astype(jnp.int32)
    core, level = feat % 2, feat // 2
    groups, feats, chunks = plan.groups, plan.feats, plan.chunks

    feeds = (group >= start_layer[:, 0]).astype(jnp.int32)
    offsets = [
        ((group ^ j) * plan.pairs + b) ^ level
        for j in range(groups)
        for b in range(plan.pairs)
    ]
    places = []
    for other in range(2):
        for d in range(plan.depth):
            owner = level ^ d
            place = ((owner // plan.pairs) ^ group) * plan.pairs + owner % plan.pairs
            places.append(place * 2 + (core ^ other))
    index = jnp.concatenate([core[None], feeds, jnp.stack(offsets), jnp.stack(places)])

    encoded = [encode(plan, i, resid, w_enc, b_enc) for i in range(len(plan.lanes))]
    active = jnp.stack([e[s] for e in encoded for s in range(e.shape[0])], axis=1)
    active = with_layout_constraint(active, Layout((0, 1, 2)))

    pieces, arrived = [], []
    for lane, bits in enumerate(plan.lanes):
        mine, = after([encoded[lane]], arrived)
        held = {0: mine}
        for bit in bits:
            held.update(
                {j | bit: swap(x, "grp", groups, bit) for j, x in list(held.items())}
            )
        pieces += [held[j] for j in range(groups)]
        arrived = [held[bit] for bit in bits]

    sends, keeps = decode(plan, index, after(pieces, [active]), w_dec)
    partial_rows = []
    earlier = []
    for c in range(chunks):
        other = swap(sends[c], "feat", feats, 1)
        held = {
            d: keeps[c][d] + other[d * plan.piece:(d + 1) * plan.piece].astype(F32)
            for d in range(plan.depth)
        }
        for bit in plan.level_bits:
            away = {d: held.pop(d).astype(BF16) for d in sorted(held, reverse=True) if d & bit}
            if bit == plan.level_bits[0]:
                away = dict(zip(away, after(away.values(), earlier)))
            got = {d: swap(x, "feat", feats, 2 * bit) for d, x in away.items()}
            if bit == plan.level_bits[0]:
                earlier = list(got.values())[:1]
            for d, x in got.items():
                held[d ^ bit] = held[d ^ bit] + x.astype(F32)
        partial_rows.append(held[0])

    recon_parts, errors, first_errors = [], [], []
    for c in range(chunks):
        recon_rows, = after([partial_rows[c]], first_errors[-1:])
        first = feat * plan.rows_feat + c * plan.piece
        own_targets = lax.dynamic_slice_in_dim(targets[0], first, plan.piece, 0)
        difference = recon_rows - own_targets.astype(F32)
        recon_parts.append(recon_rows.astype(BF16))
        held = {0: difference.astype(BF16)}
        for bit in reversed(plan.level_bits):
            held.update(
                {d | bit: swap(x, "feat", feats, 2 * bit) for d, x in list(held.items())}
            )
        first_errors.append(held[plan.level_bits[-1]])
        every = [held[d] for d in range(plan.depth)]
        errors.append(every + [swap(e, "feat", feats, 1) for e in every])

    squares = jnp.zeros((8, 128), F32)
    feat_grad = None
    earlier, first_got = [], []
    for c in range(chunks):
        ready = after(errors[c], [e[0] for e in errors[c + 1:c + 2]] + first_got)
        lanes, total = gradient(plan, index, ready, w_dec)
        squares = squares + total
        kept_all, got_all, second, first_got = [], [], [], []
        for bits, (away, kept) in zip(plan.lanes, lanes):
            away = after(away, earlier)
            for step, bit in enumerate(bits):
                got = [swap(x, "grp", groups, bit) for x in away]
                cut = len(got) // 2
                if cut:
                    sums = [x + y.astype(F32) for x, y in zip(kept, got)]
                    away, kept = [x.astype(BF16) for x in sums[:cut]], sums[cut:]
                    if not step:
                        first_got.append(got[0])
                        second += away
                        away = after(away, [] if feat_grad is None else [feat_grad])
            kept_all.append(kept[0])
            got_all.append(got[0])
        feat_grad = finish(plan, c, kept_all, got_all, feat_grad)
        earlier = second

    squares, = after([squares], first_got)
    loss = jnp.full((8, 128), jnp.sum(squares), F32)
    for bit in (1 << i for i in range(groups.bit_length() - 1)):
        loss = loss + swap(loss, "grp", groups, bit)
    entries = targets.shape[0] * groups * plan.tokens * plan.model
    recon_loss = loss[0, 0] / entries
    recon = jnp.concatenate(recon_parts, axis=0)[None]
    return active, recon, recon_loss, feat_grad


def solution(mesh):
    in_specs = (
        P(None, "grp", None),
        P(None, None, "feat"),
        P(None, "feat"),
        P(None, "grp", "feat", None),
        P("grp", None, None),
        P(None, "feat"),
    )
    out_specs = (P("grp", None, "feat"), P("grp", "feat", None), P(), P("grp", None, "feat"))
    return jax.shard_map(
        per_device, mesh=mesh, in_specs=in_specs, out_specs=out_specs, check_vma=False
    )
```

```python
from functools import partial

import jax
import jax.numpy as jnp
from jax import lax
from jax.experimental import pallas as pl
from jax.experimental.layout import Layout, with_layout_constraint
from jax.experimental.pallas import tpu as pltpu
from jax.sharding import PartitionSpec as P

BF16 = jnp.bfloat16
F32 = jnp.float32
WANTED_CHUNKS = 2
ROW_TILE = 16
WEIGHT_SLOTS = 4
VMEM_BYTES = 44 << 20
MOST_VMEM_BYTES = 59 << 20
SMALL_COST = pl.CostEstimate(flops=1 << 20, bytes_accessed=1 << 10, transcendentals=0)
FAR = pl.BlockSpec(memory_space=pltpu.HBM)
ANYWHERE = pl.BlockSpec(memory_space=pl.ANY)
SCALARS = pl.BlockSpec(memory_space=pltpu.SMEM)
NEAR = pl.BlockSpec(memory_space=pltpu.VMEM)


def pick_tile(size, wanted):
    return wanted if size % wanted == 0 else size


def swap(x, axis, size, offset):
    return lax.ppermute(x, axis, [(i, i ^ offset) for i in range(size)])


def after(values, earlier):
    if not earlier:
        return list(values)
    return list(lax.optimization_barrier(list(values) + list(earlier)))[:len(values)]


class Plan:
    def __init__(self, resid, w_dec):
        self.sources, self.rows, self.model = resid.shape
        self.width = w_dec.shape[2]
        self.groups = lax.axis_size("grp")
        self.feats = lax.axis_size("feat")
        self.depth = self.feats // 2
        self.tokens = self.rows * self.groups
        self.rows_feat = self.tokens // self.feats
        self.per_group = self.rows // self.rows_feat
        self.pairs = self.per_group // 2
        self.chunks = WANTED_CHUNKS
        while self.rows_feat % (self.chunks * ROW_TILE):
            self.chunks -= 1
        self.piece = self.rows_feat // self.chunks
        self.block = self.per_group * self.piece
        self.chunk_rows = self.groups * self.block
        bits = [1 << i for i in range(self.groups.bit_length() - 1)]
        self.lanes = [bits[i:] + bits[:i] for i in range(len(bits))]
        starts = [i * self.sources // len(bits) for i in range(len(bits) + 1)]
        self.lane_sources = list(zip(starts[:-1], starts[1:]))
        self.level_bits = [1 << i for i in range(self.depth.bit_length() - 1)]

    def kept_order(self, lane):
        kept = [0]
        for bit in reversed(self.lanes[lane][1:]):
            kept = [j | bit for j in kept] + kept
        return kept


def streamed(count, slots, copies_of, body):
    for i in range(min(slots - 1, count)):
        for copy in copies_of(i, i):
            copy.start()

    @pl.loop(0, count)
    def _(i):
        ahead = i + slots - 1

        @pl.when(ahead < count)
        def _():
            for copy in copies_of(ahead, lax.rem(ahead, slots)):
                copy.start()

        slot = lax.rem(i, slots)
        for copy in copies_of(i, slot):
            copy.wait()
        body(i, slot)


def call(kernel, name, in_specs, out_shape, scratch, args, vmem=VMEM_BYTES, **options):
    return pl.pallas_call(
        kernel,
        in_specs=in_specs,
        out_shape=out_shape,
        scratch_shapes=scratch,
        cost_estimate=SMALL_COST,
        compiler_params=pltpu.CompilerParams(vmem_limit_bytes=vmem),
        name=name,
        **options,
    )(*args)


def encode_kernel(plan, source, resid_ref, w_ref, b_ref, out_ref, x_buf, w_buf, b_buf, x_sem, w_sem):
    tile = w_buf.shape[2]
    near = [
        pltpu.make_async_copy(resid_ref.at[source], x_buf, x_sem.at[0]),
        pltpu.make_async_copy(b_ref, b_buf, x_sem.at[1]),
    ]
    for copy in near:
        copy.start()

    def copies_of(i, slot):
        cols = pl.ds(pl.multiple_of(i * tile, tile), tile)
        return [pltpu.make_async_copy(w_ref.at[source, :, cols], w_buf.at[slot], w_sem.at[slot])]

    def step(i, slot):
        @pl.when(i == 0)
        def _():
            for copy in near:
                copy.wait()

        cols = pl.ds(pl.multiple_of(i * tile, tile), tile)
        product = jnp.dot(x_buf[...], w_buf[slot], preferred_element_type=F32)
        value = jnp.maximum(product + b_buf[source:source + 1, cols], 0.0)
        out_ref[:, cols] = value.astype(BF16)

    streamed(plan.width // tile, w_buf.shape[0], copies_of, step)


def encode(plan, source, resid, w_enc, b_enc):
    tile = pick_tile(plan.width, 256)
    return call(
        partial(encode_kernel, plan, source),
        "encode",
        [FAR, FAR, FAR],
        jax.ShapeDtypeStruct((plan.rows, plan.width), BF16),
        [
            pltpu.VMEM((plan.rows, plan.model), BF16),
            pltpu.VMEM((WEIGHT_SLOTS + 1, plan.model, tile), BF16),
            pltpu.VMEM((plan.sources, plan.width), F32),
            pltpu.SemaphoreType.DMA((2,)),
            pltpu.SemaphoreType.DMA((WEIGHT_SLOTS + 1,)),
        ],
        (resid, w_enc, b_enc),
        vmem=MOST_VMEM_BYTES,
    )


def decode_kernel(plan, index_ref, *refs):
    n_in = plan.groups * plan.sources
    pieces, w_ref, outs = refs[:n_in], refs[n_in], refs[n_in + 1:-4]
    x_buf, w_buf, x_sem, w_sem = refs[-4:]
    half = plan.tokens // 2
    core = index_ref[0]
    tile = w_buf.shape[2]

    placing = []
    for j in range(plan.groups):
        for b in range(plan.pairs):
            place = index_ref[1 + plan.sources + j * plan.pairs + b] * plan.rows_feat
            for owner in range(2):
                to = pl.multiple_of(place + jnp.where(core == owner, half, 0), ROW_TILE)
                for s in range(plan.sources):
                    placing.append(pltpu.make_async_copy(
                        pieces[s * plan.groups + j].at[
                            pl.ds((2 * b + owner) * plan.rows_feat, plan.rows_feat)
                        ],
                        x_buf.at[
                            pl.ds(to, plan.rows_feat), pl.ds(s * plan.width, plan.width)
                        ],
                        x_sem.at[len(placing)],
                    ))
    for copy in placing:
        copy.start()

    def copies_of(i, slot):
        cols = pl.ds(pl.multiple_of(i * tile, tile), tile)
        return [
            pltpu.make_async_copy(
                w_ref.at[s, 0, :, cols],
                w_buf.at[slot, pl.ds(s * plan.width, plan.width)],
                w_sem.at[slot, s],
            )
            for s in range(plan.sources)
        ]

    def step(i, slot):
        @pl.when(i == 0)
        def _():
            for copy in placing:
                copy.wait()
            for s in range(plan.sources):
                @pl.when(index_ref[1 + s] == 0)
                def _(s=s):
                    x_buf[:, s * plan.width:(s + 1) * plan.width] = jnp.zeros(
                        (plan.tokens, plan.width), BF16
                    )

        cols = pl.ds(pl.multiple_of(i * tile, tile), tile)
        product = jnp.dot(x_buf[...], w_buf[slot], preferred_element_type=F32)
        for c in range(plan.chunks):
            for d in range(plan.depth):
                first = d * plan.rows_feat + c * plan.piece
                to = slice(d * plan.piece, (d + 1) * plan.piece)
                outs[c][to, cols] = product[first:first + plan.piece].astype(BF16)
                outs[plan.chunks + c][to, cols] = product[half + first:half + first + plan.piece]

    streamed(plan.model // tile, w_buf.shape[0], copies_of, step)


def decode(plan, index, pieces, w_dec):
    tile = pick_tile(plan.model, 256)
    shape = (plan.depth * plan.piece, plan.model)
    outs = call(
        partial(decode_kernel, plan),
        "decode",
        [SCALARS] + [ANYWHERE] * len(pieces) + [FAR],
        [jax.ShapeDtypeStruct(shape, BF16)] * plan.chunks
        + [jax.ShapeDtypeStruct(shape, F32)] * plan.chunks,
        [
            pltpu.VMEM((plan.tokens, plan.sources * plan.width), BF16),
            pltpu.VMEM((WEIGHT_SLOTS, plan.sources * plan.width, tile), BF16),
            pltpu.SemaphoreType.DMA((len(pieces) * plan.per_group,)),
            pltpu.SemaphoreType.DMA((WEIGHT_SLOTS, plan.sources)),
        ],
        (index, *pieces, w_dec),
    )
    return outs[:plan.chunks], outs[plan.chunks:]


def gradient_kernel(plan, index_ref, *refs):
    n_in = 2 * plan.depth
    errors, w_ref, outs = refs[:n_in], refs[n_in], refs[n_in + 1:-4]
    e_buf, w_buf, e_sem, w_sem = refs[-4:]
    depth = pick_tile(plan.width, 256)
    steps = plan.width // depth
    base = 1 + plan.sources + plan.groups * plan.pairs

    placing = [
        pltpu.make_async_copy(
            errors[i],
            e_buf.at[
                pl.ds(pl.multiple_of(index_ref[base + i] * plan.piece, ROW_TILE), plan.piece)
            ],
            e_sem.at[i],
        )
        for i in range(n_in)
    ]
    for copy in placing:
        copy.start()
    def copies_of(i, slot):
        rows = pl.ds(pl.multiple_of(lax.rem(i, steps) * depth, depth), depth)
        return [pltpu.make_async_copy(
            w_ref.at[lax.div(i, steps), 0, rows], w_buf.at[slot], w_sem.at[slot]
        )]

    half = plan.groups // 2

    def step(i, slot):
        @pl.when(i == 0)
        def _():
            for copy in placing:
                copy.wait()

        source = lax.div(i, steps)
        cols = pl.ds(pl.multiple_of(lax.rem(i, steps) * depth, depth), depth)
        product = lax.dot_general(
            e_buf[...], w_buf[slot], (((1,), (1,)), ((), ())), preferred_element_type=F32
        )
        product = jnp.where(index_ref[1 + source] > 0, product, 0.0)
        for lane, (lo, hi) in enumerate(plan.lane_sources):
            first, kept = plan.lanes[lane][0], plan.kept_order(lane)
            away, keep = outs[2 * lane * half:][:half], outs[(2 * lane + 1) * half:][:half]

            @pl.when((source >= lo) & (source < hi))
            def _():
                for p, j in enumerate(kept):
                    far = (j ^ first) * plan.block
                    away[p][source - lo, :, cols] = product[far:far + plan.block].astype(BF16)
                    keep[p][source - lo, :, cols] = product[j * plan.block:(j + 1) * plan.block]

    streamed(plan.sources * steps, w_buf.shape[0], copies_of, step)

    def add_squares(i, total):
        rows = pl.ds(pl.multiple_of(i * ROW_TILE, ROW_TILE), ROW_TILE)
        value = e_buf[rows, :].astype(F32)
        value = value * value
        value = value[:8] + value[8:]
        for col in range(0, plan.model, 128):
            total = total + value[:, col:col + 128]
        return total

    outs[-1][...] = lax.fori_loop(
        0, plan.chunk_rows // ROW_TILE, add_squares, jnp.zeros((8, 128), F32)
    )


def gradient(plan, index, errors, w_dec):
    depth = pick_tile(plan.width, 256)
    half = plan.groups // 2
    out_shape = []
    for lo, hi in plan.lane_sources:
        shape = (hi - lo, plan.block, plan.width)
        out_shape += [jax.ShapeDtypeStruct(shape, BF16)] * half
        out_shape += [jax.ShapeDtypeStruct(shape, F32)] * half
    outs = call(
        partial(gradient_kernel, plan),
        "gradient",
        [SCALARS] + [ANYWHERE] * len(errors) + [FAR],
        out_shape + [jax.ShapeDtypeStruct((8, 128), F32)],
        [
            pltpu.VMEM((plan.chunk_rows, plan.model), BF16),
            pltpu.VMEM((2 * WEIGHT_SLOTS, depth, plan.model), BF16),
            pltpu.SemaphoreType.DMA((len(errors),)),
            pltpu.SemaphoreType.DMA((2 * WEIGHT_SLOTS,)),
        ],
        (index, *errors, w_dec),
    )
    lanes = [outs[2 * i * half:2 * (i + 1) * half] for i in range(len(plan.lanes))]
    return [(lane[:half], lane[half:]) for lane in lanes], outs[-1]


def finish_kernel(plan, chunk, with_previous, *refs):
    lanes = len(plan.lanes)
    kept, got = refs[:lanes], refs[lanes:2 * lanes]
    out_ref, stage, sem = refs[-3:]
    for lane, (lo, hi) in enumerate(plan.lane_sources):
        for s in range(lo, hi):
            stage[:, s, :] = kept[lane][s - lo] + got[lane][s - lo].astype(F32)
    copies = [
        pltpu.make_async_copy(
            stage.at[pl.ds(b * plan.piece, plan.piece)],
            out_ref.at[pl.ds((b * plan.chunks + chunk) * plan.piece, plan.piece)],
            sem.at[b],
        )
        for b in range(plan.per_group)
    ]
    for copy in copies:
        copy.start()
    for copy in copies:
        copy.wait()


def finish(plan, chunk, kept, got, previous):
    options = {}
    if previous is not None:
        options["input_output_aliases"] = {2 * len(kept): 0}
    previous = [] if previous is None else [previous]
    return call(
        partial(finish_kernel, plan, chunk, bool(previous)),
        "finish",
        [NEAR] * (2 * len(kept)) + [FAR] * len(previous),
        jax.ShapeDtypeStruct((plan.rows, plan.sources, plan.width), F32),
        [
            pltpu.VMEM((plan.block, plan.sources, plan.width), F32),
            pltpu.SemaphoreType.DMA((plan.per_group,)),
        ],
        (*kept, *got, *previous),
        out_specs=FAR,
        **options,
    )


def per_device(resid, w_enc, b_enc, w_dec, targets, start_layer):
    plan = Plan(resid, w_dec)
    group = lax.axis_index("grp").astype(jnp.int32)
    feat = lax.axis_index("feat").astype(jnp.int32)
    core, level = feat % 2, feat // 2
    groups, feats, chunks = plan.groups, plan.feats, plan.chunks

    feeds = (group >= start_layer[:, 0]).astype(jnp.int32)
    offsets = [
        ((group ^ j) * plan.pairs + b) ^ level
        for j in range(groups)
        for b in range(plan.pairs)
    ]
    places = []
    for other in range(2):
        for d in range(plan.depth):
            owner = level ^ d
            place = ((owner // plan.pairs) ^ group) * plan.pairs + owner % plan.pairs
            places.append(place * 2 + (core ^ other))
    index = jnp.concatenate([core[None], feeds, jnp.stack(offsets), jnp.stack(places)])

    encoded = [encode(plan, s, resid, w_enc, b_enc) for s in range(plan.sources)]
    active = with_layout_constraint(jnp.stack(encoded, axis=1), Layout((0, 1, 2)))

    pieces, arrived = [], []
    for s, mine in enumerate(encoded):
        bits = plan.lanes[s % len(plan.lanes)]
        mine, = after([mine], arrived[s - 2] if s >= 2 else [])
        held = {0: mine}
        for bit in bits:
            held.update(
                {j | bit: swap(x, "grp", groups, bit) for j, x in list(held.items())}
            )
        pieces += [held[j] for j in range(groups)]
        arrived.append([held[bit] for bit in bits])

    sends, keeps = decode(plan, index, after(pieces, [active]), w_dec)
    partial_rows = []
    earlier = []
    for c in range(chunks):
        other = swap(sends[c], "feat", feats, 1)
        held = {
            d: keeps[c][d * plan.piece:(d + 1) * plan.piece]
            + other[d * plan.piece:(d + 1) * plan.piece].astype(F32)
            for d in range(plan.depth)
        }
        for bit in plan.level_bits:
            away = {d: held.pop(d).astype(BF16) for d in sorted(held, reverse=True) if d & bit}
            if bit == plan.level_bits[0]:
                away = dict(zip(away, after(away.values(), earlier)))
            got = {d: swap(x, "feat", feats, 2 * bit) for d, x in away.items()}
            if bit == plan.level_bits[0]:
                earlier = list(got.values())[:1]
            for d, x in got.items():
                held[d ^ bit] = held[d ^ bit] + x.astype(F32)
        partial_rows.append(held[0])

    recon_parts, errors, first_errors = [], [], []
    for c in range(chunks):
        recon_rows, = after([partial_rows[c]], first_errors[-1:])
        first = feat * plan.rows_feat + c * plan.piece
        own_targets = lax.dynamic_slice_in_dim(targets[0], first, plan.piece, 0)
        difference = recon_rows - own_targets.astype(F32)
        recon_parts.append(recon_rows.astype(BF16))
        held = {0: difference.astype(BF16)}
        for bit in reversed(plan.level_bits):
            held.update(
                {d | bit: swap(x, "feat", feats, 2 * bit) for d, x in list(held.items())}
            )
        first_errors.append(held[plan.level_bits[-1]])
        every = [held[d] for d in range(plan.depth)]
        errors.append(every + [swap(e, "feat", feats, 1) for e in every])

    squares = jnp.zeros((8, 128), F32)
    feat_grad = None
    earlier, first_got = [], []
    for c in range(chunks):
        ready = after(errors[c], [e[0] for e in errors[c + 1:c + 2]] + first_got)
        lanes, total = gradient(plan, index, ready, w_dec)
        squares = squares + total
        kept_all, got_all, second, first_got = [], [], [], []
        for bits, (away, kept) in zip(plan.lanes, lanes):
            away = after(away, earlier)
            for step, bit in enumerate(bits):
                got = [swap(x, "grp", groups, bit) for x in away]
                cut = len(got) // 2
                if cut:
                    sums = [x + y.astype(F32) for x, y in zip(kept, got)]
                    away, kept = [x.astype(BF16) for x in sums[:cut]], sums[cut:]
                    if not step:
                        first_got.append(got[0])
                        second += away
                        away = after(away, [] if feat_grad is None else [feat_grad])
            kept_all.append(kept[0])
            got_all.append(got[0])
        feat_grad = finish(plan, c, kept_all, got_all, feat_grad)
        earlier = second

    loss = jnp.full((8, 128), jnp.sum(squares), F32)
    for i, bit in enumerate(1 << i for i in range(groups.bit_length() - 1)):
        loss = loss + swap(loss, "grp", groups, bit)
        if not i:
            loss, = after([loss], first_got)
    entries = targets.shape[0] * groups * plan.tokens * plan.model
    recon_loss = loss[0, 0] / entries
    recon = jnp.concatenate(recon_parts, axis=0)[None]
    return active, recon, recon_loss, feat_grad


def solution(mesh):
    in_specs = (
        P(None, "grp", None),
        P(None, None, "feat"),
        P(None, "feat"),
        P(None, "grp", "feat", None),
        P("grp", None, None),
        P(None, "feat"),
    )
    out_specs = (P("grp", None, "feat"), P("grp", "feat", None), P(), P("grp", None, "feat"))
    return jax.shard_map(
        per_device, mesh=mesh, in_specs=in_specs, out_specs=out_specs, check_vma=False
    )
```

```python
from functools import partial

import jax
import jax.numpy as jnp
from jax import lax
from jax.experimental import pallas as pl
from jax.experimental.pallas import tpu as pltpu
from jax.sharding import PartitionSpec as P

BF16 = jnp.bfloat16
F32 = jnp.float32
WANTED_CHUNKS = 2
ROW_TILE = 16
WEIGHT_SLOTS = 4
VMEM_BYTES = 44 << 20
MOST_VMEM_BYTES = 59 << 20
SMALL_COST = pl.CostEstimate(flops=1 << 20, bytes_accessed=1 << 10, transcendentals=0)
FAR = pl.BlockSpec(memory_space=pltpu.HBM)
ANYWHERE = pl.BlockSpec(memory_space=pl.ANY)
SCALARS = pl.BlockSpec(memory_space=pltpu.SMEM)
NEAR = pl.BlockSpec(memory_space=pltpu.VMEM)


def pick_tile(size, wanted):
    return wanted if size % wanted == 0 else size


def swap(x, axis, size, offset):
    return lax.ppermute(x, axis, [(i, i ^ offset) for i in range(size)])


def after(values, earlier):
    if not earlier:
        return list(values)
    return list(lax.optimization_barrier(list(values) + list(earlier)))[:len(values)]


class Plan:
    def __init__(self, resid, w_dec):
        self.sources, self.rows, self.model = resid.shape
        self.width = w_dec.shape[2]
        self.groups = lax.axis_size("grp")
        self.feats = lax.axis_size("feat")
        self.depth = self.feats // 2
        self.tokens = self.rows * self.groups
        self.rows_feat = self.tokens // self.feats
        self.per_group = self.rows // self.rows_feat
        self.pairs = self.per_group // 2
        self.chunks = WANTED_CHUNKS
        while self.rows_feat % (self.chunks * ROW_TILE):
            self.chunks -= 1
        self.piece = self.rows_feat // self.chunks
        self.block = self.per_group * self.piece
        self.chunk_rows = self.groups * self.block
        bits = [1 << i for i in range(self.groups.bit_length() - 1)]
        self.lanes = [bits[i:] + bits[:i] for i in range(len(bits))]
        starts = [i * self.sources // len(bits) for i in range(len(bits) + 1)]
        self.lane_sources = list(zip(starts[:-1], starts[1:]))
        self.level_bits = [1 << i for i in range(self.depth.bit_length() - 1)]

    def kept_order(self, lane):
        kept = [0]
        for bit in reversed(self.lanes[lane][1:]):
            kept = [j | bit for j in kept] + kept
        return kept


def streamed(count, slots, copies_of, body):
    early = min(2, slots - 1, count)
    for i in range(early):
        for copy in copies_of(i, i):
            copy.start()

    @pl.loop(0, count)
    def _(i):
        ahead = i + slots - 1

        @pl.when(i == 0)
        def _():
            for copy in copies_of(0, 0):
                copy.wait()
            for later in range(early, min(slots, count)):
                for copy in copies_of(later, later):
                    copy.start()

        @pl.when((i > 0) & (ahead < count))
        def _():
            for copy in copies_of(ahead, lax.rem(ahead, slots)):
                copy.start()

        slot = lax.rem(i, slots)

        @pl.when(i > 0)
        def _():
            for copy in copies_of(i, slot):
                copy.wait()

        body(i, slot)


def call(kernel, name, in_specs, out_shape, scratch, args, vmem=VMEM_BYTES, **options):
    return pl.pallas_call(
        kernel,
        in_specs=in_specs,
        out_shape=out_shape,
        scratch_shapes=scratch,
        cost_estimate=SMALL_COST,
        compiler_params=pltpu.CompilerParams(vmem_limit_bytes=vmem),
        name=name,
        **options,
    )(*args)


def encode_kernel(plan, source, resid_ref, w_ref, b_ref, out_ref, x_buf, w_buf, b_buf, x_sem, w_sem):
    tile = w_buf.shape[2]
    near = [
        pltpu.make_async_copy(resid_ref.at[source], x_buf, x_sem.at[0]),
        pltpu.make_async_copy(b_ref, b_buf, x_sem.at[1]),
    ]
    for copy in near:
        copy.start()

    def copies_of(i, slot):
        cols = pl.ds(pl.multiple_of(i * tile, tile), tile)
        return [pltpu.make_async_copy(w_ref.at[source, :, cols], w_buf.at[slot], w_sem.at[slot])]

    def step(i, slot):
        @pl.when(i == 0)
        def _():
            for copy in near:
                copy.wait()

        cols = pl.ds(pl.multiple_of(i * tile, tile), tile)
        product = jnp.dot(x_buf[...], w_buf[slot], preferred_element_type=F32)
        value = jnp.maximum(product + b_buf[source:source + 1, cols], 0.0)
        out_ref[:, cols] = value.astype(BF16)

    streamed(plan.width // tile, w_buf.shape[0], copies_of, step)


def encode(plan, source, resid, w_enc, b_enc):
    tile = pick_tile(plan.width, 256)
    return call(
        partial(encode_kernel, plan, source),
        "encode",
        [FAR, FAR, FAR],
        jax.ShapeDtypeStruct((plan.rows, plan.width), BF16),
        [
            pltpu.VMEM((plan.rows, plan.model), BF16),
            pltpu.VMEM((WEIGHT_SLOTS + 1, plan.model, tile), BF16),
            pltpu.VMEM((plan.sources, plan.width), F32),
            pltpu.SemaphoreType.DMA((2,)),
            pltpu.SemaphoreType.DMA((WEIGHT_SLOTS + 1,)),
        ],
        (resid, w_enc, b_enc),
        vmem=MOST_VMEM_BYTES,
    )


def arrange_kernel(plan, *refs):
    parts, out_ref, stage = refs[:plan.sources], refs[-2], refs[-1]
    count = stage.shape[0]

    @pl.loop(0, plan.rows // count)
    def _(i):
        rows = pl.ds(pl.multiple_of(i * count, count), count)
        for s in range(plan.sources):
            stage[:, s, :] = parts[s][rows, :].astype(F32)
        out_ref[rows] = stage[...].astype(BF16)


def arrange(plan, encoded):
    return call(
        partial(arrange_kernel, plan),
        "arrange",
        [NEAR] * plan.sources,
        jax.ShapeDtypeStruct((plan.rows, plan.sources, plan.width), BF16),
        [pltpu.VMEM((ROW_TILE, plan.sources, plan.width), F32)],
        encoded,
    )


def decode_kernel(plan, lo, hi, index_ref, *refs):
    n_in = plan.groups * (hi - lo)
    pieces, w_ref, outs = refs[:n_in], refs[n_in], refs[n_in + 1:-4]
    x_buf, w_buf, x_sem, w_sem = refs[-4:]
    if lo:
        before_ref, outs, before_buf = outs[0], outs[1:-1], outs[-1]
    half = plan.tokens // 2
    core = index_ref[0]
    tile = w_buf.shape[2]

    placing = []
    for j in range(plan.groups):
        for b in range(plan.pairs):
            place = index_ref[1 + plan.sources + j * plan.pairs + b] * plan.rows_feat
            for owner in range(2):
                to = pl.multiple_of(place + jnp.where(core == owner, half, 0), ROW_TILE)
                for s in range(hi - lo):
                    placing.append(pltpu.make_async_copy(
                        pieces[s * plan.groups + j].at[
                            pl.ds((2 * b + owner) * plan.rows_feat, plan.rows_feat)
                        ],
                        x_buf.at[
                            pl.ds(to, plan.rows_feat), pl.ds(s * plan.width, plan.width)
                        ],
                        x_sem.at[len(placing)],
                    ))
    for copy in placing:
        copy.start()

    def copies_of(i, slot):
        cols = pl.ds(pl.multiple_of(i * tile, tile), tile)
        copies = [
            pltpu.make_async_copy(
                w_ref.at[s, 0, :, cols],
                w_buf.at[slot, pl.ds((s - lo) * plan.width, plan.width)],
                w_sem.at[slot, s - lo],
            )
            for s in range(lo, hi)
        ]
        if lo:
            copies.append(pltpu.make_async_copy(
                before_ref.at[:, cols], before_buf.at[slot], w_sem.at[slot, hi - lo]
            ))
        return copies

    def step(i, slot):
        @pl.when(i == 0)
        def _():
            for copy in placing:
                copy.wait()
            for s in range(lo, hi):
                @pl.when(index_ref[1 + s] == 0)
                def _(s=s - lo):
                    x_buf[:, s * plan.width:(s + 1) * plan.width] = jnp.zeros(
                        (plan.tokens, plan.width), BF16
                    )

        cols = pl.ds(pl.multiple_of(i * tile, tile), tile)
        product = jnp.dot(x_buf[...], w_buf[slot], preferred_element_type=F32)
        if lo:
            product = product + before_buf[slot]
        if hi < plan.sources:
            outs[0][:, cols] = product
            return
        for c in range(plan.chunks):
            for d in range(plan.depth):
                first = d * plan.rows_feat + c * plan.piece
                to = slice(d * plan.piece, (d + 1) * plan.piece)
                outs[c][to, cols] = product[first:first + plan.piece].astype(BF16)
                outs[plan.chunks + c][to, cols] = product[half + first:half + first + plan.piece]

    streamed(plan.model // tile, w_buf.shape[0], copies_of, step)


def decode(plan, lo, hi, index, pieces, w_dec, before):
    tile = pick_tile(plan.model, 256)
    shape = (plan.depth * plan.piece, plan.model)
    if hi < plan.sources:
        out_shape = [jax.ShapeDtypeStruct((plan.tokens, plan.model), F32)]
    else:
        out_shape = [jax.ShapeDtypeStruct(shape, BF16)] * plan.chunks
        out_shape += [jax.ShapeDtypeStruct(shape, F32)] * plan.chunks
    scratch = [
        pltpu.VMEM((plan.tokens, (hi - lo) * plan.width), BF16),
        pltpu.VMEM((WEIGHT_SLOTS, (hi - lo) * plan.width, tile), BF16),
        pltpu.SemaphoreType.DMA((len(pieces) * plan.per_group,)),
        pltpu.SemaphoreType.DMA((WEIGHT_SLOTS, hi - lo + 1)),
    ]
    if before:
        scratch = [pltpu.VMEM((WEIGHT_SLOTS, plan.tokens, tile), F32)] + scratch
    return call(
        partial(decode_kernel, plan, lo, hi),
        "decode",
        [SCALARS] + [ANYWHERE] * len(pieces) + [FAR] * (1 + len(before)),
        out_shape,
        scratch,
        (index, *pieces, w_dec, *before),
        vmem=MOST_VMEM_BYTES,
    )


def gradient_kernel(plan, index_ref, *refs):
    n_in = 2 * plan.depth
    errors, w_ref, outs = refs[:n_in], refs[n_in], refs[n_in + 1:-4]
    e_buf, w_buf, e_sem, w_sem = refs[-4:]
    depth = pick_tile(plan.width, 256)
    steps = plan.width // depth
    base = 1 + plan.sources + plan.groups * plan.pairs

    placing = [
        pltpu.make_async_copy(
            errors[i],
            e_buf.at[
                pl.ds(pl.multiple_of(index_ref[base + i] * plan.piece, ROW_TILE), plan.piece)
            ],
            e_sem.at[i],
        )
        for i in range(n_in)
    ]
    for copy in placing:
        copy.start()
    def copies_of(i, slot):
        rows = pl.ds(pl.multiple_of(lax.rem(i, steps) * depth, depth), depth)
        return [pltpu.make_async_copy(
            w_ref.at[lax.div(i, steps), 0, rows], w_buf.at[slot], w_sem.at[slot]
        )]

    half = plan.groups // 2

    def step(i, slot):
        @pl.when(i == 0)
        def _():
            for copy in placing:
                copy.wait()

        source = lax.div(i, steps)
        cols = pl.ds(pl.multiple_of(lax.rem(i, steps) * depth, depth), depth)
        product = lax.dot_general(
            e_buf[...], w_buf[slot], (((1,), (1,)), ((), ())), preferred_element_type=F32
        )
        product = jnp.where(index_ref[1 + source] > 0, product, 0.0)
        for lane, (lo, hi) in enumerate(plan.lane_sources):
            first, kept = plan.lanes[lane][0], plan.kept_order(lane)
            away, keep = outs[2 * lane * half:][:half], outs[(2 * lane + 1) * half:][:half]

            @pl.when((source >= lo) & (source < hi))
            def _():
                for p, j in enumerate(kept):
                    far = (j ^ first) * plan.block
                    away[p][source - lo, :, cols] = product[far:far + plan.block].astype(BF16)
                    keep[p][source - lo, :, cols] = product[j * plan.block:(j + 1) * plan.block]

    streamed(plan.sources * steps, w_buf.shape[0], copies_of, step)

    def add_squares(i, total):
        rows = pl.ds(pl.multiple_of(i * ROW_TILE, ROW_TILE), ROW_TILE)
        value = e_buf[rows, :].astype(F32)
        value = value * value
        value = value[:8] + value[8:]
        for col in range(0, plan.model, 128):
            total = total + value[:, col:col + 128]
        return total

    outs[-1][...] = lax.fori_loop(
        0, plan.chunk_rows // ROW_TILE, add_squares, jnp.zeros((8, 128), F32)
    )


def gradient(plan, index, errors, w_dec):
    depth = pick_tile(plan.width, 256)
    half = plan.groups // 2
    out_shape = []
    for lo, hi in plan.lane_sources:
        shape = (hi - lo, plan.block, plan.width)
        out_shape += [jax.ShapeDtypeStruct(shape, BF16)] * half
        out_shape += [jax.ShapeDtypeStruct(shape, F32)] * half
    outs = call(
        partial(gradient_kernel, plan),
        "gradient",
        [SCALARS] + [ANYWHERE] * len(errors) + [FAR],
        out_shape + [jax.ShapeDtypeStruct((8, 128), F32)],
        [
            pltpu.VMEM((plan.chunk_rows, plan.model), BF16),
            pltpu.VMEM((2 * WEIGHT_SLOTS, depth, plan.model), BF16),
            pltpu.SemaphoreType.DMA((len(errors),)),
            pltpu.SemaphoreType.DMA((2 * WEIGHT_SLOTS,)),
        ],
        (index, *errors, w_dec),
    )
    lanes = [outs[2 * i * half:2 * (i + 1) * half] for i in range(len(plan.lanes))]
    return [(lane[:half], lane[half:]) for lane in lanes], outs[-1]


def finish_kernel(plan, chunk, with_previous, *refs):
    lanes = len(plan.lanes)
    kept, got = refs[:lanes], refs[lanes:2 * lanes]
    out_ref, stage, sem = refs[-3:]
    for lane, (lo, hi) in enumerate(plan.lane_sources):
        for s in range(lo, hi):
            stage[:, s, :] = kept[lane][s - lo] + got[lane][s - lo].astype(F32)
    copies = [
        pltpu.make_async_copy(
            stage.at[pl.ds(b * plan.piece, plan.piece)],
            out_ref.at[pl.ds((b * plan.chunks + chunk) * plan.piece, plan.piece)],
            sem.at[b],
        )
        for b in range(plan.per_group)
    ]
    for copy in copies:
        copy.start()
    for copy in copies:
        copy.wait()


def finish(plan, chunk, kept, got, previous):
    options = {}
    if previous is not None:
        options["input_output_aliases"] = {2 * len(kept): 0}
    previous = [] if previous is None else [previous]
    return call(
        partial(finish_kernel, plan, chunk, bool(previous)),
        "finish",
        [NEAR] * (2 * len(kept)) + [FAR] * len(previous),
        jax.ShapeDtypeStruct((plan.rows, plan.sources, plan.width), F32),
        [
            pltpu.VMEM((plan.block, plan.sources, plan.width), F32),
            pltpu.SemaphoreType.DMA((plan.per_group,)),
        ],
        (*kept, *got, *previous),
        out_specs=FAR,
        **options,
    )


def per_device(resid, w_enc, b_enc, w_dec, targets, start_layer):
    plan = Plan(resid, w_dec)
    group = lax.axis_index("grp").astype(jnp.int32)
    feat = lax.axis_index("feat").astype(jnp.int32)
    core, level = feat % 2, feat // 2
    groups, feats, chunks = plan.groups, plan.feats, plan.chunks

    feeds = (group >= start_layer[:, 0]).astype(jnp.int32)
    offsets = [
        ((group ^ j) * plan.pairs + b) ^ level
        for j in range(groups)
        for b in range(plan.pairs)
    ]
    places = []
    for other in range(2):
        for d in range(plan.depth):
            owner = level ^ d
            place = ((owner // plan.pairs) ^ group) * plan.pairs + owner % plan.pairs
            places.append(place * 2 + (core ^ other))
    index = jnp.concatenate([core[None], feeds, jnp.stack(offsets), jnp.stack(places)])

    encoded = [encode(plan, s, resid, w_enc, b_enc) for s in range(plan.sources)]
    active = arrange(plan, encoded)

    pieces, arrived = [], []
    for s, mine in enumerate(encoded):
        bits = plan.lanes[s % len(plan.lanes)]
        mine, = after([mine], arrived[min(s, 2) - 1] if s else [])
        held = {0: mine}
        for bit in bits:
            held.update(
                {j | bit: swap(x, "grp", groups, bit) for j, x in list(held.items())}
            )
        pieces += [held[j] for j in range(groups)]
        arrived.append([held[bit] for bit in bits])

    middle = plan.sources // 2
    head, tail = pieces[:middle * groups], pieces[middle * groups:]
    before = decode(plan, 0, middle, index, after(head, encoded), w_dec, [])
    tail = after(tail, [active, *before])
    decoded = decode(plan, middle, plan.sources, index, tail, w_dec, before)
    sends, keeps = decoded[:chunks], decoded[chunks:]
    recon_parts, errors, first_errors = [], [], []
    earlier = []
    for c in range(chunks):
        other = swap(sends[c], "feat", feats, 1)
        held = {
            d: keeps[c][d * plan.piece:(d + 1) * plan.piece]
            + other[d * plan.piece:(d + 1) * plan.piece].astype(F32)
            for d in range(plan.depth)
        }
        for step, bit in enumerate(plan.level_bits):
            away = {d: held.pop(d).astype(BF16) for d in sorted(held, reverse=True) if d & bit}
            wait = earlier if not step else first_errors[-1:]
            away = dict(zip(away, after(away.values(), wait)))
            got = {d: swap(x, "feat", feats, 2 * bit) for d, x in away.items()}
            if not step:
                earlier = list(got.values())[:1]
            for d, x in got.items():
                held[d ^ bit] = held[d ^ bit] + x.astype(F32)
        recon_rows, = after([held[0]], first_errors[-1:])

        first = feat * plan.rows_feat + c * plan.piece
        own_targets = lax.dynamic_slice_in_dim(targets[0], first, plan.piece, 0)
        difference = recon_rows - own_targets.astype(F32)
        recon_parts.append(recon_rows.astype(BF16))
        error = difference.astype(BF16)
        held = {0: error}
        if c:
            for d in range(plan.depth - 1, 0, -1):
                held[d] = swap(error, "feat", feats, 2 * d)
        else:
            for bit in reversed(plan.level_bits):
                held.update(
                    {d | bit: swap(x, "feat", feats, 2 * bit) for d, x in list(held.items())}
                )
        first_errors.append(held[plan.level_bits[-1]])
        every = [held[d] for d in range(plan.depth)]
        errors.append(every + [swap(e, "feat", feats, 1) for e in every])

    squares = jnp.zeros((8, 128), F32)
    feat_grad = None
    earlier, first_got = [], []
    for c in range(chunks):
        ready = after(errors[c], [e[0] for e in errors[c + 1:c + 2]] + first_got)
        lanes, total = gradient(plan, index, ready, w_dec)
        squares = squares + total
        kept_all, got_all, second, first_got = [], [], [], []
        for bits, (away, kept) in zip(plan.lanes, lanes):
            away = after(away, earlier)
            for step, bit in enumerate(bits):
                got = [swap(x, "grp", groups, bit) for x in away]
                cut = len(got) // 2
                if cut:
                    sums = [x + y.astype(F32) for x, y in zip(kept, got)]
                    away, kept = [x.astype(BF16) for x in sums[:cut]], sums[cut:]
                    if not step:
                        first_got.append(got[0])
                        second += away
            kept_all.append(kept[0])
            got_all.append(got[0])
        previous = feat_grad
        feat_grad = finish(plan, c, kept_all, got_all, previous)
        earlier = second

    squares, = after([squares], second)
    loss = jnp.full((8, 128), jnp.sum(squares), F32)
    for i, bit in enumerate(1 << i for i in range(groups.bit_length() - 1)):
        loss = loss + swap(loss, "grp", groups, bit)
        if not i and previous is not None:
            loss, = after([loss], [previous])
    entries = targets.shape[0] * groups * plan.tokens * plan.model
    recon_loss = loss[0, 0] / entries
    recon = jnp.concatenate(recon_parts, axis=0)[None]
    return active, recon, recon_loss, feat_grad


def solution(mesh):
    in_specs = (
        P(None, "grp", None),
        P(None, None, "feat"),
        P(None, "feat"),
        P(None, "grp", "feat", None),
        P("grp", None, None),
        P(None, "feat"),
    )
    out_specs = (P("grp", None, "feat"), P("grp", "feat", None), P(), P("grp", None, "feat"))
    return jax.shard_map(
        per_device, mesh=mesh, in_specs=in_specs, out_specs=out_specs, check_vma=False
    )
```

```python
from functools import partial

import jax
import jax.numpy as jnp
from jax import lax
from jax.experimental import pallas as pl
from jax.experimental.pallas import tpu as pltpu
from jax.sharding import PartitionSpec as P

BF16 = jnp.bfloat16
F32 = jnp.float32
WANTED_CHUNKS = 2
ROW_TILE = 16
WEIGHT_SLOTS = 4
VMEM_BYTES = 44 << 20
MOST_VMEM_BYTES = 59 << 20
SMALL_COST = pl.CostEstimate(flops=1 << 20, bytes_accessed=1 << 10, transcendentals=0)
FAR = pl.BlockSpec(memory_space=pltpu.HBM)
ANYWHERE = pl.BlockSpec(memory_space=pl.ANY)
SCALARS = pl.BlockSpec(memory_space=pltpu.SMEM)
NEAR = pl.BlockSpec(memory_space=pltpu.VMEM)


def pick_tile(size, wanted):
    return wanted if size % wanted == 0 else size


def swap(x, axis, size, offset):
    return lax.ppermute(x, axis, [(i, i ^ offset) for i in range(size)])


def after(values, earlier):
    if not earlier:
        return list(values)
    return list(lax.optimization_barrier(list(values) + list(earlier)))[:len(values)]


class Plan:
    def __init__(self, resid, w_dec):
        self.sources, self.rows, self.model = resid.shape
        self.width = w_dec.shape[2]
        self.groups = lax.axis_size("grp")
        self.feats = lax.axis_size("feat")
        self.depth = self.feats // 2
        self.tokens = self.rows * self.groups
        self.rows_feat = self.tokens // self.feats
        self.per_group = self.rows // self.rows_feat
        self.pairs = self.per_group // 2
        self.chunks = WANTED_CHUNKS
        while self.rows_feat % (self.chunks * ROW_TILE):
            self.chunks -= 1
        self.piece = self.rows_feat // self.chunks
        self.block = self.per_group * self.piece
        self.chunk_rows = self.groups * self.block
        bits = [1 << i for i in range(self.groups.bit_length() - 1)]
        self.lanes = [bits[i:] + bits[:i] for i in range(len(bits))]
        starts = [i * self.sources // len(bits) for i in range(len(bits) + 1)]
        self.lane_sources = list(zip(starts[:-1], starts[1:]))
        self.level_bits = [1 << i for i in range(self.depth.bit_length() - 1)]

    def kept_order(self, lane):
        kept = [0]
        for bit in reversed(self.lanes[lane][1:]):
            kept = [j | bit for j in kept] + kept
        return kept


def streamed(count, slots, copies_of, body):
    early = min(1, slots - 1, count)
    for i in range(early):
        for copy in copies_of(i, i):
            copy.start()

    @pl.loop(0, count)
    def _(i):
        ahead = i + slots - 1

        @pl.when(i == 0)
        def _():
            for copy in copies_of(0, 0):
                copy.wait()
            for later in range(early, min(slots, count)):
                for copy in copies_of(later, later):
                    copy.start()

        @pl.when((i > 0) & (ahead < count))
        def _():
            for copy in copies_of(ahead, lax.rem(ahead, slots)):
                copy.start()

        slot = lax.rem(i, slots)

        @pl.when(i > 0)
        def _():
            for copy in copies_of(i, slot):
                copy.wait()

        body(i, slot)


def call(kernel, name, in_specs, out_shape, scratch, args, vmem=VMEM_BYTES, **options):
    return pl.pallas_call(
        kernel,
        in_specs=in_specs,
        out_shape=out_shape,
        scratch_shapes=scratch,
        cost_estimate=SMALL_COST,
        compiler_params=pltpu.CompilerParams(vmem_limit_bytes=vmem),
        name=name,
        **options,
    )(*args)


def encode_kernel(plan, lo, hi, resid_ref, w_ref, b_ref, *refs):
    outs, (x_buf, w_buf, b_buf, x_sem, w_sem) = refs[:hi - lo], refs[hi - lo:]
    tile = w_buf.shape[2]
    steps = plan.width // tile
    near = [
        pltpu.make_async_copy(resid_ref.at[pl.ds(lo, hi - lo)], x_buf, x_sem.at[0]),
        pltpu.make_async_copy(b_ref, b_buf, x_sem.at[1]),
    ]
    for copy in near:
        copy.start()

    def copies_of(i, slot):
        cols = pl.ds(pl.multiple_of(lax.rem(i, steps) * tile, tile), tile)
        return [pltpu.make_async_copy(
            w_ref.at[lo + lax.div(i, steps), :, cols], w_buf.at[slot], w_sem.at[slot]
        )]

    def step(i, slot):
        @pl.when(i == 0)
        def _():
            for copy in near:
                copy.wait()

        source = lax.div(i, steps)
        cols = pl.ds(pl.multiple_of(lax.rem(i, steps) * tile, tile), tile)
        product = jnp.dot(x_buf[source], w_buf[slot], preferred_element_type=F32)
        bias = b_buf[pl.ds(lo + source, 1), cols]
        value = jnp.maximum(product + bias, 0.0).astype(BF16)
        for s in range(hi - lo):
            @pl.when(source == s)
            def _():
                outs[s][:, cols] = value

    streamed((hi - lo) * steps, w_buf.shape[0], copies_of, step)


def encode(plan, lo, hi, resid, w_enc, b_enc):
    tile = pick_tile(plan.width, 256)
    return call(
        partial(encode_kernel, plan, lo, hi),
        "encode",
        [FAR, FAR, FAR],
        [jax.ShapeDtypeStruct((plan.rows, plan.width), BF16)] * (hi - lo),
        [
            pltpu.VMEM((hi - lo, plan.rows, plan.model), BF16),
            pltpu.VMEM((WEIGHT_SLOTS + 1, plan.model, tile), BF16),
            pltpu.VMEM((plan.sources, plan.width), F32),
            pltpu.SemaphoreType.DMA((2,)),
            pltpu.SemaphoreType.DMA((WEIGHT_SLOTS + 1,)),
        ],
        (resid, w_enc, b_enc),
        vmem=MOST_VMEM_BYTES,
    )


def arrange_kernel(plan, *refs):
    parts, out_ref, stage = refs[:plan.sources], refs[-2], refs[-1]
    count = stage.shape[0]

    @pl.loop(0, plan.rows // count)
    def _(i):
        rows = pl.ds(pl.multiple_of(i * count, count), count)
        for s in range(plan.sources):
            stage[:, s, :] = parts[s][rows, :].astype(F32)
        out_ref[rows] = stage[...].astype(BF16)


def arrange(plan, encoded):
    return call(
        partial(arrange_kernel, plan),
        "arrange",
        [NEAR] * plan.sources,
        jax.ShapeDtypeStruct((plan.rows, plan.sources, plan.width), BF16),
        [pltpu.VMEM((ROW_TILE, plan.sources, plan.width), F32)],
        encoded,
    )


def decode_kernel(plan, index_ref, *refs):
    n_in = plan.groups * plan.sources
    pieces, w_ref, outs = refs[:n_in], refs[n_in], refs[n_in + 1:-7]
    x_buf, w_buf, send_buf, keep_buf, x_sem, w_sem, out_sem = refs[-7:]
    half = plan.tokens // 2
    core = index_ref[0]
    tile = w_buf.shape[2]
    count = plan.model // tile

    placing = []
    for j in range(plan.groups):
        for b in range(plan.pairs):
            place = index_ref[1 + plan.sources + j * plan.pairs + b] * plan.rows_feat
            for owner in range(2):
                to = pl.multiple_of(place + jnp.where(core == owner, half, 0), ROW_TILE)
                for s in range(plan.sources):
                    placing.append(pltpu.make_async_copy(
                        pieces[s * plan.groups + j].at[
                            pl.ds((2 * b + owner) * plan.rows_feat, plan.rows_feat)
                        ],
                        x_buf.at[
                            pl.ds(to, plan.rows_feat), pl.ds(s * plan.width, plan.width)
                        ],
                        x_sem.at[len(placing)],
                    ))
    for copy in placing:
        copy.start()

    def columns(i):
        return pl.ds(pl.multiple_of(i * tile, tile), tile)

    def copies_of(i, slot):
        return [
            pltpu.make_async_copy(
                w_ref.at[s, 0, :, columns(i)],
                w_buf.at[slot, pl.ds(s * plan.width, plan.width)],
                w_sem.at[slot, s],
            )
            for s in range(plan.sources)
        ]

    def leaving(i):
        slot = lax.rem(i, 2)
        return [
            pltpu.make_async_copy(
                buf.at[slot, c],
                outs[n * plan.chunks + c].at[:, columns(i)],
                out_sem.at[slot, n * plan.chunks + c],
            )
            for n, buf in enumerate((send_buf, keep_buf))
            for c in range(plan.chunks)
        ]

    def step(i, slot):
        @pl.when(i == 0)
        def _():
            for copy in placing:
                copy.wait()
            for s in range(plan.sources):
                @pl.when(index_ref[1 + s] == 0)
                def _(s=s):
                    x_buf[:, s * plan.width:(s + 1) * plan.width] = jnp.zeros(
                        (plan.tokens, plan.width), BF16
                    )

        @pl.when(i >= 2)
        def _():
            for copy in leaving(i - 2):
                copy.wait()

        product = jnp.dot(x_buf[...], w_buf[slot], preferred_element_type=F32)
        out_slot = lax.rem(i, 2)
        for c in range(plan.chunks):
            for d in range(plan.depth):
                first = d * plan.rows_feat + c * plan.piece
                to = slice(d * plan.piece, (d + 1) * plan.piece)
                send_buf[out_slot, c, to, :] = product[first:first + plan.piece].astype(BF16)
                keep_buf[out_slot, c, to, :] = product[half + first:half + first + plan.piece]
        for copy in leaving(i):
            copy.start()

    streamed(count, w_buf.shape[0], copies_of, step)
    for i in range(max(count - 2, 0), count):
        for copy in leaving(i):
            copy.wait()


def decode(plan, index, pieces, w_dec):
    tile = pick_tile(plan.model, 256)
    shape = (plan.depth * plan.piece, plan.model)
    near = (2, plan.chunks, plan.depth * plan.piece, tile)
    outs = call(
        partial(decode_kernel, plan),
        "decode",
        [SCALARS] + [ANYWHERE] * len(pieces) + [FAR],
        [jax.ShapeDtypeStruct(shape, BF16)] * plan.chunks
        + [jax.ShapeDtypeStruct(shape, F32)] * plan.chunks,
        [
            pltpu.VMEM((plan.tokens, plan.sources * plan.width), BF16),
            pltpu.VMEM((WEIGHT_SLOTS, plan.sources * plan.width, tile), BF16),
            pltpu.VMEM(near, BF16),
            pltpu.VMEM(near, F32),
            pltpu.SemaphoreType.DMA((len(pieces) * plan.per_group,)),
            pltpu.SemaphoreType.DMA((WEIGHT_SLOTS, plan.sources)),
            pltpu.SemaphoreType.DMA((2, 2 * plan.chunks)),
        ],
        (index, *pieces, w_dec),
        vmem=MOST_VMEM_BYTES,
        out_specs=[ANYWHERE] * (2 * plan.chunks),
    )
    return outs[:plan.chunks], outs[plan.chunks:]


def gradient_kernel(plan, index_ref, *refs):
    n_in = 2 * plan.depth
    errors, w_ref, outs = refs[:n_in], refs[n_in], refs[n_in + 1:-4]
    e_buf, w_buf, e_sem, w_sem = refs[-4:]
    depth = pick_tile(plan.width, 256)
    steps = plan.width // depth
    base = 1 + plan.sources + plan.groups * plan.pairs

    placing = [
        pltpu.make_async_copy(
            errors[i],
            e_buf.at[
                pl.ds(pl.multiple_of(index_ref[base + i] * plan.piece, ROW_TILE), plan.piece)
            ],
            e_sem.at[i],
        )
        for i in range(n_in)
    ]
    for copy in placing:
        copy.start()
    def copies_of(i, slot):
        rows = pl.ds(pl.multiple_of(lax.rem(i, steps) * depth, depth), depth)
        return [pltpu.make_async_copy(
            w_ref.at[lax.div(i, steps), 0, rows], w_buf.at[slot], w_sem.at[slot]
        )]

    half = plan.groups // 2

    def step(i, slot):
        @pl.when(i == 0)
        def _():
            for copy in placing:
                copy.wait()

        source = lax.div(i, steps)
        cols = pl.ds(pl.multiple_of(lax.rem(i, steps) * depth, depth), depth)
        product = lax.dot_general(
            e_buf[...], w_buf[slot], (((1,), (1,)), ((), ())), preferred_element_type=F32
        )
        product = jnp.where(index_ref[1 + source] > 0, product, 0.0)
        for lane, (lo, hi) in enumerate(plan.lane_sources):
            first, kept = plan.lanes[lane][0], plan.kept_order(lane)
            away, keep = outs[2 * lane * half:][:half], outs[(2 * lane + 1) * half:][:half]

            @pl.when((source >= lo) & (source < hi))
            def _():
                for p, j in enumerate(kept):
                    far = (j ^ first) * plan.block
                    away[p][source - lo, :, cols] = product[far:far + plan.block].astype(BF16)
                    keep[p][source - lo, :, cols] = product[j * plan.block:(j + 1) * plan.block]

    streamed(plan.sources * steps, w_buf.shape[0], copies_of, step)

    def add_squares(i, total):
        rows = pl.ds(pl.multiple_of(i * ROW_TILE, ROW_TILE), ROW_TILE)
        value = e_buf[rows, :].astype(F32)
        value = value * value
        value = value[:8] + value[8:]
        for col in range(0, plan.model, 128):
            total = total + value[:, col:col + 128]
        return total

    outs[-1][...] = lax.fori_loop(
        0, plan.chunk_rows // ROW_TILE, add_squares, jnp.zeros((8, 128), F32)
    )


def gradient(plan, index, errors, w_dec):
    depth = pick_tile(plan.width, 256)
    half = plan.groups // 2
    out_shape = []
    for lo, hi in plan.lane_sources:
        shape = (hi - lo, plan.block, plan.width)
        out_shape += [jax.ShapeDtypeStruct(shape, BF16)] * half
        out_shape += [jax.ShapeDtypeStruct(shape, F32)] * half
    outs = call(
        partial(gradient_kernel, plan),
        "gradient",
        [SCALARS] + [ANYWHERE] * len(errors) + [FAR],
        out_shape + [jax.ShapeDtypeStruct((8, 128), F32)],
        [
            pltpu.VMEM((plan.chunk_rows, plan.model), BF16),
            pltpu.VMEM((2 * WEIGHT_SLOTS, depth, plan.model), BF16),
            pltpu.SemaphoreType.DMA((len(errors),)),
            pltpu.SemaphoreType.DMA((2 * WEIGHT_SLOTS,)),
        ],
        (index, *errors, w_dec),
    )
    lanes = [outs[2 * i * half:2 * (i + 1) * half] for i in range(len(plan.lanes))]
    return [(lane[:half], lane[half:]) for lane in lanes], outs[-1]


def finish_kernel(plan, chunk, with_previous, *refs):
    lanes = len(plan.lanes)
    out_ref, stage, sem = refs[-3:]
    for lane, (lo, hi) in enumerate(plan.lane_sources):
        for s in range(lo, hi):
            total = refs[lane][s - lo]
            for got in refs[lanes + lane:lanes * (1 + lanes):lanes]:
                total = total + got[s - lo].astype(F32)
            stage[:, s, :] = total
    copies = [
        pltpu.make_async_copy(
            stage.at[pl.ds(b * plan.piece, plan.piece)],
            out_ref.at[pl.ds((b * plan.chunks + chunk) * plan.piece, plan.piece)],
            sem.at[b],
        )
        for b in range(plan.per_group)
    ]
    for copy in copies:
        copy.start()
    for copy in copies:
        copy.wait()


def finish(plan, chunk, kept, got, previous):
    options = {}
    if previous is not None:
        options["input_output_aliases"] = {len(kept) + len(got): 0}
    previous = [] if previous is None else [previous]
    return call(
        partial(finish_kernel, plan, chunk, bool(previous)),
        "finish",
        [NEAR] * (len(kept) + len(got)) + [FAR] * len(previous),
        jax.ShapeDtypeStruct((plan.rows, plan.sources, plan.width), F32),
        [
            pltpu.VMEM((plan.block, plan.sources, plan.width), F32),
            pltpu.SemaphoreType.DMA((plan.per_group,)),
        ],
        (*kept, *got, *previous),
        out_specs=FAR,
        **options,
    )


def per_device(resid, w_enc, b_enc, w_dec, targets, start_layer):
    plan = Plan(resid, w_dec)
    group = lax.axis_index("grp").astype(jnp.int32)
    feat = lax.axis_index("feat").astype(jnp.int32)
    core, level = feat % 2, feat // 2
    groups, feats, chunks = plan.groups, plan.feats, plan.chunks

    feeds = (group >= start_layer[:, 0]).astype(jnp.int32)
    offsets = [
        ((group ^ j) * plan.pairs + b) ^ level
        for j in range(groups)
        for b in range(plan.pairs)
    ]
    places = []
    for other in range(2):
        for d in range(plan.depth):
            owner = level ^ d
            place = ((owner // plan.pairs) ^ group) * plan.pairs + owner % plan.pairs
            places.append(place * 2 + (core ^ other))
    index = jnp.concatenate([core[None], feeds, jnp.stack(offsets), jnp.stack(places)])

    encoded, batches = [], []
    for lo, hi in plan.lane_sources:
        batches.append(range(lo, hi))
        encoded += encode(plan, lo, hi, resid, w_enc, b_enc)
    active = arrange(plan, encoded)

    pieces, arrived, forwarded = [], [], []
    for batch in batches:
        before, arrived, before_forward, forwarded = arrived, [], forwarded, []
        for s in batch:
            bits = plan.lanes[s % len(plan.lanes)]
            mine, = after([encoded[s]], before)
            held = {0: mine}
            for bit in bits:
                old = dict(held)
                for j, x in old.items():
                    if j:
                        x, = after([x], before_forward)
                    held[j | bit] = swap(x, "grp", groups, bit)
            pieces += [held[j] for j in range(groups)]
            arrived += [held[bit] for bit in bits]
            forwarded += [held[j] for j in range(groups) if j & (j - 1)]

    sends, keeps = decode(plan, index, after(pieces, [active]), w_dec)
    recon_parts, errors = [], []
    for c in range(chunks):
        other = swap(sends[c], "feat", feats, 1)
        held = {
            d: keeps[c][d * plan.piece:(d + 1) * plan.piece]
            + other[d * plan.piece:(d + 1) * plan.piece].astype(F32)
            for d in range(plan.depth)
        }
        for bit in plan.level_bits:
            away = {d: held.pop(d).astype(BF16) for d in sorted(held, reverse=True) if d & bit}
            for d, x in away.items():
                held[d ^ bit] = held[d ^ bit] + swap(x, "feat", feats, 2 * bit).astype(F32)
        recon_rows, = after([held[0]], [e[0] for e in errors])

        first = feat * plan.rows_feat + c * plan.piece
        own_targets = lax.dynamic_slice_in_dim(targets[0], first, plan.piece, 0)
        difference = recon_rows - own_targets.astype(F32)
        recon_parts.append(recon_rows.astype(BF16))
        error = difference.astype(BF16)
        held = {0: error}
        if c:
            for d in range(plan.depth - 1, 0, -1):
                held[d] = swap(error, "feat", feats, 2 * d)
        else:
            for bit in reversed(plan.level_bits):
                held.update(
                    {d | bit: swap(x, "feat", feats, 2 * bit) for d, x in list(held.items())}
                )
        every = [held[d] for d in range(plan.depth)]
        errors.append(every + [swap(e, "feat", feats, 1) for e in every])

    squares = jnp.zeros((8, 128), F32)
    feat_grad = None
    second, got_all = [], []
    for c in range(chunks):
        ready = after(errors[c], [e[0] for e in errors[c + 1:c + 2]] + second)
        lanes, total = gradient(plan, index, ready, w_dec)
        squares = squares + total
        second = []
        earlier = got_all + [x for every in errors[c + 1:c + 2] for x in every[1:plan.depth]]
        lanes = [(after(away, earlier), kept) for away, kept in lanes]
        kept_all = []
        for bits, (away, kept) in zip(plan.lanes, lanes):
            kept = [[x] for x in kept]
            for step, bit in enumerate(bits):
                cut = len(away) // 2
                got = [swap(x, "grp", groups, bit) for x in away[:cut]]
                rest = after(away[cut:], got[:1])
                got += [swap(x, "grp", groups, bit) for x in rest]
                for own, x in zip(kept, got):
                    own.append(x)
                if cut:
                    away = [sum(x.astype(F32) for x in own).astype(BF16) for own in kept[:cut]]
                    kept = kept[cut:]
                    second += away if not step else []
            kept_all.append(kept[0])
        got_all = [own[i] for i in range(1, len(kept_all[0])) for own in kept_all]
        previous = feat_grad
        feat_grad = finish(plan, c, [own[0] for own in kept_all], got_all, previous)

    loss = jnp.full((8, 128), jnp.sum(squares), F32)
    for i, bit in enumerate(1 << i for i in range(groups.bit_length() - 1)):
        loss = loss + swap(loss, "grp", groups, bit)
        if not i:
            loss, = after([loss], second + ([] if previous is None else [previous]))
    entries = targets.shape[0] * groups * plan.tokens * plan.model
    recon_loss = loss[0, 0] / entries
    recon = jnp.concatenate(recon_parts, axis=0)[None]
    return active, recon, recon_loss, feat_grad


def solution(mesh):
    in_specs = (
        P(None, "grp", None),
        P(None, None, "feat"),
        P(None, "feat"),
        P(None, "grp", "feat", None),
        P("grp", None, None),
        P(None, "feat"),
    )
    out_specs = (P("grp", None, "feat"), P("grp", "feat", None), P(), P("grp", None, "feat"))
    return jax.shard_map(
        per_device, mesh=mesh, in_specs=in_specs, out_specs=out_specs, check_vma=False
    )
```

```python
from functools import partial

import jax
import jax.numpy as jnp
from jax import lax
from jax.experimental import pallas as pl
from jax.experimental.pallas import tpu as pltpu
from jax.sharding import PartitionSpec as P

BF16 = jnp.bfloat16
F32 = jnp.float32
WANTED_CHUNKS = 2
ROW_TILE = 16
WEIGHT_SLOTS = 4
VMEM_BYTES = 44 << 20
MOST_VMEM_BYTES = 59 << 20
SMALL_COST = pl.CostEstimate(flops=1 << 20, bytes_accessed=1 << 10, transcendentals=0)
FAR = pl.BlockSpec(memory_space=pltpu.HBM)
ANYWHERE = pl.BlockSpec(memory_space=pl.ANY)
SCALARS = pl.BlockSpec(memory_space=pltpu.SMEM)
NEAR = pl.BlockSpec(memory_space=pltpu.VMEM)


def pick_tile(size, wanted):
    return wanted if size % wanted == 0 else size


def swap(x, axis, size, offset):
    return lax.ppermute(x, axis, [(i, i ^ offset) for i in range(size)])


def after(values, earlier):
    if not earlier:
        return list(values)
    return list(lax.optimization_barrier(list(values) + list(earlier)))[:len(values)]


class Plan:
    def __init__(self, resid, w_dec):
        self.sources, self.rows, self.model = resid.shape
        self.width = w_dec.shape[2]
        self.groups = lax.axis_size("grp")
        self.feats = lax.axis_size("feat")
        self.depth = self.feats // 2
        self.tokens = self.rows * self.groups
        self.rows_feat = self.tokens // self.feats
        self.per_group = self.rows // self.rows_feat
        self.pairs = self.per_group // 2
        self.chunks = WANTED_CHUNKS
        while self.rows_feat % (self.chunks * ROW_TILE):
            self.chunks -= 1
        self.piece = self.rows_feat // self.chunks
        self.block = self.per_group * self.piece
        self.chunk_rows = self.groups * self.block
        bits = [1 << i for i in range(self.groups.bit_length() - 1)]
        self.lanes = [bits[i:] + bits[:i] for i in range(len(bits))]
        starts = [i * self.sources // len(bits) for i in range(len(bits) + 1)]
        self.lane_sources = list(zip(starts[:-1], starts[1:]))
        self.level_bits = [1 << i for i in range(self.depth.bit_length() - 1)]

    def kept_order(self, lane):
        kept = [0]
        for bit in reversed(self.lanes[lane][1:]):
            kept = [j | bit for j in kept] + kept
        return kept


def streamed(count, slots, copies_of, body):
    early = min(slots - 1, count)
    for i in range(early):
        for copy in copies_of(i, i):
            copy.start()

    @pl.loop(0, count)
    def _(i):
        ahead = i + slots - 1

        @pl.when(i == 0)
        def _():
            for copy in copies_of(0, 0):
                copy.wait()
            for later in range(early, min(slots, count)):
                for copy in copies_of(later, later):
                    copy.start()

        @pl.when((i > 0) & (ahead < count))
        def _():
            for copy in copies_of(ahead, lax.rem(ahead, slots)):
                copy.start()

        slot = lax.rem(i, slots)

        @pl.when(i > 0)
        def _():
            for copy in copies_of(i, slot):
                copy.wait()

        body(i, slot)


def call(kernel, name, in_specs, out_shape, scratch, args, vmem=VMEM_BYTES, **options):
    return pl.pallas_call(
        kernel,
        in_specs=in_specs,
        out_shape=out_shape,
        scratch_shapes=scratch,
        cost_estimate=SMALL_COST,
        compiler_params=pltpu.CompilerParams(vmem_limit_bytes=vmem),
        name=name,
        **options,
    )(*args)


def encode_kernel(plan, lo, hi, resid_ref, w_ref, b_ref, *refs):
    outs, (x_buf, w_buf, b_buf, x_sem, w_sem) = refs[:hi - lo], refs[hi - lo:]
    tile = w_buf.shape[2]
    steps = plan.width // tile
    near = [
        pltpu.make_async_copy(resid_ref.at[pl.ds(lo, hi - lo)], x_buf, x_sem.at[0]),
        pltpu.make_async_copy(b_ref, b_buf, x_sem.at[1]),
    ]
    for copy in near:
        copy.start()

    def copies_of(i, slot):
        cols = pl.ds(pl.multiple_of(lax.rem(i, steps) * tile, tile), tile)
        return [pltpu.make_async_copy(
            w_ref.at[lo + lax.div(i, steps), :, cols], w_buf.at[slot], w_sem.at[slot]
        )]

    def step(i, slot):
        @pl.when(i == 0)
        def _():
            for copy in near:
                copy.wait()

        source = lax.div(i, steps)
        cols = pl.ds(pl.multiple_of(lax.rem(i, steps) * tile, tile), tile)
        product = jnp.dot(x_buf[source], w_buf[slot], preferred_element_type=F32)
        bias = b_buf[pl.ds(lo + source, 1), cols]
        value = jnp.maximum(product + bias, 0.0).astype(BF16)
        for s in range(hi - lo):
            @pl.when(source == s)
            def _():
                outs[s][:, cols] = value

    streamed((hi - lo) * steps, w_buf.shape[0], copies_of, step)


def encode(plan, lo, hi, resid, w_enc, b_enc):
    tile = pick_tile(plan.width, 256)
    return call(
        partial(encode_kernel, plan, lo, hi),
        "encode",
        [FAR, FAR, FAR],
        [jax.ShapeDtypeStruct((plan.rows, plan.width), BF16)] * (hi - lo),
        [
            pltpu.VMEM((hi - lo, plan.rows, plan.model), BF16),
            pltpu.VMEM((2 * WEIGHT_SLOTS, plan.model, tile), BF16),
            pltpu.VMEM((plan.sources, plan.width), F32),
            pltpu.SemaphoreType.DMA((2,)),
            pltpu.SemaphoreType.DMA((2 * WEIGHT_SLOTS,)),
        ],
        (resid, w_enc, b_enc),
        vmem=MOST_VMEM_BYTES,
    )


def arrange_kernel(plan, *refs):
    parts, out_ref, stage = refs[:plan.sources], refs[-2], refs[-1]
    count = stage.shape[0]

    @pl.loop(0, plan.rows // count)
    def _(i):
        rows = pl.ds(pl.multiple_of(i * count, count), count)
        for s in range(plan.sources):
            stage[:, s, :] = parts[s][rows, :].astype(F32)
        out_ref[rows] = stage[...].astype(BF16)


def arrange(plan, encoded):
    return call(
        partial(arrange_kernel, plan),
        "arrange",
        [NEAR] * plan.sources,
        jax.ShapeDtypeStruct((plan.rows, plan.sources, plan.width), BF16),
        [pltpu.VMEM((ROW_TILE, plan.sources, plan.width), F32)],
        encoded,
    )


def decode_kernel(plan, index_ref, *refs):
    n_in = plan.groups * plan.sources
    pieces, w_ref, outs = refs[:n_in], refs[n_in], refs[n_in + 1:-7]
    x_buf, w_buf, send_buf, keep_buf, x_sem, w_sem, out_sem = refs[-7:]
    half = plan.tokens // 2
    core = index_ref[0]
    tile = w_buf.shape[2]
    count = plan.model // tile

    placing = []
    for j in range(plan.groups):
        for b in range(plan.pairs):
            place = index_ref[1 + plan.sources + j * plan.pairs + b] * plan.rows_feat
            for owner in range(2):
                to = pl.multiple_of(place + jnp.where(core == owner, half, 0), ROW_TILE)
                for s in range(plan.sources):
                    placing.append(pltpu.make_async_copy(
                        pieces[s * plan.groups + j].at[
                            pl.ds((2 * b + owner) * plan.rows_feat, plan.rows_feat)
                        ],
                        x_buf.at[
                            pl.ds(to, plan.rows_feat), pl.ds(s * plan.width, plan.width)
                        ],
                        x_sem.at[len(placing)],
                    ))
    for copy in placing:
        copy.start()

    def columns(i):
        return pl.ds(pl.multiple_of(i * tile, tile), tile)

    def copies_of(i, slot):
        return [
            pltpu.make_async_copy(
                w_ref.at[s, 0, :, columns(i)],
                w_buf.at[slot, pl.ds(s * plan.width, plan.width)],
                w_sem.at[slot, s],
            )
            for s in range(plan.sources)
        ]

    def leaving(i):
        slot = lax.rem(i, 2)
        return [
            pltpu.make_async_copy(
                buf.at[slot, c],
                outs[n * plan.chunks + c].at[:, columns(i)],
                out_sem.at[slot, n * plan.chunks + c],
            )
            for n, buf in enumerate((send_buf, keep_buf))
            for c in range(plan.chunks)
        ]

    def step(i, slot):
        @pl.when(i == 0)
        def _():
            for copy in placing:
                copy.wait()
            for s in range(plan.sources):
                @pl.when(index_ref[1 + s] == 0)
                def _(s=s):
                    x_buf[:, s * plan.width:(s + 1) * plan.width] = jnp.zeros(
                        (plan.tokens, plan.width), BF16
                    )

        @pl.when(i >= 2)
        def _():
            for copy in leaving(i - 2):
                copy.wait()

        product = jnp.dot(x_buf[...], w_buf[slot], preferred_element_type=F32)
        out_slot = lax.rem(i, 2)
        for c in range(plan.chunks):
            for d in range(plan.depth):
                first = d * plan.rows_feat + c * plan.piece
                to = slice(d * plan.piece, (d + 1) * plan.piece)
                send_buf[out_slot, c, to, :] = product[first:first + plan.piece].astype(BF16)
                keep_buf[out_slot, c, to, :] = product[half + first:half + first + plan.piece]
        for copy in leaving(i):
            copy.start()

    streamed(count, w_buf.shape[0], copies_of, step)
    for i in range(max(count - 2, 0), count):
        for copy in leaving(i):
            copy.wait()


def decode(plan, index, pieces, w_dec):
    tile = pick_tile(plan.model, 256)
    shape = (plan.depth * plan.piece, plan.model)
    near = (2, plan.chunks, plan.depth * plan.piece, tile)
    outs = call(
        partial(decode_kernel, plan),
        "decode",
        [SCALARS] + [ANYWHERE] * len(pieces) + [FAR],
        [jax.ShapeDtypeStruct(shape, BF16)] * plan.chunks
        + [jax.ShapeDtypeStruct(shape, F32)] * plan.chunks,
        [
            pltpu.VMEM((plan.tokens, plan.sources * plan.width), BF16),
            pltpu.VMEM((WEIGHT_SLOTS, plan.sources * plan.width, tile), BF16),
            pltpu.VMEM(near, BF16),
            pltpu.VMEM(near, F32),
            pltpu.SemaphoreType.DMA((len(pieces) * plan.per_group,)),
            pltpu.SemaphoreType.DMA((WEIGHT_SLOTS, plan.sources)),
            pltpu.SemaphoreType.DMA((2, 2 * plan.chunks)),
        ],
        (index, *pieces, w_dec),
        vmem=MOST_VMEM_BYTES,
        out_specs=[ANYWHERE] * (2 * plan.chunks),
    )
    return outs[:plan.chunks], outs[plan.chunks:]


def gradient_kernel(plan, index_ref, *refs):
    n_in = 2 * plan.depth
    errors, w_ref, outs = refs[:n_in], refs[n_in], refs[n_in + 1:-4]
    e_buf, w_buf, e_sem, w_sem = refs[-4:]
    depth = pick_tile(plan.width, 512)
    steps = plan.width // depth
    base = 1 + plan.sources + plan.groups * plan.pairs

    placing = [
        pltpu.make_async_copy(
            errors[i],
            e_buf.at[
                pl.ds(pl.multiple_of(index_ref[base + i] * plan.piece, ROW_TILE), plan.piece)
            ],
            e_sem.at[i],
        )
        for i in range(n_in)
    ]
    for copy in placing:
        copy.start()
    def copies_of(i, slot):
        rows = pl.ds(pl.multiple_of(lax.rem(i, steps) * depth, depth), depth)
        return [pltpu.make_async_copy(
            w_ref.at[lax.div(i, steps), 0, rows], w_buf.at[slot], w_sem.at[slot]
        )]

    half = plan.groups // 2

    def step(i, slot):
        @pl.when(i == 0)
        def _():
            for copy in placing:
                copy.wait()

        source = lax.div(i, steps)
        cols = pl.ds(pl.multiple_of(lax.rem(i, steps) * depth, depth), depth)
        product = lax.dot_general(
            w_buf[slot], e_buf[...], (((1,), (1,)), ((), ())), preferred_element_type=F32
        ).T
        product = jnp.where(index_ref[1 + source] > 0, product, 0.0)
        for lane, (lo, hi) in enumerate(plan.lane_sources):
            first, kept = plan.lanes[lane][0], plan.kept_order(lane)
            away, keep = outs[2 * lane * half:][:half], outs[(2 * lane + 1) * half:][:half]

            @pl.when((source >= lo) & (source < hi))
            def _():
                for p, j in enumerate(kept):
                    far = (j ^ first) * plan.block
                    away[p][source - lo, :, cols] = product[far:far + plan.block].astype(BF16)
                    keep[p][source - lo, :, cols] = product[j * plan.block:(j + 1) * plan.block]

    streamed(plan.sources * steps, w_buf.shape[0], copies_of, step)

    def add_squares(i, total):
        rows = pl.ds(pl.multiple_of(i * ROW_TILE, ROW_TILE), ROW_TILE)
        value = e_buf[rows, :].astype(F32)
        value = value * value
        value = value[:8] + value[8:]
        for col in range(0, plan.model, 128):
            total = total + value[:, col:col + 128]
        return total

    outs[-1][...] = lax.fori_loop(
        0, plan.chunk_rows // ROW_TILE, add_squares, jnp.zeros((8, 128), F32)
    )


def gradient(plan, index, errors, w_dec):
    depth = pick_tile(plan.width, 512)
    half = plan.groups // 2
    out_shape = []
    for lo, hi in plan.lane_sources:
        shape = (hi - lo, plan.block, plan.width)
        out_shape += [jax.ShapeDtypeStruct(shape, BF16)] * half
        out_shape += [jax.ShapeDtypeStruct(shape, F32)] * half
    outs = call(
        partial(gradient_kernel, plan),
        "gradient",
        [SCALARS] + [ANYWHERE] * len(errors) + [FAR],
        out_shape + [jax.ShapeDtypeStruct((8, 128), F32)],
        [
            pltpu.VMEM((plan.chunk_rows, plan.model), BF16),
            pltpu.VMEM((WEIGHT_SLOTS, depth, plan.model), BF16),
            pltpu.SemaphoreType.DMA((len(errors),)),
            pltpu.SemaphoreType.DMA((WEIGHT_SLOTS,)),
        ],
        (index, *errors, w_dec),
    )
    lanes = [outs[2 * i * half:2 * (i + 1) * half] for i in range(len(plan.lanes))]
    return [(lane[:half], lane[half:]) for lane in lanes], outs[-1]


def finish_kernel(plan, chunk, with_previous, *refs):
    lanes = len(plan.lanes)
    out_ref, stage, sem = refs[-3:]
    for lane, (lo, hi) in enumerate(plan.lane_sources):
        for s in range(lo, hi):
            total = refs[lane][s - lo]
            for got in refs[lanes + lane:lanes * (1 + lanes):lanes]:
                total = total + got[s - lo].astype(F32)
            stage[:, s, :] = total
    copies = [
        pltpu.make_async_copy(
            stage.at[pl.ds(b * plan.piece, plan.piece)],
            out_ref.at[pl.ds((b * plan.chunks + chunk) * plan.piece, plan.piece)],
            sem.at[b],
        )
        for b in range(plan.per_group)
    ]
    for copy in copies:
        copy.start()
    for copy in copies:
        copy.wait()


def finish(plan, chunk, kept, got, previous):
    options = {}
    if previous is not None:
        options["input_output_aliases"] = {len(kept) + len(got): 0}
    previous = [] if previous is None else [previous]
    return call(
        partial(finish_kernel, plan, chunk, bool(previous)),
        "finish",
        [NEAR] * (len(kept) + len(got)) + [FAR] * len(previous),
        jax.ShapeDtypeStruct((plan.rows, plan.sources, plan.width), F32),
        [
            pltpu.VMEM((plan.block, plan.sources, plan.width), F32),
            pltpu.SemaphoreType.DMA((plan.per_group,)),
        ],
        (*kept, *got, *previous),
        out_specs=FAR,
        **options,
    )


def per_device(resid, w_enc, b_enc, w_dec, targets, start_layer):
    plan = Plan(resid, w_dec)
    group = lax.axis_index("grp").astype(jnp.int32)
    feat = lax.axis_index("feat").astype(jnp.int32)
    core, level = feat % 2, feat // 2
    groups, feats, chunks = plan.groups, plan.feats, plan.chunks

    feeds = (group >= start_layer[:, 0]).astype(jnp.int32)
    offsets = [
        ((group ^ j) * plan.pairs + b) ^ level
        for j in range(groups)
        for b in range(plan.pairs)
    ]
    places = []
    for other in range(2):
        for d in range(plan.depth):
            owner = level ^ d
            place = ((owner // plan.pairs) ^ group) * plan.pairs + owner % plan.pairs
            places.append(place * 2 + (core ^ other))
    index = jnp.concatenate([core[None], feeds, jnp.stack(offsets), jnp.stack(places)])

    encoded, batches = [], []
    for lo, hi in plan.lane_sources:
        batches.append(range(lo, hi))
        encoded += encode(plan, lo, hi, resid, w_enc, b_enc)
    active = arrange(plan, encoded)

    pieces, arrived, also, forwarded = [], [], [], []
    for batch in batches:
        before, arrived, before_forward, forwarded = arrived, [], also + forwarded, []
        for s in batch:
            bits = plan.lanes[s % len(plan.lanes)]
            mine, = after([encoded[s]], before)
            held = {0: mine}
            for bit in bits:
                old = dict(held)
                for j, x in old.items():
                    if j:
                        x, = after([x], before_forward)
                    held[j | bit] = swap(x, "grp", groups, bit)
            pieces += [held[j] for j in range(groups)]
            arrived.append(held[bits[0]])
            also += [held[bit] for bit in bits[1:]]
            forwarded += [held[j] for j in range(groups) if j & (j - 1)]

    sends, keeps = decode(plan, index, after(pieces, [active]), w_dec)
    held_all, others = [], []
    for c in range(chunks):
        send, = after([sends[c]], others[-1:])
        other = swap(send, "feat", feats, 1)
        others.append(other)
        held_all.append({
            d: keeps[c][d * plan.piece:(d + 1) * plan.piece]
            + other[d * plan.piece:(d + 1) * plan.piece].astype(F32)
            for d in range(plan.depth)
        })
    for bit in plan.level_bits:
        away_all = [
            {d: held.pop(d).astype(BF16) for d in sorted(held, reverse=True) if d & bit}
            for held in held_all
        ]
        for c in range(1, chunks):
            ready = after(away_all[c].values(), away_all[c - 1].values())
            away_all[c] = dict(zip(away_all[c], ready))
        for c, (held, away) in enumerate(zip(held_all, away_all)):
            got = [swap(x, "feat", feats, 2 * bit) for x in away.values()]
            later = [x for away_later in away_all[c + 1:c + 2] for x in away_later.values()]
            got = [after([x], later)[0] for x in got]
            for d, x in zip(away, got):
                held[d ^ bit] = held[d ^ bit] + x.astype(F32)

    recon_parts, errors = [], []
    for c, held in enumerate(held_all):
        recon_rows, = after([held[0]], [e[0] for e in errors])

        first = feat * plan.rows_feat + c * plan.piece
        own_targets = lax.dynamic_slice_in_dim(targets[0], first, plan.piece, 0)
        difference = recon_rows - own_targets.astype(F32)
        recon_parts.append(recon_rows.astype(BF16))
        error = difference.astype(BF16)
        held = {0: error}
        if c:
            for d in range(plan.depth - 1, 0, -1):
                held[d] = swap(error, "feat", feats, 2 * d)
        else:
            for bit in reversed(plan.level_bits):
                held.update(
                    {d | bit: swap(x, "feat", feats, 2 * bit) for d, x in list(held.items())}
                )
        every = [held[d] for d in range(plan.depth)]
        errors.append(every + [swap(e, "feat", feats, 1) for e in every])

    squares = jnp.zeros((8, 128), F32)
    unfinished = []
    second, got_all = [], []
    for c in range(chunks):
        ready = after(errors[c], [e[0] for e in errors[c + 1:c + 2]] + second)
        lanes, total = gradient(plan, index, ready, w_dec)
        squares = squares + total
        second, near = [], []
        earlier = got_all + [x for every in errors[c + 1:c + 2] for x in every[1:plan.depth]]
        lanes = [(after(away, earlier), kept) for away, kept in lanes]
        kept_all = []
        for bits, (away, kept) in zip(plan.lanes, lanes):
            kept = [[x] for x in kept]
            for step, bit in enumerate(bits):
                cut = len(away) // 2
                got = [swap(x, "grp", groups, bit) for x in away[:cut]]
                rest = after(away[cut:], got[:1])
                got += [swap(x, "grp", groups, bit) for x in rest]
                if not step:
                    near += got[-1:]
                for own, x in zip(kept, got):
                    own.append(x)
                if cut:
                    away = [sum(x.astype(F32) for x in own).astype(BF16) for own in kept[:cut]]
                    kept = kept[cut:]
                    second += away if not step else []
            kept_all.append(kept[0])
        got_all = [own[i] for i in range(1, len(kept_all[0])) for own in kept_all]
        unfinished.append(([own[0] for own in kept_all], got_all))

    feat_grad = None
    for c, (kept, got) in enumerate(unfinished):
        if c + 1 < chunks:
            kept = after(kept, near)
        feat_grad = finish(plan, c, kept, got, feat_grad)

    loss = jnp.full((8, 128), jnp.sum(squares), F32)
    for i, bit in enumerate(1 << i for i in range(groups.bit_length() - 1)):
        loss = loss + swap(loss, "grp", groups, bit)
        if not i:
            loss, = after([loss], second)
    entries = targets.shape[0] * groups * plan.tokens * plan.model
    recon_loss = loss[0, 0] / entries
    recon = jnp.concatenate(recon_parts, axis=0)[None]
    return active, recon, recon_loss, feat_grad


def solution(mesh):
    in_specs = (
        P(None, "grp", None),
        P(None, None, "feat"),
        P(None, "feat"),
        P(None, "grp", "feat", None),
        P("grp", None, None),
        P(None, "feat"),
    )
    out_specs = (P("grp", None, "feat"), P("grp", "feat", None), P(), P("grp", None, "feat"))
    return jax.shard_map(
        per_device, mesh=mesh, in_specs=in_specs, out_specs=out_specs, check_vma=False
    )
```

```python
from functools import partial

import jax
import jax.numpy as jnp
from jax import lax
from jax.experimental import pallas as pl
from jax.experimental.pallas import tpu as pltpu
from jax.sharding import PartitionSpec as P

BF16 = jnp.bfloat16
F32 = jnp.float32
WANTED_CHUNKS = 2
ROW_TILE = 16
WEIGHT_SLOTS = 4
IN_FLIGHT = 3
VMEM_BYTES = 44 << 20
MOST_VMEM_BYTES = 59 << 20
SMALL_COST = pl.CostEstimate(flops=1 << 20, bytes_accessed=1 << 10, transcendentals=0)
FAR = pl.BlockSpec(memory_space=pltpu.HBM)
ANYWHERE = pl.BlockSpec(memory_space=pl.ANY)
SCALARS = pl.BlockSpec(memory_space=pltpu.SMEM)
NEAR = pl.BlockSpec(memory_space=pltpu.VMEM)


def pick_tile(size, wanted):
    return wanted if size % wanted == 0 else size


def swap(x, axis, size, offset):
    return lax.ppermute(x, axis, [(i, i ^ offset) for i in range(size)])


def after(values, earlier):
    if not earlier:
        return list(values)
    return list(lax.optimization_barrier(list(values) + list(earlier)))[:len(values)]


class Plan:
    def __init__(self, resid, w_dec):
        self.sources, self.rows, self.model = resid.shape
        self.width = w_dec.shape[2]
        self.groups = lax.axis_size("grp")
        self.feats = lax.axis_size("feat")
        self.depth = self.feats // 2
        self.tokens = self.rows * self.groups
        self.rows_feat = self.tokens // self.feats
        self.per_group = self.rows // self.rows_feat
        self.pairs = self.per_group // 2
        self.chunks = WANTED_CHUNKS
        while self.rows_feat % (self.chunks * ROW_TILE):
            self.chunks -= 1
        self.piece = self.rows_feat // self.chunks
        self.block = self.per_group * self.piece
        self.chunk_rows = self.groups * self.block
        bits = [1 << i for i in range(self.groups.bit_length() - 1)]
        self.lanes = [bits[i:] + bits[:i] for i in range(len(bits))]
        starts = [i * self.sources // len(bits) for i in range(len(bits) + 1)]
        self.lane_sources = list(zip(starts[:-1], starts[1:]))
        self.level_bits = [1 << i for i in range(self.depth.bit_length() - 1)]

    def kept_order(self, lane):
        kept = [0]
        for bit in reversed(self.lanes[lane][1:]):
            kept = [j | bit for j in kept] + kept
        return kept


def streamed(count, slots, copies_of, body):
    early = min(2, slots - 1, count)
    for i in range(early):
        for copy in copies_of(i, i):
            copy.start()

    @pl.loop(0, count)
    def _(i):
        ahead = i + slots - 1

        @pl.when(i == 0)
        def _():
            for copy in copies_of(0, 0):
                copy.wait()
            for later in range(early, min(slots, count)):
                for copy in copies_of(later, later):
                    copy.start()

        @pl.when((i > 0) & (ahead < count))
        def _():
            for copy in copies_of(ahead, lax.rem(ahead, slots)):
                copy.start()

        slot = lax.rem(i, slots)

        @pl.when(i > 0)
        def _():
            for copy in copies_of(i, slot):
                copy.wait()

        body(i, slot)


def call(kernel, name, in_specs, out_shape, scratch, args, vmem=VMEM_BYTES, **options):
    return pl.pallas_call(
        kernel,
        in_specs=in_specs,
        out_shape=out_shape,
        scratch_shapes=scratch,
        cost_estimate=SMALL_COST,
        compiler_params=pltpu.CompilerParams(vmem_limit_bytes=vmem),
        name=name,
        **options,
    )(*args)


def encode_kernel(plan, lo, hi, resid_ref, w_ref, b_ref, *refs):
    outs, (x_buf, w_buf, b_buf, total, x_sem, w_sem) = refs[:hi - lo], refs[hi - lo:]
    steps = w_sem.shape[0] // (hi - lo)
    depth = plan.model // steps
    near = [
        pltpu.make_async_copy(resid_ref.at[pl.ds(lo, hi - lo)], x_buf, x_sem.at[0]),
        pltpu.make_async_copy(b_ref, b_buf, x_sem.at[1]),
    ]
    copies = [
        pltpu.make_async_copy(
            w_ref.at[lo + s, pl.ds(i * depth, depth)],
            w_buf.at[s, pl.ds(i * depth, depth)],
            w_sem.at[s * steps + i],
        )
        for s in range(hi - lo)
        for i in range(steps)
    ]
    near[0].start()
    for copy in copies[:IN_FLIGHT]:
        copy.start()
    near[1].start()
    near[0].wait()
    for s in range(hi - lo):
        for i in range(steps):
            step = s * steps + i
            copies[step].wait()
            for copy in copies[step + IN_FLIGHT:step + IN_FLIGHT + 1]:
                copy.start()
            part = slice(i * depth, (i + 1) * depth)
            product = jnp.dot(x_buf[s, :, part], w_buf[s, part, :], preferred_element_type=F32)
            if i:
                product = total[...] + product
            if i < steps - 1:
                total[...] = product
        if not s:
            near[1].wait()
        value = jnp.maximum(product + b_buf[lo + s:lo + s + 1, :], 0.0)
        outs[s][...] = value.astype(BF16)


def encode(plan, lo, hi, resid, w_enc, b_enc):
    n = hi - lo
    steps = plan.model // pick_tile(plan.model, 768)
    return call(
        partial(encode_kernel, plan, lo, hi),
        "encode",
        [FAR, FAR, FAR],
        [jax.ShapeDtypeStruct((plan.rows, plan.width), BF16)] * n,
        [
            pltpu.VMEM((n, plan.rows, plan.model), BF16),
            pltpu.VMEM((n, plan.model, plan.width), BF16),
            pltpu.VMEM((plan.sources, plan.width), F32),
            pltpu.VMEM((plan.rows, plan.width), F32),
            pltpu.SemaphoreType.DMA((2,)),
            pltpu.SemaphoreType.DMA((n * steps,)),
        ],
        (resid, w_enc, b_enc),
        vmem=MOST_VMEM_BYTES,
    )


def arrange_kernel(plan, *refs):
    parts, out_ref, stage = refs[:plan.sources], refs[-2], refs[-1]
    count = stage.shape[0]

    @pl.loop(0, plan.rows // count)
    def _(i):
        rows = pl.ds(pl.multiple_of(i * count, count), count)
        for s in range(plan.sources):
            stage[:, s, :] = parts[s][rows, :].astype(F32)
        out_ref[rows] = stage[...].astype(BF16)


def arrange(plan, encoded):
    return call(
        partial(arrange_kernel, plan),
        "arrange",
        [NEAR] * plan.sources,
        jax.ShapeDtypeStruct((plan.rows, plan.sources, plan.width), BF16),
        [pltpu.VMEM((ROW_TILE, plan.sources, plan.width), F32)],
        encoded,
    )


def decode_kernel(plan, index_ref, *refs):
    n_in = plan.groups * plan.sources
    pieces, w_ref, outs = refs[:n_in], refs[n_in], refs[n_in + 1:-5]
    x_buf, w_buf, total, x_sem, w_sem = refs[-5:]
    half = plan.tokens // 2
    core = index_ref[0]
    tile = w_buf.shape[2]

    placing = [[] for _ in range(plan.sources)]
    for s in range(plan.sources):
        for j in range(plan.groups):
            for b in range(plan.pairs):
                place = index_ref[1 + plan.sources + j * plan.pairs + b] * plan.rows_feat
                for owner in range(2):
                    to = pl.multiple_of(place + jnp.where(core == owner, half, 0), ROW_TILE)
                    placing[s].append(pltpu.make_async_copy(
                        pieces[s * plan.groups + j].at[
                            pl.ds((2 * b + owner) * plan.rows_feat, plan.rows_feat)
                        ],
                        x_buf.at[s, pl.ds(to, plan.rows_feat)],
                        x_sem.at[s, len(placing[s])],
                    ))
    for copies in placing:
        for copy in copies:
            copy.start()

    def columns(i):
        return pl.ds(pl.multiple_of(lax.div(i, plan.sources) * tile, tile), tile)

    def copies_of(i, slot):
        return [pltpu.make_async_copy(
            w_ref.at[lax.rem(i, plan.sources), 0, :, columns(i)], w_buf.at[slot], w_sem.at[slot]
        )]

    def step(i, slot):
        source = lax.rem(i, plan.sources)
        for s in range(plan.sources):
            @pl.when(i == s)
            def _(s=s):
                for copy in placing[s]:
                    copy.wait()

                @pl.when(index_ref[1 + s] == 0)
                def _():
                    x_buf[s] = jnp.zeros(x_buf.shape[1:], BF16)

        product = jnp.dot(x_buf[source], w_buf[slot], preferred_element_type=F32)

        @pl.when(source == 0)
        def _():
            total[...] = product

        @pl.when((source > 0) & (source < plan.sources - 1))
        def _():
            total[...] = total[...] + product

        @pl.when(source == plan.sources - 1)
        def _():
            cols = columns(i)
            for c in range(plan.chunks):
                for d in range(plan.depth):
                    first = d * plan.rows_feat + c * plan.piece
                    last = half + first
                    to = slice(d * plan.piece, (d + 1) * plan.piece)
                    outs[c][to, cols] = (
                        total[first:first + plan.piece] + product[first:first + plan.piece]
                    ).astype(BF16)
                    outs[plan.chunks + c][to, cols] = (
                        total[last:last + plan.piece] + product[last:last + plan.piece]
                    )

    count = plan.model // tile * plan.sources
    streamed(count, w_buf.shape[0], copies_of, step)


def decode(plan, index, pieces, w_dec):
    tile = pick_tile(plan.model, 768)
    shape = (plan.depth * plan.piece, plan.model)
    outs = call(
        partial(decode_kernel, plan),
        "decode",
        [SCALARS] + [ANYWHERE] * len(pieces) + [FAR],
        [jax.ShapeDtypeStruct(shape, BF16)] * plan.chunks
        + [jax.ShapeDtypeStruct(shape, F32)] * plan.chunks,
        [
            pltpu.VMEM((plan.sources, plan.tokens, plan.width), BF16),
            pltpu.VMEM((WEIGHT_SLOTS, plan.width, tile), BF16),
            pltpu.VMEM((plan.tokens, tile), F32),
            pltpu.SemaphoreType.DMA((plan.sources, plan.groups * plan.per_group)),
            pltpu.SemaphoreType.DMA((WEIGHT_SLOTS,)),
        ],
        (index, *pieces, w_dec),
        vmem=MOST_VMEM_BYTES,
    )
    return outs[:plan.chunks], outs[plan.chunks:]


def gradient_kernel(plan, index_ref, *refs):
    n_in = 2 * plan.depth
    errors, w_ref, outs = refs[:n_in], refs[n_in], refs[n_in + 1:-4]
    e_buf, w_buf, e_sem, w_sem = refs[-4:]
    depth = pick_tile(plan.width, 512)
    steps = plan.width // depth
    base = 1 + plan.sources + plan.groups * plan.pairs

    placing = [
        pltpu.make_async_copy(
            errors[i],
            e_buf.at[
                pl.ds(pl.multiple_of(index_ref[base + i] * plan.piece, ROW_TILE), plan.piece)
            ],
            e_sem.at[i],
        )
        for i in range(n_in)
    ]
    for copy in placing:
        copy.start()
    def copies_of(i, slot):
        part = depth // 4
        return [
            pltpu.make_async_copy(
                w_ref.at[
                    lax.div(i, steps),
                    0,
                    pl.ds(pl.multiple_of(lax.rem(i, steps) * depth + p * part, part), part),
                ],
                w_buf.at[slot, pl.ds(p * part, part)],
                w_sem.at[slot, p],
            )
            for p in range(4)
        ]

    half = plan.groups // 2

    def step(i, slot):
        @pl.when(i == 0)
        def _():
            for copy in placing:
                copy.wait()

        source = lax.div(i, steps)
        cols = pl.ds(pl.multiple_of(lax.rem(i, steps) * depth, depth), depth)
        product = lax.dot_general(
            w_buf[slot], e_buf[...], (((1,), (1,)), ((), ())), preferred_element_type=F32
        ).T
        product = jnp.where(index_ref[1 + source] > 0, product, 0.0)
        for lane, (lo, hi) in enumerate(plan.lane_sources):
            first, kept = plan.lanes[lane][0], plan.kept_order(lane)
            away, keep = outs[2 * lane * half:][:half], outs[(2 * lane + 1) * half:][:half]

            @pl.when((source >= lo) & (source < hi))
            def _():
                for p, j in enumerate(kept):
                    far = (j ^ first) * plan.block
                    away[p][source - lo, :, cols] = product[far:far + plan.block].astype(BF16)
                    keep[p][source - lo, :, cols] = product[j * plan.block:(j + 1) * plan.block]

    streamed(plan.sources * steps, w_buf.shape[0], copies_of, step)

    def add_squares(i, total):
        rows = pl.ds(pl.multiple_of(i * ROW_TILE, ROW_TILE), ROW_TILE)
        value = e_buf[rows, :].astype(F32)
        value = value * value
        value = value[:8] + value[8:]
        for col in range(0, plan.model, 128):
            total = total + value[:, col:col + 128]
        return total

    outs[-1][...] = lax.fori_loop(
        0, plan.chunk_rows // ROW_TILE, add_squares, jnp.zeros((8, 128), F32)
    )


def gradient(plan, index, errors, w_dec):
    depth = pick_tile(plan.width, 512)
    half = plan.groups // 2
    out_shape = []
    for lo, hi in plan.lane_sources:
        shape = (hi - lo, plan.block, plan.width)
        out_shape += [jax.ShapeDtypeStruct(shape, BF16)] * half
        out_shape += [jax.ShapeDtypeStruct(shape, F32)] * half
    outs = call(
        partial(gradient_kernel, plan),
        "gradient",
        [SCALARS] + [ANYWHERE] * len(errors) + [FAR],
        out_shape + [jax.ShapeDtypeStruct((8, 128), F32)],
        [
            pltpu.VMEM((plan.chunk_rows, plan.model), BF16),
            pltpu.VMEM((WEIGHT_SLOTS, depth, plan.model), BF16),
            pltpu.SemaphoreType.DMA((len(errors),)),
            pltpu.SemaphoreType.DMA((WEIGHT_SLOTS, 4)),
        ],
        (index, *errors, w_dec),
    )
    lanes = [outs[2 * i * half:2 * (i + 1) * half] for i in range(len(plan.lanes))]
    return [(lane[:half], lane[half:]) for lane in lanes], outs[-1]


def finish_kernel(plan, chunk, with_previous, *refs):
    lanes = len(plan.lanes)
    out_ref, stage, sem = refs[-3:]
    for lane, (lo, hi) in enumerate(plan.lane_sources):
        for s in range(lo, hi):
            total = refs[lane][s - lo]
            for got in refs[lanes + lane:lanes * (1 + lanes):lanes]:
                total = total + got[s - lo].astype(F32)
            stage[:, s, :] = total
    copies = [
        pltpu.make_async_copy(
            stage.at[pl.ds(b * plan.piece, plan.piece)],
            out_ref.at[pl.ds((b * plan.chunks + chunk) * plan.piece, plan.piece)],
            sem.at[b],
        )
        for b in range(plan.per_group)
    ]
    for copy in copies:
        copy.start()
    for copy in copies:
        copy.wait()


def finish(plan, chunk, kept, got, previous):
    options = {}
    if previous is not None:
        options["input_output_aliases"] = {len(kept) + len(got): 0}
    previous = [] if previous is None else [previous]
    return call(
        partial(finish_kernel, plan, chunk, bool(previous)),
        "finish",
        [NEAR] * (len(kept) + len(got)) + [FAR] * len(previous),
        jax.ShapeDtypeStruct((plan.rows, plan.sources, plan.width), F32),
        [
            pltpu.VMEM((plan.block, plan.sources, plan.width), F32),
            pltpu.SemaphoreType.DMA((plan.per_group,)),
        ],
        (*kept, *got, *previous),
        out_specs=FAR,
        **options,
    )


def per_device(resid, w_enc, b_enc, w_dec, targets, start_layer):
    plan = Plan(resid, w_dec)
    group = lax.axis_index("grp").astype(jnp.int32)
    feat = lax.axis_index("feat").astype(jnp.int32)
    core, level = feat % 2, feat // 2
    groups, feats, chunks = plan.groups, plan.feats, plan.chunks

    feeds = (group >= start_layer[:, 0]).astype(jnp.int32)
    offsets = [
        ((group ^ j) * plan.pairs + b) ^ level
        for j in range(groups)
        for b in range(plan.pairs)
    ]
    places = []
    for other in range(2):
        for d in range(plan.depth):
            owner = level ^ d
            place = ((owner // plan.pairs) ^ group) * plan.pairs + owner % plan.pairs
            places.append(place * 2 + (core ^ other))
    index = jnp.concatenate([core[None], feeds, jnp.stack(offsets), jnp.stack(places)])

    encoded, batches = [], []
    for lo, hi in plan.lane_sources:
        batches.append(range(lo, hi))
        encoded += encode(plan, lo, hi, resid, w_enc, b_enc)
    active = arrange(plan, encoded)

    pieces, arrived, also, forwarded = [], [], [], []
    for batch in batches:
        before, arrived, before_forward, forwarded = arrived, [], also + forwarded, []
        for s in batch:
            bits = plan.lanes[s % len(plan.lanes)]
            mine, = after([encoded[s]], before)
            held = {0: mine}
            for bit in bits:
                old = dict(held)
                for j, x in old.items():
                    if j:
                        x, = after([x], before_forward)
                    held[j | bit] = swap(x, "grp", groups, bit)
            pieces += [held[j] for j in range(groups)]
            arrived.append(held[bits[0]])
            also += [held[bit] for bit in bits[1:]]
            forwarded += [held[j] for j in range(groups) if j & (j - 1)]

    sends, keeps = decode(plan, index, after(pieces, [active]), w_dec)
    recon_parts, errors, first_errors = [], [], []
    for c in range(chunks):
        other = swap(sends[c], "feat", feats, 1)
        held = {
            d: keeps[c][d * plan.piece:(d + 1) * plan.piece]
            + other[d * plan.piece:(d + 1) * plan.piece].astype(F32)
            for d in range(plan.depth)
        }
        for bit in plan.level_bits:
            away = {d: held.pop(d).astype(BF16) for d in sorted(held, reverse=True) if d & bit}
            for d, x in away.items():
                held[d ^ bit] = held[d ^ bit] + swap(x, "feat", feats, 2 * bit).astype(F32)
        recon_rows, = after([held[0]], [e[0] for e in errors])

        first = feat * plan.rows_feat + c * plan.piece
        own_targets = lax.dynamic_slice_in_dim(targets[0], first, plan.piece, 0)
        difference = recon_rows - own_targets.astype(F32)
        recon_parts.append(recon_rows.astype(BF16))
        error = difference.astype(BF16)
        held = {0: error}
        if c:
            for d in range(plan.depth - 1, 0, -1):
                held[d] = swap(error, "feat", feats, 2 * d)
        else:
            for bit in reversed(plan.level_bits):
                held.update(
                    {d | bit: swap(x, "feat", feats, 2 * bit) for d, x in list(held.items())}
                )
        first_errors.append([held[d] for d in range(1, plan.depth)])
        every = [held[d] for d in range(plan.depth)]
        errors.append(every + [swap(e, "feat", feats, 1) for e in every])

    squares = jnp.zeros((8, 128), F32)
    totals, results = [], []
    for c in range(chunks):
        ready = after(errors[c], [e[0] for e in errors[c + 1:c + 2]] + totals[-1:])
        lanes, total = gradient(plan, index, ready, w_dec)
        totals.append(total)
        squares = squares + total
        results.append(lanes)

    unfinished = []
    for c, lanes in enumerate(results):
        earlier = [x for each in first_errors[c + 1:c + 2] for x in each]
        first_step = []
        for bits, (away, kept) in zip(plan.lanes, lanes):
            away = after(away, earlier)
            cut = len(away) // 2
            got = [swap(x, "grp", groups, bits[0]) for x in away[:cut]]
            rest = away[cut:] if c + 1 < chunks else after(away[cut:], got[:1])
            got += [swap(x, "grp", groups, bits[0]) for x in rest]
            first_step.append(got)
        wait = totals[c + 1:c + 2]
        if wait:
            wait = wait + [got[-1] for got in first_step]
        second, kept_all = [], []
        for bits, (away, kept), got in zip(plan.lanes, lanes, first_step):
            kept = [[x, after([y], wait)[0]] for x, y in zip(kept, got)]
            for bit in bits[1:]:
                cut = len(kept) // 2
                away = [sum(x.astype(F32) for x in own).astype(BF16) for own in kept[:cut]]
                second += away
                kept = kept[cut:]
                for own, x in zip(kept, away):
                    own.append(swap(x, "grp", groups, bit))
            kept_all.append(kept[0])
        got_all = [own[i] for i in range(1, len(kept_all[0])) for own in kept_all]
        unfinished.append(([own[0] for own in kept_all], got_all))

    feat_grad = None
    for c, (kept, got) in enumerate(unfinished):
        before_last = feat_grad
        feat_grad = finish(plan, c, kept, got, feat_grad)

    loss = jnp.full((8, 128), jnp.sum(squares), F32)
    parts = [loss] + [swap(loss, "grp", groups, j) for j in range(1, groups)]
    parts = after(parts, second + ([] if before_last is None else [before_last]))
    while len(parts) > 1:
        parts = [x + y for x, y in zip(parts[::2], parts[1::2])]
    loss = parts[0]
    entries = targets.shape[0] * groups * plan.tokens * plan.model
    recon_loss = loss[0, 0] / entries
    recon = jnp.concatenate(recon_parts, axis=0)[None]
    return active, recon, recon_loss, feat_grad


def solution(mesh):
    in_specs = (
        P(None, "grp", None),
        P(None, None, "feat"),
        P(None, "feat"),
        P(None, "grp", "feat", None),
        P("grp", None, None),
        P(None, "feat"),
    )
    out_specs = (P("grp", None, "feat"), P("grp", "feat", None), P(), P("grp", None, "feat"))
    return jax.shard_map(
        per_device, mesh=mesh, in_specs=in_specs, out_specs=out_specs, check_vma=False
    )
```

```python
from functools import partial

import jax
import jax.numpy as jnp
from jax import lax
from jax.experimental import pallas as pl
from jax.experimental.pallas import tpu as pltpu
from jax.sharding import PartitionSpec as P

BF16 = jnp.bfloat16
F32 = jnp.float32
WANTED_CHUNKS = 2
ROW_TILE = 16
WEIGHT_SLOTS = 4
IN_FLIGHT = 3
VMEM_BYTES = 44 << 20
MOST_VMEM_BYTES = 59 << 20
SMALL_COST = pl.CostEstimate(flops=1 << 20, bytes_accessed=1 << 10, transcendentals=0)
FAR = pl.BlockSpec(memory_space=pltpu.HBM)
ANYWHERE = pl.BlockSpec(memory_space=pl.ANY)
SCALARS = pl.BlockSpec(memory_space=pltpu.SMEM)
NEAR = pl.BlockSpec(memory_space=pltpu.VMEM)


def pick_tile(size, wanted):
    return wanted if size % wanted == 0 else size


def swap(x, axis, size, offset):
    return lax.ppermute(x, axis, [(i, i ^ offset) for i in range(size)])


def after(values, earlier):
    if not earlier:
        return list(values)
    return list(lax.optimization_barrier(list(values) + list(earlier)))[:len(values)]


class Plan:
    def __init__(self, resid, w_dec):
        self.sources, self.rows, self.model = resid.shape
        self.width = w_dec.shape[2]
        self.groups = lax.axis_size("grp")
        self.feats = lax.axis_size("feat")
        self.depth = self.feats // 2
        self.tokens = self.rows * self.groups
        self.rows_feat = self.tokens // self.feats
        self.per_group = self.rows // self.rows_feat
        self.pairs = self.per_group // 2
        self.chunks = WANTED_CHUNKS
        while self.rows_feat % (self.chunks * ROW_TILE):
            self.chunks -= 1
        self.piece = self.rows_feat // self.chunks
        self.block = self.per_group * self.piece
        self.chunk_rows = self.groups * self.block
        bits = [1 << i for i in range(self.groups.bit_length() - 1)]
        self.lanes = [bits[i:] + bits[:i] for i in range(len(bits))]
        starts = [i * self.sources // len(bits) for i in range(len(bits) + 1)]
        self.lane_sources = list(zip(starts[:-1], starts[1:]))
        self.level_bits = [1 << i for i in range(self.depth.bit_length() - 1)]

    def kept_order(self, lane):
        kept = [0]
        for bit in reversed(self.lanes[lane][1:]):
            kept = [j | bit for j in kept] + kept
        return kept


def streamed(count, slots, copies_of, body, first):
    early = min(first, slots - 1, count)
    for i in range(early):
        for copy in copies_of(i, i):
            copy.start()

    @pl.loop(0, count)
    def _(i):
        ahead = i + slots - 1

        @pl.when(i == 0)
        def _():
            for copy in copies_of(0, 0):
                copy.wait()
            for later in range(early, min(slots, count)):
                for copy in copies_of(later, later):
                    copy.start()

        @pl.when((i > 0) & (ahead < count))
        def _():
            for copy in copies_of(ahead, lax.rem(ahead, slots)):
                copy.start()

        slot = lax.rem(i, slots)

        @pl.when(i > 0)
        def _():
            for copy in copies_of(i, slot):
                copy.wait()

        body(i, slot)


def call(kernel, name, in_specs, out_shape, scratch, args, vmem=VMEM_BYTES, **options):
    return pl.pallas_call(
        kernel,
        in_specs=in_specs,
        out_shape=out_shape,
        scratch_shapes=scratch,
        cost_estimate=SMALL_COST,
        compiler_params=pltpu.CompilerParams(vmem_limit_bytes=vmem),
        name=name,
        **options,
    )(*args)


def encode_kernel(plan, lo, hi, resid_ref, w_ref, b_ref, *refs):
    outs, (x_buf, w_buf, b_buf, total, x_sem, w_sem) = refs[:hi - lo], refs[hi - lo:]
    steps = w_sem.shape[0] // (hi - lo)
    depth = plan.model // steps
    near = [
        pltpu.make_async_copy(resid_ref.at[pl.ds(lo, hi - lo)], x_buf, x_sem.at[0]),
        pltpu.make_async_copy(b_ref, b_buf, x_sem.at[1]),
    ]
    copies = [
        pltpu.make_async_copy(
            w_ref.at[lo + s, pl.ds(i * depth, depth)],
            w_buf.at[s, pl.ds(i * depth, depth)],
            w_sem.at[s * steps + i],
        )
        for s in range(hi - lo)
        for i in range(steps)
    ]
    near[0].start()
    for copy in copies[:IN_FLIGHT]:
        copy.start()
    near[1].start()
    near[0].wait()
    for s in range(hi - lo):
        for i in range(steps):
            step = s * steps + i
            copies[step].wait()
            for copy in copies[step + IN_FLIGHT:step + IN_FLIGHT + 1]:
                copy.start()
            part = slice(i * depth, (i + 1) * depth)
            product = jnp.dot(x_buf[s, :, part], w_buf[s, part, :], preferred_element_type=F32)
            if i:
                product = total[...] + product
            if i < steps - 1:
                total[...] = product
        if not s:
            near[1].wait()
        value = jnp.maximum(product + b_buf[lo + s:lo + s + 1, :], 0.0)
        outs[s][...] = value.astype(BF16)


def encode(plan, lo, hi, resid, w_enc, b_enc):
    n = hi - lo
    steps = plan.model // pick_tile(plan.model, 768)
    return call(
        partial(encode_kernel, plan, lo, hi),
        "encode",
        [FAR, FAR, FAR],
        [jax.ShapeDtypeStruct((plan.rows, plan.width), BF16)] * n,
        [
            pltpu.VMEM((n, plan.rows, plan.model), BF16),
            pltpu.VMEM((n, plan.model, plan.width), BF16),
            pltpu.VMEM((plan.sources, plan.width), F32),
            pltpu.VMEM((plan.rows, plan.width), F32),
            pltpu.SemaphoreType.DMA((2,)),
            pltpu.SemaphoreType.DMA((n * steps,)),
        ],
        (resid, w_enc, b_enc),
        vmem=MOST_VMEM_BYTES,
    )


def arrange_kernel(plan, *refs):
    parts, out_ref, stage = refs[:plan.sources], refs[-2], refs[-1]
    count = stage.shape[0]

    @pl.loop(0, plan.rows // count)
    def _(i):
        rows = pl.ds(pl.multiple_of(i * count, count), count)
        for s in range(plan.sources):
            stage[:, s, :] = parts[s][rows, :].astype(F32)
        out_ref[rows] = stage[...].astype(BF16)


def arrange(plan, encoded):
    return call(
        partial(arrange_kernel, plan),
        "arrange",
        [NEAR] * plan.sources,
        jax.ShapeDtypeStruct((plan.rows, plan.sources, plan.width), BF16),
        [pltpu.VMEM((ROW_TILE, plan.sources, plan.width), F32)],
        encoded,
    )


def decode_kernel(plan, index_ref, *refs):
    n_in = plan.groups * plan.sources
    pieces, w_ref, outs = refs[:n_in], refs[n_in], refs[n_in + 1:-4]
    x_buf, w_buf, x_sem, w_sem = refs[-4:]
    half = plan.tokens // 2
    core = index_ref[0]
    tile = w_buf.shape[2]

    placing = []
    for j in range(plan.groups):
        for b in range(plan.pairs):
            place = index_ref[1 + plan.sources + j * plan.pairs + b] * plan.rows_feat
            for owner in range(2):
                to = pl.multiple_of(place + jnp.where(core == owner, half, 0), ROW_TILE)
                for s in range(plan.sources):
                    placing.append(pltpu.make_async_copy(
                        pieces[s * plan.groups + j].at[
                            pl.ds((2 * b + owner) * plan.rows_feat, plan.rows_feat)
                        ],
                        x_buf.at[
                            pl.ds(to, plan.rows_feat), pl.ds(s * plan.width, plan.width)
                        ],
                        x_sem.at[len(placing)],
                    ))
    for copy in placing:
        copy.start()

    def copies_of(i, slot):
        cols = pl.ds(pl.multiple_of(i * tile, tile), tile)
        return [
            pltpu.make_async_copy(
                w_ref.at[s, 0, :, cols],
                w_buf.at[slot, pl.ds(s * plan.width, plan.width)],
                w_sem.at[slot, s],
            )
            for s in range(plan.sources)
        ]

    def step(i, slot):
        @pl.when(i == 0)
        def _():
            for copy in placing:
                copy.wait()
            for s in range(plan.sources):
                @pl.when(index_ref[1 + s] == 0)
                def _(s=s):
                    x_buf[:, s * plan.width:(s + 1) * plan.width] = jnp.zeros(
                        (plan.tokens, plan.width), BF16
                    )

        cols = pl.ds(pl.multiple_of(i * tile, tile), tile)
        product = jnp.dot(x_buf[...], w_buf[slot], preferred_element_type=F32)
        for c in range(plan.chunks):
            for d in range(plan.depth):
                first = d * plan.rows_feat + c * plan.piece
                to = slice(d * plan.piece, (d + 1) * plan.piece)
                outs[c][to, cols] = product[first:first + plan.piece].astype(BF16)
                outs[plan.chunks + c][to, cols] = product[half + first:half + first + plan.piece]

    streamed(plan.model // tile, w_buf.shape[0], copies_of, step, 1)


def decode(plan, index, pieces, w_dec):
    tile = pick_tile(plan.model, 256)
    shape = (plan.depth * plan.piece, plan.model)
    outs = call(
        partial(decode_kernel, plan),
        "decode",
        [SCALARS] + [ANYWHERE] * len(pieces) + [FAR],
        [jax.ShapeDtypeStruct(shape, BF16)] * plan.chunks
        + [jax.ShapeDtypeStruct(shape, F32)] * plan.chunks,
        [
            pltpu.VMEM((plan.tokens, plan.sources * plan.width), BF16),
            pltpu.VMEM((WEIGHT_SLOTS, plan.sources * plan.width, tile), BF16),
            pltpu.SemaphoreType.DMA((len(pieces) * plan.per_group,)),
            pltpu.SemaphoreType.DMA((WEIGHT_SLOTS, plan.sources)),
        ],
        (index, *pieces, w_dec),
        vmem=MOST_VMEM_BYTES,
    )
    return outs[:plan.chunks], outs[plan.chunks:]


def gradient_kernel(plan, index_ref, *refs):
    n_in = 2 * plan.depth
    errors, w_ref, outs = refs[:n_in], refs[n_in], refs[n_in + 1:-4]
    e_buf, w_buf, e_sem, w_sem = refs[-4:]
    depth = pick_tile(plan.width, 512)
    steps = plan.width // depth
    base = 1 + plan.sources + plan.groups * plan.pairs

    placing = [
        pltpu.make_async_copy(
            errors[i],
            e_buf.at[
                pl.ds(pl.multiple_of(index_ref[base + i] * plan.piece, ROW_TILE), plan.piece)
            ],
            e_sem.at[i],
        )
        for i in range(n_in)
    ]
    for copy in placing:
        copy.start()
    def copies_of(i, slot):
        rows = pl.ds(pl.multiple_of(lax.rem(i, steps) * depth, depth), depth)
        return [pltpu.make_async_copy(
            w_ref.at[lax.div(i, steps), 0, rows], w_buf.at[slot], w_sem.at[slot]
        )]

    half = plan.groups // 2

    def step(i, slot):
        @pl.when(i == 0)
        def _():
            for copy in placing:
                copy.wait()

        source = lax.div(i, steps)
        cols = pl.ds(pl.multiple_of(lax.rem(i, steps) * depth, depth), depth)
        product = lax.dot_general(
            w_buf[slot], e_buf[...], (((1,), (1,)), ((), ())), preferred_element_type=F32
        ).T
        product = jnp.where(index_ref[1 + source] > 0, product, 0.0)
        for lane, (lo, hi) in enumerate(plan.lane_sources):
            first, kept = plan.lanes[lane][0], plan.kept_order(lane)
            away, keep = outs[2 * lane * half:][:half], outs[(2 * lane + 1) * half:][:half]

            @pl.when((source >= lo) & (source < hi))
            def _():
                for p, j in enumerate(kept):
                    far = (j ^ first) * plan.block
                    away[p][source - lo, :, cols] = product[far:far + plan.block].astype(BF16)
                    keep[p][source - lo, :, cols] = product[j * plan.block:(j + 1) * plan.block]

    streamed(plan.sources * steps, w_buf.shape[0], copies_of, step, 3)

    def add_squares(i, total):
        rows = pl.ds(pl.multiple_of(i * ROW_TILE, ROW_TILE), ROW_TILE)
        value = e_buf[rows, :].astype(F32)
        value = value * value
        value = value[:8] + value[8:]
        for col in range(0, plan.model, 128):
            total = total + value[:, col:col + 128]
        return total

    outs[-1][...] = lax.fori_loop(
        0, plan.chunk_rows // ROW_TILE, add_squares, jnp.zeros((8, 128), F32)
    )


def gradient(plan, index, errors, w_dec):
    depth = pick_tile(plan.width, 512)
    half = plan.groups // 2
    out_shape = []
    for lo, hi in plan.lane_sources:
        shape = (hi - lo, plan.block, plan.width)
        out_shape += [jax.ShapeDtypeStruct(shape, BF16)] * half
        out_shape += [jax.ShapeDtypeStruct(shape, F32)] * half
    outs = call(
        partial(gradient_kernel, plan),
        "gradient",
        [SCALARS] + [ANYWHERE] * len(errors) + [FAR],
        out_shape + [jax.ShapeDtypeStruct((8, 128), F32)],
        [
            pltpu.VMEM((plan.chunk_rows, plan.model), BF16),
            pltpu.VMEM((WEIGHT_SLOTS, depth, plan.model), BF16),
            pltpu.SemaphoreType.DMA((len(errors),)),
            pltpu.SemaphoreType.DMA((WEIGHT_SLOTS,)),
        ],
        (index, *errors, w_dec),
    )
    lanes = [outs[2 * i * half:2 * (i + 1) * half] for i in range(len(plan.lanes))]
    return [(lane[:half], lane[half:]) for lane in lanes], outs[-1]


def finish_kernel(plan, chunk, with_previous, *refs):
    lanes = len(plan.lanes)
    out_ref, stage, sem = refs[-3:]
    for lane, (lo, hi) in enumerate(plan.lane_sources):
        for s in range(lo, hi):
            total = refs[lane][s - lo]
            for got in refs[lanes + lane:lanes * (1 + lanes):lanes]:
                total = total + got[s - lo].astype(F32)
            stage[:, s, :] = total
    copies = [
        pltpu.make_async_copy(
            stage.at[pl.ds(b * plan.piece, plan.piece)],
            out_ref.at[pl.ds((b * plan.chunks + chunk) * plan.piece, plan.piece)],
            sem.at[b],
        )
        for b in range(plan.per_group)
    ]
    for copy in copies:
        copy.start()
    for copy in copies:
        copy.wait()


def finish(plan, chunk, kept, got, previous):
    options = {}
    if previous is not None:
        options["input_output_aliases"] = {len(kept) + len(got): 0}
    previous = [] if previous is None else [previous]
    return call(
        partial(finish_kernel, plan, chunk, bool(previous)),
        "finish",
        [NEAR] * (len(kept) + len(got)) + [FAR] * len(previous),
        jax.ShapeDtypeStruct((plan.rows, plan.sources, plan.width), F32),
        [
            pltpu.VMEM((plan.block, plan.sources, plan.width), F32),
            pltpu.SemaphoreType.DMA((plan.per_group,)),
        ],
        (*kept, *got, *previous),
        out_specs=FAR,
        **options,
    )


def per_device(resid, w_enc, b_enc, w_dec, targets, start_layer):
    plan = Plan(resid, w_dec)
    group = lax.axis_index("grp").astype(jnp.int32)
    feat = lax.axis_index("feat").astype(jnp.int32)
    core, level = feat % 2, feat // 2
    groups, feats, chunks = plan.groups, plan.feats, plan.chunks

    feeds = (group >= start_layer[:, 0]).astype(jnp.int32)
    offsets = [
        ((group ^ j) * plan.pairs + b) ^ level
        for j in range(groups)
        for b in range(plan.pairs)
    ]
    places = []
    for other in range(2):
        for d in range(plan.depth):
            owner = level ^ d
            place = ((owner // plan.pairs) ^ group) * plan.pairs + owner % plan.pairs
            places.append(place * 2 + (core ^ other))
    index = jnp.concatenate([core[None], feeds, jnp.stack(offsets), jnp.stack(places)])

    encoded, batches = [], []
    for lo, hi in plan.lane_sources:
        batches.append(range(lo, hi))
        encoded += encode(plan, lo, hi, resid, w_enc, b_enc)
    active = arrange(plan, encoded)

    pieces, arrived, also, forwarded = [], [], [], []
    for batch in batches:
        before, arrived, before_forward, forwarded = arrived, [], also + forwarded, []
        for s in batch:
            bits = plan.lanes[s % len(plan.lanes)]
            mine, = after([encoded[s]], before)
            held = {0: mine}
            for bit in bits:
                old = dict(held)
                for j, x in old.items():
                    if j:
                        x, = after([x], before_forward)
                    held[j | bit] = swap(x, "grp", groups, bit)
            pieces += [held[j] for j in range(groups)]
            arrived.append(held[bits[0]])
            also += [held[bit] for bit in bits[1:]]
            forwarded += [held[j] for j in range(groups) if j & (j - 1)]

    sends, keeps = decode(plan, index, after(pieces, [active]), w_dec)
    recon_parts, errors, first_errors, earlier = [], [], [], []
    for c in range(chunks):
        other = swap(sends[c], "feat", feats, 1)
        held = {
            d: keeps[c][d * plan.piece:(d + 1) * plan.piece]
            + other[d * plan.piece:(d + 1) * plan.piece].astype(F32)
            for d in range(plan.depth)
        }
        for step, bit in enumerate(plan.level_bits):
            away = {d: held.pop(d).astype(BF16) for d in sorted(held, reverse=True) if d & bit}
            wait = earlier if not step else [e[0] for e in errors]
            away = dict(zip(away, after(away.values(), wait)))
            got = {d: swap(x, "feat", feats, 2 * bit) for d, x in away.items()}
            if not step:
                earlier = list(got.values())[:1]
            for d, x in got.items():
                held[d ^ bit] = held[d ^ bit] + x.astype(F32)
        recon_rows, = after([held[0]], [e[0] for e in errors])

        first = feat * plan.rows_feat + c * plan.piece
        own_targets = lax.dynamic_slice_in_dim(targets[0], first, plan.piece, 0)
        difference = recon_rows - own_targets.astype(F32)
        recon_parts.append(recon_rows.astype(BF16))
        error = difference.astype(BF16)
        held = {0: error}
        if c:
            for d in range(plan.depth - 1, 0, -1):
                held[d] = swap(error, "feat", feats, 2 * d)
        else:
            for bit in reversed(plan.level_bits):
                held.update(
                    {d | bit: swap(x, "feat", feats, 2 * bit) for d, x in list(held.items())}
                )
        first_errors.append([held[d] for d in range(1, plan.depth)])
        errors.append([held[d] for d in range(plan.depth)])

    squares = jnp.zeros((8, 128), F32)
    totals, results = [], []
    for c in range(chunks):
        every = after(errors[c], totals[-1:])
        every += [swap(x, "feat", feats, 1) for x in every]
        ready = after(every, [e[0] for e in errors[c + 1:c + 2]])
        lanes, total = gradient(plan, index, ready, w_dec)
        totals.append(total)
        squares = squares + total
        results.append(lanes)

    unfinished, seconds = [], []
    for c, lanes in enumerate(results):
        earlier = [x for each in first_errors[c + 1:c + 2] for x in each]
        first_step = []
        for bits, (away, kept) in zip(plan.lanes, lanes):
            away = after(away, earlier)
            cut = len(away) // 2
            got = [swap(x, "grp", groups, bits[0]) for x in away[:cut]]
            rest = away[cut:] if c + 1 < chunks else after(away[cut:], got[:1])
            got += [swap(x, "grp", groups, bits[0]) for x in rest]
            first_step.append(got)
        wait = totals[c + 1:c + 2]
        if wait:
            wait = wait + [got[-1] for got in first_step]
        second, kept_all = [], []
        for bits, (away, kept), got in zip(plan.lanes, lanes, first_step):
            kept = [[x, after([y], wait)[0]] for x, y in zip(kept, got)]
            for bit in bits[1:]:
                cut = len(kept) // 2
                away = [sum(x.astype(F32) for x in own).astype(BF16) for own in kept[:cut]]
                second += away
                kept = kept[cut:]
                for own, x in zip(kept, away):
                    own.append(swap(x, "grp", groups, bit))
            kept_all.append(kept[0])
        got_all = [own[i] for i in range(1, len(kept_all[0])) for own in kept_all]
        unfinished.append(([own[0] for own in kept_all], got_all))
        seconds.append(second)

    feat_grad = None
    for c, (kept, got) in enumerate(unfinished):
        before_last = feat_grad
        feat_grad = finish(plan, c, kept, got, feat_grad)

    squares, = after([squares], seconds[0])
    loss = jnp.full((8, 128), jnp.sum(squares), F32)
    parts = [loss] + [swap(loss, "grp", groups, j) for j in range(1, groups)]
    parts = after(parts, second + ([] if before_last is None else [before_last]))
    while len(parts) > 1:
        parts = [x + y for x, y in zip(parts[::2], parts[1::2])]
    loss = parts[0]
    entries = targets.shape[0] * groups * plan.tokens * plan.model
    recon_loss = loss[0, 0] / entries
    recon = jnp.concatenate(recon_parts, axis=0)[None]
    return active, recon, recon_loss, feat_grad


def solution(mesh):
    in_specs = (
        P(None, "grp", None),
        P(None, None, "feat"),
        P(None, "feat"),
        P(None, "grp", "feat", None),
        P("grp", None, None),
        P(None, "feat"),
    )
    out_specs = (P("grp", None, "feat"), P("grp", "feat", None), P(), P("grp", None, "feat"))
    return jax.shard_map(
        per_device, mesh=mesh, in_specs=in_specs, out_specs=out_specs, check_vma=False
    )
```

```python
from functools import partial

import jax
import jax.numpy as jnp
from jax import lax
from jax.experimental import pallas as pl
from jax.experimental.pallas import tpu as pltpu
from jax.sharding import PartitionSpec as P

BF16 = jnp.bfloat16
F32 = jnp.float32
WANTED_CHUNKS = 2
ROW_TILE = 16
WEIGHT_SLOTS = 4
IN_FLIGHT = 3
VMEM_BYTES = 44 << 20
MOST_VMEM_BYTES = 59 << 20
SMALL_COST = pl.CostEstimate(flops=1 << 20, bytes_accessed=1 << 10, transcendentals=0)
FAR = pl.BlockSpec(memory_space=pltpu.HBM)
ANYWHERE = pl.BlockSpec(memory_space=pl.ANY)
SCALARS = pl.BlockSpec(memory_space=pltpu.SMEM)
NEAR = pl.BlockSpec(memory_space=pltpu.VMEM)


def pick_tile(size, wanted):
    return wanted if size % wanted == 0 else size


def swap(x, axis, size, offset):
    return lax.ppermute(x, axis, [(i, i ^ offset) for i in range(size)])


def after(values, earlier):
    if not earlier:
        return list(values)
    return list(lax.optimization_barrier(list(values) + list(earlier)))[:len(values)]


class Plan:
    def __init__(self, resid, w_dec):
        self.sources, self.rows, self.model = resid.shape
        self.width = w_dec.shape[2]
        self.groups = lax.axis_size("grp")
        self.feats = lax.axis_size("feat")
        self.depth = self.feats // 2
        self.tokens = self.rows * self.groups
        self.rows_feat = self.tokens // self.feats
        self.per_group = self.rows // self.rows_feat
        self.pairs = self.per_group // 2
        self.chunks = WANTED_CHUNKS
        while self.rows_feat % (self.chunks * ROW_TILE):
            self.chunks -= 1
        self.piece = self.rows_feat // self.chunks
        self.block = self.per_group * self.piece
        self.chunk_rows = self.groups * self.block
        bits = [1 << i for i in range(self.groups.bit_length() - 1)]
        self.lanes = [bits[i:] + bits[:i] for i in range(len(bits))]
        starts = [i * self.sources // len(bits) for i in range(len(bits) + 1)]
        self.lane_sources = list(zip(starts[:-1], starts[1:]))
        self.level_bits = [1 << i for i in range(self.depth.bit_length() - 1)]

    def kept_order(self, lane):
        kept = [0]
        for bit in reversed(self.lanes[lane][1:]):
            kept = [j | bit for j in kept] + kept
        return kept


def streamed(count, slots, copies_of, body, first):
    early = min(first, slots - 1, count)
    for i in range(early):
        for copy in copies_of(i, i):
            copy.start()

    @pl.loop(0, count)
    def _(i):
        ahead = i + slots - 1

        @pl.when(i == 0)
        def _():
            for copy in copies_of(0, 0):
                copy.wait()
            for later in range(early, min(slots, count)):
                for copy in copies_of(later, later):
                    copy.start()

        @pl.when((i > 0) & (ahead < count))
        def _():
            for copy in copies_of(ahead, lax.rem(ahead, slots)):
                copy.start()

        slot = lax.rem(i, slots)

        @pl.when(i > 0)
        def _():
            for copy in copies_of(i, slot):
                copy.wait()

        body(i, slot)


def call(kernel, name, in_specs, out_shape, scratch, args, vmem=VMEM_BYTES, **options):
    return pl.pallas_call(
        kernel,
        in_specs=in_specs,
        out_shape=out_shape,
        scratch_shapes=scratch,
        cost_estimate=SMALL_COST,
        compiler_params=pltpu.CompilerParams(vmem_limit_bytes=vmem),
        name=name,
        **options,
    )(*args)


def encode_kernel(plan, lo, hi, resid_ref, w_ref, b_ref, *refs):
    outs, (x_buf, w_buf, b_buf, total, x_sem, w_sem) = refs[:hi - lo], refs[hi - lo:]
    steps = w_sem.shape[0] // (hi - lo)
    depth = plan.model // steps
    near = [
        pltpu.make_async_copy(resid_ref.at[pl.ds(lo, hi - lo)], x_buf, x_sem.at[0]),
        pltpu.make_async_copy(b_ref, b_buf, x_sem.at[1]),
    ]
    copies = [
        pltpu.make_async_copy(
            w_ref.at[lo + s, pl.ds(i * depth, depth)],
            w_buf.at[s, pl.ds(i * depth, depth)],
            w_sem.at[s * steps + i],
        )
        for s in range(hi - lo)
        for i in range(steps)
    ]
    near[0].start()
    for copy in copies[:IN_FLIGHT]:
        copy.start()
    near[1].start()
    near[0].wait()
    for s in range(hi - lo):
        for i in range(steps):
            step = s * steps + i
            copies[step].wait()
            for copy in copies[step + IN_FLIGHT:step + IN_FLIGHT + 1]:
                copy.start()
            part = slice(i * depth, (i + 1) * depth)
            product = jnp.dot(x_buf[s, :, part], w_buf[s, part, :], preferred_element_type=F32)
            if i:
                product = total[...] + product
            if i < steps - 1:
                total[...] = product
        if not s:
            near[1].wait()
        value = jnp.maximum(product + b_buf[lo + s:lo + s + 1, :], 0.0)
        outs[s][...] = value.astype(BF16)


def encode(plan, lo, hi, resid, w_enc, b_enc):
    n = hi - lo
    steps = plan.model // pick_tile(plan.model, 768)
    return call(
        partial(encode_kernel, plan, lo, hi),
        "encode",
        [FAR, FAR, FAR],
        [jax.ShapeDtypeStruct((plan.rows, plan.width), BF16)] * n,
        [
            pltpu.VMEM((n, plan.rows, plan.model), BF16),
            pltpu.VMEM((n, plan.model, plan.width), BF16),
            pltpu.VMEM((plan.sources, plan.width), F32),
            pltpu.VMEM((plan.rows, plan.width), F32),
            pltpu.SemaphoreType.DMA((2,)),
            pltpu.SemaphoreType.DMA((n * steps,)),
        ],
        (resid, w_enc, b_enc),
        vmem=MOST_VMEM_BYTES,
    )


def arrange_kernel(plan, *refs):
    parts, out_ref, stage = refs[:plan.sources], refs[-2], refs[-1]
    count = stage.shape[0]

    @pl.loop(0, plan.rows // count)
    def _(i):
        rows = pl.ds(pl.multiple_of(i * count, count), count)
        for s in range(plan.sources):
            stage[:, s, :] = parts[s][rows, :].astype(F32)
        out_ref[rows] = stage[...].astype(BF16)


def arrange(plan, encoded):
    return call(
        partial(arrange_kernel, plan),
        "arrange",
        [NEAR] * plan.sources,
        jax.ShapeDtypeStruct((plan.rows, plan.sources, plan.width), BF16),
        [pltpu.VMEM((ROW_TILE, plan.sources, plan.width), F32)],
        encoded,
    )


def decode_kernel(plan, index_ref, *refs):
    n_in = plan.groups * plan.sources
    pieces, w_ref, outs = refs[:n_in], refs[n_in], refs[n_in + 1:-4]
    x_buf, w_buf, x_sem, w_sem = refs[-4:]
    half = plan.tokens // 2
    core = index_ref[0]
    tile = w_buf.shape[2]

    placing = []
    for j in range(plan.groups):
        for b in range(plan.pairs):
            place = index_ref[1 + plan.sources + j * plan.pairs + b] * plan.rows_feat
            for owner in range(2):
                to = pl.multiple_of(place + jnp.where(core == owner, half, 0), ROW_TILE)
                for s in range(plan.sources):
                    placing.append(pltpu.make_async_copy(
                        pieces[s * plan.groups + j].at[
                            pl.ds((2 * b + owner) * plan.rows_feat, plan.rows_feat)
                        ],
                        x_buf.at[
                            pl.ds(to, plan.rows_feat), pl.ds(s * plan.width, plan.width)
                        ],
                        x_sem.at[len(placing)],
                    ))
    for copy in placing:
        copy.start()

    def copies_of(i, slot):
        cols = pl.ds(pl.multiple_of(i * tile, tile), tile)
        return [
            pltpu.make_async_copy(
                w_ref.at[s, 0, :, cols],
                w_buf.at[slot, pl.ds(s * plan.width, plan.width)],
                w_sem.at[slot, s],
            )
            for s in range(plan.sources)
        ]

    def step(i, slot):
        @pl.when(i == 0)
        def _():
            for copy in placing:
                copy.wait()
            for s in range(plan.sources):
                @pl.when(index_ref[1 + s] == 0)
                def _(s=s):
                    x_buf[:, s * plan.width:(s + 1) * plan.width] = jnp.zeros(
                        (plan.tokens, plan.width), BF16
                    )

        cols = pl.ds(pl.multiple_of(i * tile, tile), tile)
        product = jnp.dot(x_buf[...], w_buf[slot], preferred_element_type=F32)
        for c in range(plan.chunks):
            for d in range(plan.depth):
                first = d * plan.rows_feat + c * plan.piece
                to = slice(d * plan.piece, (d + 1) * plan.piece)
                outs[c][to, cols] = product[first:first + plan.piece].astype(BF16)
                outs[plan.chunks + c][to, cols] = product[half + first:half + first + plan.piece]

    streamed(plan.model // tile, w_buf.shape[0], copies_of, step, 2)


def decode(plan, index, pieces, w_dec):
    tile = pick_tile(plan.model, 256)
    shape = (plan.depth * plan.piece, plan.model)
    outs = call(
        partial(decode_kernel, plan),
        "decode",
        [SCALARS] + [ANYWHERE] * len(pieces) + [FAR],
        [jax.ShapeDtypeStruct(shape, BF16)] * plan.chunks
        + [jax.ShapeDtypeStruct(shape, F32)] * plan.chunks,
        [
            pltpu.VMEM((plan.tokens, plan.sources * plan.width), BF16),
            pltpu.VMEM((WEIGHT_SLOTS, plan.sources * plan.width, tile), BF16),
            pltpu.SemaphoreType.DMA((len(pieces) * plan.per_group,)),
            pltpu.SemaphoreType.DMA((WEIGHT_SLOTS, plan.sources)),
        ],
        (index, *pieces, w_dec),
        vmem=MOST_VMEM_BYTES,
    )
    return outs[:plan.chunks], outs[plan.chunks:]


def gradient_kernel(plan, index_ref, *refs):
    n_in = 2 * plan.depth
    errors, w_ref, outs = refs[:n_in], refs[n_in], refs[n_in + 1:-4]
    e_buf, w_buf, e_sem, w_sem = refs[-4:]
    depth = pick_tile(plan.width, 512)
    steps = plan.width // depth
    base = 1 + plan.sources + plan.groups * plan.pairs

    placing = [
        pltpu.make_async_copy(
            errors[i],
            e_buf.at[
                pl.ds(pl.multiple_of(index_ref[base + i] * plan.piece, ROW_TILE), plan.piece)
            ],
            e_sem.at[i],
        )
        for i in range(n_in)
    ]
    for copy in placing:
        copy.start()
    def copies_of(i, slot):
        rows = pl.ds(pl.multiple_of(lax.rem(i, steps) * depth, depth), depth)
        return [pltpu.make_async_copy(
            w_ref.at[lax.div(i, steps), 0, rows], w_buf.at[slot], w_sem.at[slot]
        )]

    half = plan.groups // 2

    def step(i, slot):
        @pl.when(i == 0)
        def _():
            for copy in placing:
                copy.wait()

        source = lax.div(i, steps)
        cols = pl.ds(pl.multiple_of(lax.rem(i, steps) * depth, depth), depth)
        product = lax.dot_general(
            w_buf[slot], e_buf[...], (((1,), (1,)), ((), ())), preferred_element_type=F32
        ).T
        product = jnp.where(index_ref[1 + source] > 0, product, 0.0)
        for lane, (lo, hi) in enumerate(plan.lane_sources):
            first, kept = plan.lanes[lane][0], plan.kept_order(lane)
            away, keep = outs[2 * lane * half:][:half], outs[(2 * lane + 1) * half:][:half]

            @pl.when((source >= lo) & (source < hi))
            def _():
                for p, j in enumerate(kept):
                    far = (j ^ first) * plan.block
                    away[p][source - lo, :, cols] = product[far:far + plan.block].astype(BF16)
                    keep[p][source - lo, :, cols] = product[j * plan.block:(j + 1) * plan.block]

    streamed(plan.sources * steps, w_buf.shape[0], copies_of, step, 3)

    def add_squares(i, total):
        rows = pl.ds(pl.multiple_of(i * ROW_TILE, ROW_TILE), ROW_TILE)
        value = e_buf[rows, :].astype(F32)
        value = value * value
        value = value[:8] + value[8:]
        for col in range(0, plan.model, 128):
            total = total + value[:, col:col + 128]
        return total

    outs[-1][...] = lax.fori_loop(
        0, plan.chunk_rows // ROW_TILE, add_squares, jnp.zeros((8, 128), F32)
    )


def gradient(plan, index, errors, w_dec):
    depth = pick_tile(plan.width, 512)
    half = plan.groups // 2
    out_shape = []
    for lo, hi in plan.lane_sources:
        shape = (hi - lo, plan.block, plan.width)
        out_shape += [jax.ShapeDtypeStruct(shape, BF16)] * half
        out_shape += [jax.ShapeDtypeStruct(shape, F32)] * half
    outs = call(
        partial(gradient_kernel, plan),
        "gradient",
        [SCALARS] + [ANYWHERE] * len(errors) + [FAR],
        out_shape + [jax.ShapeDtypeStruct((8, 128), F32)],
        [
            pltpu.VMEM((plan.chunk_rows, plan.model), BF16),
            pltpu.VMEM((WEIGHT_SLOTS, depth, plan.model), BF16),
            pltpu.SemaphoreType.DMA((len(errors),)),
            pltpu.SemaphoreType.DMA((WEIGHT_SLOTS,)),
        ],
        (index, *errors, w_dec),
    )
    lanes = [outs[2 * i * half:2 * (i + 1) * half] for i in range(len(plan.lanes))]
    return [(lane[:half], lane[half:]) for lane in lanes], outs[-1]


def finish_kernel(plan, chunk, with_previous, *refs):
    lanes = len(plan.lanes)
    out_ref, stage, sem = refs[-3:]
    for lane, (lo, hi) in enumerate(plan.lane_sources):
        for s in range(lo, hi):
            total = refs[lane][s - lo]
            for got in refs[lanes + lane:lanes * (1 + lanes):lanes]:
                total = total + got[s - lo].astype(F32)
            stage[:, s, :] = total
    copies = [
        pltpu.make_async_copy(
            stage.at[pl.ds(b * plan.piece, plan.piece)],
            out_ref.at[pl.ds((b * plan.chunks + chunk) * plan.piece, plan.piece)],
            sem.at[b],
        )
        for b in range(plan.per_group)
    ]
    for copy in copies:
        copy.start()
    for copy in copies:
        copy.wait()


def finish(plan, chunk, kept, got, previous):
    options = {}
    if previous is not None:
        options["input_output_aliases"] = {len(kept) + len(got): 0}
    previous = [] if previous is None else [previous]
    return call(
        partial(finish_kernel, plan, chunk, bool(previous)),
        "finish",
        [NEAR] * (len(kept) + len(got)) + [FAR] * len(previous),
        jax.ShapeDtypeStruct((plan.rows, plan.sources, plan.width), F32),
        [
            pltpu.VMEM((plan.block, plan.sources, plan.width), F32),
            pltpu.SemaphoreType.DMA((plan.per_group,)),
        ],
        (*kept, *got, *previous),
        out_specs=FAR,
        **options,
    )


def per_device(resid, w_enc, b_enc, w_dec, targets, start_layer):
    plan = Plan(resid, w_dec)
    group = lax.axis_index("grp").astype(jnp.int32)
    feat = lax.axis_index("feat").astype(jnp.int32)
    core, level = feat % 2, feat // 2
    groups, feats, chunks = plan.groups, plan.feats, plan.chunks

    feeds = (group >= start_layer[:, 0]).astype(jnp.int32)
    offsets = [
        ((group ^ j) * plan.pairs + b) ^ level
        for j in range(groups)
        for b in range(plan.pairs)
    ]
    places = []
    for other in range(2):
        for d in range(plan.depth):
            owner = level ^ d
            place = ((owner // plan.pairs) ^ group) * plan.pairs + owner % plan.pairs
            places.append(place * 2 + (core ^ other))
    index = jnp.concatenate([core[None], feeds, jnp.stack(offsets), jnp.stack(places)])

    encoded, batches = [], []
    for lo, hi in plan.lane_sources:
        batches.append(range(lo, hi))
        encoded += encode(plan, lo, hi, resid, w_enc, b_enc)
    active = arrange(plan, encoded)

    pieces, arrived, also, forwarded = [], [], [], []
    for batch in batches:
        before, arrived, before_forward, forwarded = arrived, [], also + forwarded, []
        for s in batch:
            bits = plan.lanes[s % len(plan.lanes)]
            mine, = after([encoded[s]], before)
            held = {0: mine}
            for bit in bits:
                old = dict(held)
                for j, x in old.items():
                    if j:
                        x, = after([x], before_forward)
                    held[j | bit] = swap(x, "grp", groups, bit)
            pieces += [held[j] for j in range(groups)]
            arrived.append(held[bits[0]])
            also += [held[bit] for bit in bits[1:]]
            forwarded += [held[j] for j in range(groups) if j & (j - 1)]

    sends, keeps = decode(plan, index, after(pieces, [active]), w_dec)
    recon_parts, errors, first_errors, earlier = [], [], [], []
    for c in range(chunks):
        other = swap(sends[c], "feat", feats, 1)
        held = {
            d: keeps[c][d * plan.piece:(d + 1) * plan.piece]
            + other[d * plan.piece:(d + 1) * plan.piece].astype(F32)
            for d in range(plan.depth)
        }
        for step, bit in enumerate(plan.level_bits):
            away = {d: held.pop(d).astype(BF16) for d in sorted(held, reverse=True) if d & bit}
            wait = earlier if not step else [e[0] for e in errors]
            away = dict(zip(away, after(away.values(), wait)))
            got = {d: swap(x, "feat", feats, 2 * bit) for d, x in away.items()}
            if not step:
                earlier = list(got.values())[:1]
            for d, x in got.items():
                held[d ^ bit] = held[d ^ bit] + x.astype(F32)
        recon_rows, = after([held[0]], [e[0] for e in errors])

        first = feat * plan.rows_feat + c * plan.piece
        own_targets = lax.dynamic_slice_in_dim(targets[0], first, plan.piece, 0)
        difference = recon_rows - own_targets.astype(F32)
        recon_parts.append(recon_rows.astype(BF16))
        error = difference.astype(BF16)
        held = {0: error}
        if c:
            for d in range(plan.depth - 1, 0, -1):
                held[d] = swap(error, "feat", feats, 2 * d)
        else:
            for bit in reversed(plan.level_bits):
                held.update(
                    {d | bit: swap(x, "feat", feats, 2 * bit) for d, x in list(held.items())}
                )
        first_errors.append([held[d] for d in range(1, plan.depth)])
        errors.append([held[d] for d in range(plan.depth)])

    squares = jnp.zeros((8, 128), F32)
    totals, results = [], []
    for c in range(chunks):
        every = after(errors[c], totals[-1:])
        every += [swap(x, "feat", feats, 1) for x in every]
        ready = after(every, [e[0] for e in errors[c + 1:c + 2]])
        lanes, total = gradient(plan, index, ready, w_dec)
        totals.append(total)
        squares = squares + total
        results.append(lanes)

    unfinished = []
    for c, lanes in enumerate(results):
        earlier = [x for each in first_errors[c + 1:c + 2] for x in each]
        first_step = []
        for bits, (away, kept) in zip(plan.lanes, lanes):
            away = after(away, earlier)
            cut = len(away) // 2
            got = [swap(x, "grp", groups, bits[0]) for x in away[:cut]]
            rest = away[cut:] if c + 1 < chunks else after(away[cut:], got[:1])
            got += [swap(x, "grp", groups, bits[0]) for x in rest]
            first_step.append(got)
        wait = totals[c + 1:c + 2]
        if wait:
            wait = wait + [got[-1] for got in first_step]
        second, kept_all = [], []
        for bits, (away, kept), got in zip(plan.lanes, lanes, first_step):
            kept = [[x, after([y], wait)[0]] for x, y in zip(kept, got)]
            for bit in bits[1:]:
                cut = len(kept) // 2
                away = [sum(x.astype(F32) for x in own).astype(BF16) for own in kept[:cut]]
                second += away
                kept = kept[cut:]
                for own, x in zip(kept, away):
                    own.append(swap(x, "grp", groups, bit))
            kept_all.append(kept[0])
        got_all = [own[i] for i in range(1, len(kept_all[0])) for own in kept_all]
        unfinished.append(([own[0] for own in kept_all], got_all))

    feat_grad = None
    for c, (kept, got) in enumerate(unfinished):
        before_last = feat_grad
        feat_grad = finish(plan, c, kept, got, feat_grad)

    arrived = unfinished[0][1][-len(plan.lanes):] if chunks > 1 else []
    squares, = after([squares], arrived + second)
    parts = [squares] + [swap(squares, "grp", groups, j) for j in range(1, groups)]
    parts = after(parts, second + ([] if before_last is None else [before_last]))
    while len(parts) > 1:
        parts = [x + y for x, y in zip(parts[::2], parts[1::2])]
    loss = jnp.sum(parts[0])
    entries = targets.shape[0] * groups * plan.tokens * plan.model
    recon_loss = loss / entries
    recon = jnp.concatenate(recon_parts, axis=0)[None]
    return active, recon, recon_loss, feat_grad


def solution(mesh):
    in_specs = (
        P(None, "grp", None),
        P(None, None, "feat"),
        P(None, "feat"),
        P(None, "grp", "feat", None),
        P("grp", None, None),
        P(None, "feat"),
    )
    out_specs = (P("grp", None, "feat"), P("grp", "feat", None), P(), P("grp", None, "feat"))
    return jax.shard_map(
        per_device, mesh=mesh, in_specs=in_specs, out_specs=out_specs, check_vma=False
    )
```

```python
from functools import partial

import jax
import jax.numpy as jnp
from jax import lax
from jax.experimental import pallas as pl
from jax.experimental.pallas import tpu as pltpu
from jax.sharding import PartitionSpec as P

BF16 = jnp.bfloat16
F32 = jnp.float32
WANTED_CHUNKS = 2
ROW_TILE = 16
WEIGHT_SLOTS = 4
IN_FLIGHT = 3
VMEM_BYTES = 44 << 20
MOST_VMEM_BYTES = 59 << 20
SMALL_COST = pl.CostEstimate(flops=1 << 20, bytes_accessed=1 << 10, transcendentals=0)
FAR = pl.BlockSpec(memory_space=pltpu.HBM)
ANYWHERE = pl.BlockSpec(memory_space=pl.ANY)
SCALARS = pl.BlockSpec(memory_space=pltpu.SMEM)
NEAR = pl.BlockSpec(memory_space=pltpu.VMEM)


def pick_tile(size, wanted):
    return wanted if size % wanted == 0 else size


def swap(x, axis, size, offset):
    return lax.ppermute(x, axis, [(i, i ^ offset) for i in range(size)])


def after(values, earlier):
    if not earlier:
        return list(values)
    return list(lax.optimization_barrier(list(values) + list(earlier)))[:len(values)]


class Plan:
    def __init__(self, resid, w_dec):
        self.sources, self.rows, self.model = resid.shape
        self.width = w_dec.shape[2]
        self.groups = lax.axis_size("grp")
        self.feats = lax.axis_size("feat")
        self.depth = self.feats // 2
        self.tokens = self.rows * self.groups
        self.rows_feat = self.tokens // self.feats
        self.per_group = self.rows // self.rows_feat
        self.pairs = self.per_group // 2
        self.chunks = WANTED_CHUNKS
        while self.rows_feat % (self.chunks * ROW_TILE):
            self.chunks -= 1
        self.piece = self.rows_feat // self.chunks
        self.block = self.per_group * self.piece
        self.chunk_rows = self.groups * self.block
        bits = [1 << i for i in range(self.groups.bit_length() - 1)]
        self.lanes = [bits[i:] + bits[:i] for i in range(len(bits))]
        starts = [i * self.sources // len(bits) for i in range(len(bits) + 1)]
        self.lane_sources = list(zip(starts[:-1], starts[1:]))
        self.level_bits = [1 << i for i in range(self.depth.bit_length() - 1)]

    def kept_order(self, lane):
        kept = [0]
        for bit in reversed(self.lanes[lane][1:]):
            kept = [j | bit for j in kept] + kept
        return kept


def streamed(count, slots, copies_of, body, first):
    early = min(first, slots - 1, count)
    for i in range(early):
        for copy in copies_of(i, i):
            copy.start()

    @pl.loop(0, count)
    def _(i):
        ahead = i + slots - 1

        @pl.when(i == 0)
        def _():
            for copy in copies_of(0, 0):
                copy.wait()
            for later in range(early, min(slots, count)):
                for copy in copies_of(later, later):
                    copy.start()

        @pl.when((i > 0) & (ahead < count))
        def _():
            for copy in copies_of(ahead, lax.rem(ahead, slots)):
                copy.start()

        slot = lax.rem(i, slots)

        @pl.when(i > 0)
        def _():
            for copy in copies_of(i, slot):
                copy.wait()

        body(i, slot)


def call(kernel, name, in_specs, out_shape, scratch, args, vmem=VMEM_BYTES, **options):
    return pl.pallas_call(
        kernel,
        in_specs=in_specs,
        out_shape=out_shape,
        scratch_shapes=scratch,
        cost_estimate=SMALL_COST,
        compiler_params=pltpu.CompilerParams(vmem_limit_bytes=vmem),
        name=name,
        **options,
    )(*args)


def encode_kernel(plan, lo, hi, resid_ref, w_ref, b_ref, *refs):
    outs, (x_buf, w_buf, b_buf, total, x_sem, w_sem) = refs[:hi - lo], refs[hi - lo:]
    steps = w_sem.shape[0] // (hi - lo)
    depth = plan.model // steps
    near = [
        pltpu.make_async_copy(resid_ref.at[pl.ds(lo, hi - lo)], x_buf, x_sem.at[0]),
        pltpu.make_async_copy(b_ref, b_buf, x_sem.at[1]),
    ]
    copies = [
        pltpu.make_async_copy(
            w_ref.at[lo + s, pl.ds(i * depth, depth)],
            w_buf.at[s, pl.ds(i * depth, depth)],
            w_sem.at[s * steps + i],
        )
        for s in range(hi - lo)
        for i in range(steps)
    ]
    near[0].start()
    for copy in copies[:IN_FLIGHT]:
        copy.start()
    near[1].start()
    near[0].wait()
    for s in range(hi - lo):
        for i in range(steps):
            step = s * steps + i
            copies[step].wait()
            for copy in copies[step + IN_FLIGHT:step + IN_FLIGHT + 1]:
                copy.start()
            part = slice(i * depth, (i + 1) * depth)
            product = jnp.dot(x_buf[s, :, part], w_buf[s, part, :], preferred_element_type=F32)
            if i:
                product = total[...] + product
            if i < steps - 1:
                total[...] = product
        if not s:
            near[1].wait()
        value = jnp.maximum(product + b_buf[lo + s:lo + s + 1, :], 0.0)
        outs[s][...] = value.astype(BF16)


def encode(plan, lo, hi, resid, w_enc, b_enc):
    n = hi - lo
    steps = plan.model // pick_tile(plan.model, 768)
    return call(
        partial(encode_kernel, plan, lo, hi),
        "encode",
        [FAR, FAR, FAR],
        [jax.ShapeDtypeStruct((plan.rows, plan.width), BF16)] * n,
        [
            pltpu.VMEM((n, plan.rows, plan.model), BF16),
            pltpu.VMEM((n, plan.model, plan.width), BF16),
            pltpu.VMEM((plan.sources, plan.width), F32),
            pltpu.VMEM((plan.rows, plan.width), F32),
            pltpu.SemaphoreType.DMA((2,)),
            pltpu.SemaphoreType.DMA((n * steps,)),
        ],
        (resid, w_enc, b_enc),
        vmem=MOST_VMEM_BYTES,
    )


def arrange_kernel(plan, *refs):
    parts, out_ref, stage = refs[:plan.sources], refs[-2], refs[-1]
    count = stage.shape[0]

    @pl.loop(0, plan.rows // count)
    def _(i):
        rows = pl.ds(pl.multiple_of(i * count, count), count)
        for s in range(plan.sources):
            stage[:, s, :] = parts[s][rows, :].astype(F32)
        out_ref[rows] = stage[...].astype(BF16)


def arrange(plan, encoded):
    return call(
        partial(arrange_kernel, plan),
        "arrange",
        [NEAR] * plan.sources,
        jax.ShapeDtypeStruct((plan.rows, plan.sources, plan.width), BF16),
        [pltpu.VMEM((ROW_TILE, plan.sources, plan.width), F32)],
        encoded,
    )


def decode_kernel(plan, index_ref, *refs):
    n_in = plan.groups * plan.sources
    pieces, w_ref, outs = refs[:n_in], refs[n_in], refs[n_in + 1:-4]
    x_buf, w_buf, x_sem, w_sem = refs[-4:]
    half = plan.tokens // 2
    core = index_ref[0]
    tile = w_buf.shape[2]

    placing = []
    for j in range(plan.groups):
        for b in range(plan.pairs):
            place = index_ref[1 + plan.sources + j * plan.pairs + b] * plan.rows_feat
            for owner in range(2):
                to = pl.multiple_of(place + jnp.where(core == owner, half, 0), ROW_TILE)
                for s in range(plan.sources):
                    placing.append(pltpu.make_async_copy(
                        pieces[s * plan.groups + j].at[
                            pl.ds((2 * b + owner) * plan.rows_feat, plan.rows_feat)
                        ],
                        x_buf.at[
                            pl.ds(to, plan.rows_feat), pl.ds(s * plan.width, plan.width)
                        ],
                        x_sem.at[len(placing)],
                    ))
    for copy in placing:
        copy.start()

    def copies_of(i, slot):
        cols = pl.ds(pl.multiple_of(i * tile, tile), tile)
        return [
            pltpu.make_async_copy(
                w_ref.at[s, 0, :, cols],
                w_buf.at[slot, pl.ds(s * plan.width, plan.width)],
                w_sem.at[slot, s],
            )
            for s in range(plan.sources)
        ]

    def step(i, slot):
        @pl.when(i == 0)
        def _():
            for copy in placing:
                copy.wait()
            for s in range(plan.sources):
                @pl.when(index_ref[1 + s] == 0)
                def _(s=s):
                    x_buf[:, s * plan.width:(s + 1) * plan.width] = jnp.zeros(
                        (plan.tokens, plan.width), BF16
                    )

        cols = pl.ds(pl.multiple_of(i * tile, tile), tile)
        product = jnp.dot(x_buf[...], w_buf[slot], preferred_element_type=F32)
        for c in range(plan.chunks):
            for d in range(plan.depth):
                first = d * plan.rows_feat + c * plan.piece
                to = slice(d * plan.piece, (d + 1) * plan.piece)
                outs[c][to, cols] = product[first:first + plan.piece].astype(BF16)
                outs[plan.chunks + c][to, cols] = product[half + first:half + first + plan.piece]

    streamed(plan.model // tile, w_buf.shape[0], copies_of, step, 1)


def decode(plan, index, pieces, w_dec):
    tile = pick_tile(plan.model, 256)
    shape = (plan.depth * plan.piece, plan.model)
    outs = call(
        partial(decode_kernel, plan),
        "decode",
        [SCALARS] + [ANYWHERE] * len(pieces) + [FAR],
        [jax.ShapeDtypeStruct(shape, BF16)] * plan.chunks
        + [jax.ShapeDtypeStruct(shape, F32)] * plan.chunks,
        [
            pltpu.VMEM((plan.tokens, plan.sources * plan.width), BF16),
            pltpu.VMEM((WEIGHT_SLOTS, plan.sources * plan.width, tile), BF16),
            pltpu.SemaphoreType.DMA((len(pieces) * plan.per_group,)),
            pltpu.SemaphoreType.DMA((WEIGHT_SLOTS, plan.sources)),
        ],
        (index, *pieces, w_dec),
        vmem=MOST_VMEM_BYTES,
    )
    return outs[:plan.chunks], outs[plan.chunks:]


def gradient_kernel(plan, index_ref, *refs):
    n_in = 2 * plan.depth
    errors, w_ref, outs = refs[:n_in], refs[n_in], refs[n_in + 1:-4]
    e_buf, w_buf, e_sem, w_sem = refs[-4:]
    depth = pick_tile(plan.width, 512)
    steps = plan.width // depth
    base = 1 + plan.sources + plan.groups * plan.pairs

    placing = [
        pltpu.make_async_copy(
            errors[i],
            e_buf.at[
                pl.ds(pl.multiple_of(index_ref[base + i] * plan.piece, ROW_TILE), plan.piece)
            ],
            e_sem.at[i],
        )
        for i in range(n_in)
    ]
    for copy in placing:
        copy.start()
    def copies_of(i, slot):
        rows = pl.ds(pl.multiple_of(lax.rem(i, steps) * depth, depth), depth)
        return [pltpu.make_async_copy(
            w_ref.at[lax.div(i, steps), 0, rows], w_buf.at[slot], w_sem.at[slot]
        )]

    half = plan.groups // 2

    def step(i, slot):
        @pl.when(i == 0)
        def _():
            for copy in placing:
                copy.wait()

        source = lax.div(i, steps)
        cols = pl.ds(pl.multiple_of(lax.rem(i, steps) * depth, depth), depth)
        product = lax.dot_general(
            w_buf[slot], e_buf[...], (((1,), (1,)), ((), ())), preferred_element_type=F32
        ).T
        product = jnp.where(index_ref[1 + source] > 0, product, 0.0)
        for lane, (lo, hi) in enumerate(plan.lane_sources):
            first, kept = plan.lanes[lane][0], plan.kept_order(lane)
            away, keep = outs[2 * lane * half:][:half], outs[(2 * lane + 1) * half:][:half]

            @pl.when((source >= lo) & (source < hi))
            def _():
                for p, j in enumerate(kept):
                    far = (j ^ first) * plan.block
                    away[p][source - lo, :, cols] = product[far:far + plan.block].astype(BF16)
                    keep[p][source - lo, :, cols] = product[j * plan.block:(j + 1) * plan.block]

    streamed(plan.sources * steps, w_buf.shape[0], copies_of, step, 3)

    def add_squares(i, total):
        rows = pl.ds(pl.multiple_of(i * ROW_TILE, ROW_TILE), ROW_TILE)
        value = e_buf[rows, :].astype(F32)
        value = value * value
        value = value[:8] + value[8:]
        for col in range(0, plan.model, 128):
            total = total + value[:, col:col + 128]
        return total

    outs[-1][...] = lax.fori_loop(
        0, plan.chunk_rows // ROW_TILE, add_squares, jnp.zeros((8, 128), F32)
    )


def gradient(plan, index, errors, w_dec):
    depth = pick_tile(plan.width, 512)
    half = plan.groups // 2
    out_shape = []
    for lo, hi in plan.lane_sources:
        shape = (hi - lo, plan.block, plan.width)
        out_shape += [jax.ShapeDtypeStruct(shape, BF16)] * half
        out_shape += [jax.ShapeDtypeStruct(shape, F32)] * half
    outs = call(
        partial(gradient_kernel, plan),
        "gradient",
        [SCALARS] + [ANYWHERE] * len(errors) + [FAR],
        out_shape + [jax.ShapeDtypeStruct((8, 128), F32)],
        [
            pltpu.VMEM((plan.chunk_rows, plan.model), BF16),
            pltpu.VMEM((WEIGHT_SLOTS, depth, plan.model), BF16),
            pltpu.SemaphoreType.DMA((len(errors),)),
            pltpu.SemaphoreType.DMA((WEIGHT_SLOTS,)),
        ],
        (index, *errors, w_dec),
    )
    lanes = [outs[2 * i * half:2 * (i + 1) * half] for i in range(len(plan.lanes))]
    return [(lane[:half], lane[half:]) for lane in lanes], outs[-1]


def finish_kernel(plan, chunk, with_previous, *refs):
    lanes = len(plan.lanes)
    out_ref, stage, sem = refs[-3:]
    for lane, (lo, hi) in enumerate(plan.lane_sources):
        for s in range(lo, hi):
            total = refs[lane][s - lo]
            for got in refs[lanes + lane:lanes * (1 + lanes):lanes]:
                total = total + got[s - lo].astype(F32)
            stage[:, s, :] = total
    copies = [
        pltpu.make_async_copy(
            stage.at[pl.ds(b * plan.piece, plan.piece)],
            out_ref.at[pl.ds((b * plan.chunks + chunk) * plan.piece, plan.piece)],
            sem.at[b],
        )
        for b in range(plan.per_group)
    ]
    for copy in copies:
        copy.start()
    for copy in copies:
        copy.wait()


def finish(plan, chunk, kept, got, previous):
    options = {}
    if previous is not None:
        options["input_output_aliases"] = {len(kept) + len(got): 0}
    previous = [] if previous is None else [previous]
    return call(
        partial(finish_kernel, plan, chunk, bool(previous)),
        "finish",
        [NEAR] * (len(kept) + len(got)) + [FAR] * len(previous),
        jax.ShapeDtypeStruct((plan.rows, plan.sources, plan.width), F32),
        [
            pltpu.VMEM((plan.block, plan.sources, plan.width), F32),
            pltpu.SemaphoreType.DMA((plan.per_group,)),
        ],
        (*kept, *got, *previous),
        out_specs=FAR,
        **options,
    )


def per_device(resid, w_enc, b_enc, w_dec, targets, start_layer):
    plan = Plan(resid, w_dec)
    group = lax.axis_index("grp").astype(jnp.int32)
    feat = lax.axis_index("feat").astype(jnp.int32)
    core, level = feat % 2, feat // 2
    groups, feats, chunks = plan.groups, plan.feats, plan.chunks

    feeds = (group >= start_layer[:, 0]).astype(jnp.int32)
    offsets = [
        ((group ^ j) * plan.pairs + b) ^ level
        for j in range(groups)
        for b in range(plan.pairs)
    ]
    places = []
    for other in range(2):
        for d in range(plan.depth):
            owner = level ^ d
            place = ((owner // plan.pairs) ^ group) * plan.pairs + owner % plan.pairs
            places.append(place * 2 + (core ^ other))
    index = jnp.concatenate([core[None], feeds, jnp.stack(offsets), jnp.stack(places)])

    encoded, batches = [], []
    for lo, hi in plan.lane_sources:
        batches.append(range(lo, hi))
        encoded += encode(plan, lo, hi, resid, w_enc, b_enc)
    active = arrange(plan, encoded)

    pieces, arrived, also, forwarded = [], [], [], []
    for batch in batches:
        before, arrived, before_forward, forwarded = arrived, [], also + forwarded, []
        for s in batch:
            bits = plan.lanes[s % len(plan.lanes)]
            mine, = after([encoded[s]], before)
            held = {0: mine}
            for bit in bits:
                old = dict(held)
                for j, x in old.items():
                    if j:
                        x, = after([x], before_forward)
                    held[j | bit] = swap(x, "grp", groups, bit)
            pieces += [held[j] for j in range(groups)]
            arrived.append(held[bits[0]])
            also += [held[bit] for bit in bits[1:]]
            forwarded += [held[j] for j in range(groups) if j & (j - 1)]

    sends, keeps = decode(plan, index, after(pieces, [active]), w_dec)
    recon_parts, errors, first_errors, earlier = [], [], [], []
    for c in range(chunks):
        other = swap(sends[c], "feat", feats, 1)
        held = {
            d: keeps[c][d * plan.piece:(d + 1) * plan.piece]
            + other[d * plan.piece:(d + 1) * plan.piece].astype(F32)
            for d in range(plan.depth)
        }
        for step, bit in enumerate(plan.level_bits):
            away = {d: held.pop(d).astype(BF16) for d in sorted(held, reverse=True) if d & bit}
            wait = earlier if not step else [e[0] for e in errors]
            away = dict(zip(away, after(away.values(), wait)))
            got = {d: swap(x, "feat", feats, 2 * bit) for d, x in away.items()}
            if not step:
                earlier = list(got.values())[:1]
            for d, x in got.items():
                held[d ^ bit] = held[d ^ bit] + x.astype(F32)
        recon_rows, = after([held[0]], [e[0] for e in errors])

        first = feat * plan.rows_feat + c * plan.piece
        own_targets = lax.dynamic_slice_in_dim(targets[0], first, plan.piece, 0)
        difference = recon_rows - own_targets.astype(F32)
        recon_parts.append(recon_rows.astype(BF16))
        error = difference.astype(BF16)
        held = {0: error}
        if c:
            for d in range(plan.depth - 1, 0, -1):
                held[d] = swap(error, "feat", feats, 2 * d)
        else:
            for bit in reversed(plan.level_bits):
                held.update(
                    {d | bit: swap(x, "feat", feats, 2 * bit) for d, x in list(held.items())}
                )
        first_errors.append([held[d] for d in range(1, plan.depth)])
        errors.append([held[d] for d in range(plan.depth)])

    squares = jnp.zeros((8, 128), F32)
    totals, results = [], []
    for c in range(chunks):
        every = after(errors[c], totals[-1:])
        every += [swap(x, "feat", feats, 1) for x in every]
        ready = after(every, [e[0] for e in errors[c + 1:c + 2]])
        lanes, total = gradient(plan, index, ready, w_dec)
        totals.append(total)
        squares = squares + total
        results.append(lanes)

    unfinished, seconds = [], []
    for c, lanes in enumerate(results):
        earlier = [x for each in first_errors[c + 1:c + 2] for x in each]
        first_step = []
        for bits, (away, kept) in zip(plan.lanes, lanes):
            away = after(away, earlier)
            cut = len(away) // 2
            got = [swap(x, "grp", groups, bits[0]) for x in away[:cut]]
            rest = away[cut:] if c + 1 < chunks else after(away[cut:], got[:1])
            got += [swap(x, "grp", groups, bits[0]) for x in rest]
            first_step.append(got)
        wait = totals[c + 1:c + 2]
        if wait:
            wait = wait + [got[-1] for got in first_step]
        second, kept_all = [], []
        for bits, (away, kept), got in zip(plan.lanes, lanes, first_step):
            kept = [[x, after([y], wait)[0]] for x, y in zip(kept, got)]
            for bit in bits[1:]:
                cut = len(kept) // 2
                away = [sum(x.astype(F32) for x in own).astype(BF16) for own in kept[:cut]]
                second += away
                kept = kept[cut:]
                for own, x in zip(kept, away):
                    own.append(swap(x, "grp", groups, bit))
            kept_all.append(kept[0])
        got_all = [own[i] for i in range(1, len(kept_all[0])) for own in kept_all]
        unfinished.append(([own[0] for own in kept_all], got_all))
        seconds.append(second)

    feat_grad = None
    for c, (kept, got) in enumerate(unfinished):
        before_last = feat_grad
        feat_grad = finish(plan, c, kept, got, feat_grad)

    squares, = after([squares], seconds[0])
    parts = [squares] + [swap(squares, "grp", groups, j) for j in range(1, groups)]
    parts = after(parts, second + ([] if before_last is None else [before_last]))
    while len(parts) > 1:
        parts = [x + y for x, y in zip(parts[::2], parts[1::2])]
    loss = jnp.sum(parts[0])
    entries = targets.shape[0] * groups * plan.tokens * plan.model
    recon_loss = loss / entries
    recon = jnp.concatenate(recon_parts, axis=0)[None]
    return active, recon, recon_loss, feat_grad


def solution(mesh):
    in_specs = (
        P(None, "grp", None),
        P(None, None, "feat"),
        P(None, "feat"),
        P(None, "grp", "feat", None),
        P("grp", None, None),
        P(None, "feat"),
    )
    out_specs = (P("grp", None, "feat"), P("grp", "feat", None), P(), P("grp", None, "feat"))
    return jax.shard_map(
        per_device, mesh=mesh, in_specs=in_specs, out_specs=out_specs, check_vma=False
    )
```

```python
from functools import partial

import jax
import jax.numpy as jnp
from jax import lax
from jax.experimental import pallas as pl
from jax.experimental.pallas import tpu as pltpu
from jax.sharding import PartitionSpec as P

BF16 = jnp.bfloat16
F32 = jnp.float32
WANTED_CHUNKS = 2
ROW_TILE = 16
WEIGHT_SLOTS = 4
IN_FLIGHT = 3
VMEM_BYTES = 44 << 20
MOST_VMEM_BYTES = 59 << 20
DECODE_VMEM_BYTES = 56 << 20
SMALL_COST = pl.CostEstimate(flops=1 << 20, bytes_accessed=1 << 10, transcendentals=0)
FAR = pl.BlockSpec(memory_space=pltpu.HBM)
ANYWHERE = pl.BlockSpec(memory_space=pl.ANY)
SCALARS = pl.BlockSpec(memory_space=pltpu.SMEM)
NEAR = pl.BlockSpec(memory_space=pltpu.VMEM)


def pick_tile(size, wanted):
    return wanted if size % wanted == 0 else size


def swap(x, axis, size, offset):
    return lax.ppermute(x, axis, [(i, i ^ offset) for i in range(size)])


def after(values, earlier):
    if not earlier:
        return list(values)
    return list(lax.optimization_barrier(list(values) + list(earlier)))[:len(values)]


class Plan:
    def __init__(self, resid, w_dec):
        self.sources, self.rows, self.model = resid.shape
        self.width = w_dec.shape[2]
        self.groups = lax.axis_size("grp")
        self.feats = lax.axis_size("feat")
        self.depth = self.feats // 2
        self.tokens = self.rows * self.groups
        self.rows_feat = self.tokens // self.feats
        self.per_group = self.rows // self.rows_feat
        self.pairs = self.per_group // 2
        self.chunks = WANTED_CHUNKS
        while self.rows_feat % (self.chunks * ROW_TILE):
            self.chunks -= 1
        self.piece = self.rows_feat // self.chunks
        self.block = self.per_group * self.piece
        self.chunk_rows = self.groups * self.block
        bits = [1 << i for i in range(self.groups.bit_length() - 1)]
        self.lanes = [bits[i:] + bits[:i] for i in range(len(bits))]
        starts = [i * self.sources // len(bits) for i in range(len(bits) + 1)]
        self.lane_sources = list(zip(starts[:-1], starts[1:]))
        self.level_bits = [1 << i for i in range(self.depth.bit_length() - 1)]

    def kept_order(self, lane):
        kept = [0]
        for bit in reversed(self.lanes[lane][1:]):
            kept = [j | bit for j in kept] + kept
        return kept


def streamed(count, slots, copies_of, body, first):
    early = min(first, slots - 1, count)
    for i in range(early):
        for copy in copies_of(i, i):
            copy.start()

    @pl.loop(0, count)
    def _(i):
        ahead = i + slots - 1

        @pl.when(i == 0)
        def _():
            for copy in copies_of(0, 0):
                copy.wait()
            for later in range(early, min(slots, count)):
                for copy in copies_of(later, later):
                    copy.start()

        @pl.when((i > 0) & (ahead < count))
        def _():
            for copy in copies_of(ahead, lax.rem(ahead, slots)):
                copy.start()

        slot = lax.rem(i, slots)

        @pl.when(i > 0)
        def _():
            for copy in copies_of(i, slot):
                copy.wait()

        body(i, slot)


def call(kernel, name, in_specs, out_shape, scratch, args, vmem=VMEM_BYTES, **options):
    return pl.pallas_call(
        kernel,
        in_specs=in_specs,
        out_shape=out_shape,
        scratch_shapes=scratch,
        cost_estimate=SMALL_COST,
        compiler_params=pltpu.CompilerParams(vmem_limit_bytes=vmem),
        name=name,
        **options,
    )(*args)


def encode_kernel(plan, lo, hi, resid_ref, w_ref, b_ref, *refs):
    outs, (x_buf, w_buf, b_buf, total, x_sem, w_sem) = refs[:hi - lo], refs[hi - lo:]
    steps = w_sem.shape[0] // (hi - lo)
    depth = plan.model // steps
    near = [
        pltpu.make_async_copy(resid_ref.at[pl.ds(lo, hi - lo)], x_buf, x_sem.at[0]),
        pltpu.make_async_copy(b_ref, b_buf, x_sem.at[1]),
    ]
    copies = [
        pltpu.make_async_copy(
            w_ref.at[lo + s, pl.ds(i * depth, depth)],
            w_buf.at[s, pl.ds(i * depth, depth)],
            w_sem.at[s * steps + i],
        )
        for s in range(hi - lo)
        for i in range(steps)
    ]
    near[0].start()
    for copy in copies[:IN_FLIGHT]:
        copy.start()
    near[1].start()
    near[0].wait()
    for s in range(hi - lo):
        for i in range(steps):
            step = s * steps + i
            copies[step].wait()
            for copy in copies[step + IN_FLIGHT:step + IN_FLIGHT + 1]:
                copy.start()
            part = slice(i * depth, (i + 1) * depth)
            product = jnp.dot(x_buf[s, :, part], w_buf[s, part, :], preferred_element_type=F32)
            if i:
                product = total[...] + product
            if i < steps - 1:
                total[...] = product
        if not s:
            near[1].wait()
        value = jnp.maximum(product + b_buf[lo + s:lo + s + 1, :], 0.0)
        outs[s][...] = value.astype(BF16)


def encode(plan, lo, hi, resid, w_enc, b_enc):
    n = hi - lo
    steps = plan.model // pick_tile(plan.model, 768)
    return call(
        partial(encode_kernel, plan, lo, hi),
        "encode",
        [FAR, FAR, FAR],
        [jax.ShapeDtypeStruct((plan.rows, plan.width), BF16)] * n,
        [
            pltpu.VMEM((n, plan.rows, plan.model), BF16),
            pltpu.VMEM((n, plan.model, plan.width), BF16),
            pltpu.VMEM((plan.sources, plan.width), F32),
            pltpu.VMEM((plan.rows, plan.width), F32),
            pltpu.SemaphoreType.DMA((2,)),
            pltpu.SemaphoreType.DMA((n * steps,)),
        ],
        (resid, w_enc, b_enc),
        vmem=MOST_VMEM_BYTES,
    )


def arrange_kernel(plan, *refs):
    parts, out_ref, stage = refs[:plan.sources], refs[-2], refs[-1]
    count = stage.shape[0]

    @pl.loop(0, plan.rows // count)
    def _(i):
        rows = pl.ds(pl.multiple_of(i * count, count), count)
        for s in range(plan.sources):
            stage[:, s, :] = parts[s][rows, :].astype(F32)
        out_ref[rows] = stage[...].astype(BF16)


def arrange(plan, encoded):
    return call(
        partial(arrange_kernel, plan),
        "arrange",
        [NEAR] * plan.sources,
        jax.ShapeDtypeStruct((plan.rows, plan.sources, plan.width), BF16),
        [pltpu.VMEM((ROW_TILE, plan.sources, plan.width), F32)],
        encoded,
    )


def decode_kernel(plan, index_ref, *refs):
    n_in = plan.groups * plan.sources
    pieces, w_ref, outs = refs[:n_in], refs[n_in], refs[n_in + 1:-4]
    x_buf, w_buf, x_sem, w_sem = refs[-4:]
    half = plan.tokens // 2
    core = index_ref[0]
    tile = w_buf.shape[2]

    placing = []
    for j in range(plan.groups):
        for b in range(plan.pairs):
            place = index_ref[1 + plan.sources + j * plan.pairs + b] * plan.rows_feat
            for owner in range(2):
                to = pl.multiple_of(place + jnp.where(core == owner, half, 0), ROW_TILE)
                for s in range(plan.sources):
                    placing.append(pltpu.make_async_copy(
                        pieces[s * plan.groups + j].at[
                            pl.ds((2 * b + owner) * plan.rows_feat, plan.rows_feat)
                        ],
                        x_buf.at[
                            pl.ds(to, plan.rows_feat), pl.ds(s * plan.width, plan.width)
                        ],
                        x_sem.at[len(placing)],
                    ))
    for copy in placing:
        copy.start()

    def copies_of(i, slot):
        cols = pl.ds(pl.multiple_of(i * tile, tile), tile)
        return [
            pltpu.make_async_copy(
                w_ref.at[s, 0, :, cols],
                w_buf.at[slot, pl.ds(s * plan.width, plan.width)],
                w_sem.at[slot, s],
            )
            for s in range(plan.sources)
        ]

    def step(i, slot):
        @pl.when(i == 0)
        def _():
            for copy in placing:
                copy.wait()
            for s in range(plan.sources):
                @pl.when(index_ref[1 + s] == 0)
                def _(s=s):
                    x_buf[:, s * plan.width:(s + 1) * plan.width] = jnp.zeros(
                        (plan.tokens, plan.width), BF16
                    )

        cols = pl.ds(pl.multiple_of(i * tile, tile), tile)
        product = jnp.dot(x_buf[...], w_buf[slot], preferred_element_type=F32)
        for c in range(plan.chunks):
            for d in range(plan.depth):
                first = d * plan.rows_feat + c * plan.piece
                to = slice(d * plan.piece, (d + 1) * plan.piece)
                outs[c][to, cols] = product[first:first + plan.piece].astype(BF16)
                outs[plan.chunks + c][to, cols] = product[half + first:half + first + plan.piece]

    streamed(plan.model // tile, w_buf.shape[0], copies_of, step, 1)


def decode(plan, index, pieces, w_dec):
    tile = pick_tile(plan.model, 256)
    shape = (plan.depth * plan.piece, plan.model)
    outs = call(
        partial(decode_kernel, plan),
        "decode",
        [SCALARS] + [ANYWHERE] * len(pieces) + [FAR],
        [jax.ShapeDtypeStruct(shape, BF16)] * plan.chunks
        + [jax.ShapeDtypeStruct(shape, F32)] * plan.chunks,
        [
            pltpu.VMEM((plan.tokens, plan.sources * plan.width), BF16),
            pltpu.VMEM((WEIGHT_SLOTS, plan.sources * plan.width, tile), BF16),
            pltpu.SemaphoreType.DMA((len(pieces) * plan.per_group,)),
            pltpu.SemaphoreType.DMA((WEIGHT_SLOTS, plan.sources)),
        ],
        (index, *pieces, w_dec),
        vmem=DECODE_VMEM_BYTES,
    )
    return outs[:plan.chunks], outs[plan.chunks:]


def gradient_kernel(plan, index_ref, *refs):
    n_in = 2 * plan.depth
    errors, w_ref, outs = refs[:n_in], refs[n_in], refs[n_in + 1:-4]
    e_buf, w_buf, e_sem, w_sem = refs[-4:]
    depth = pick_tile(plan.width, 512)
    steps = plan.width // depth
    base = 1 + plan.sources + plan.groups * plan.pairs

    placing = [
        pltpu.make_async_copy(
            errors[i],
            e_buf.at[
                pl.ds(pl.multiple_of(index_ref[base + i] * plan.piece, ROW_TILE), plan.piece)
            ],
            e_sem.at[i],
        )
        for i in range(n_in)
    ]
    for copy in placing:
        copy.start()
    def copies_of(i, slot):
        rows = pl.ds(pl.multiple_of(lax.rem(i, steps) * depth, depth), depth)
        return [pltpu.make_async_copy(
            w_ref.at[lax.div(i, steps), 0, rows], w_buf.at[slot], w_sem.at[slot]
        )]

    half = plan.groups // 2

    def step(i, slot):
        @pl.when(i == 0)
        def _():
            for copy in placing:
                copy.wait()

        source = lax.div(i, steps)
        cols = pl.ds(pl.multiple_of(lax.rem(i, steps) * depth, depth), depth)
        product = lax.dot_general(
            w_buf[slot], e_buf[...], (((1,), (1,)), ((), ())), preferred_element_type=F32
        ).T
        product = jnp.where(index_ref[1 + source] > 0, product, 0.0)
        for lane, (lo, hi) in enumerate(plan.lane_sources):
            first, kept = plan.lanes[lane][0], plan.kept_order(lane)
            away, keep = outs[2 * lane * half:][:half], outs[(2 * lane + 1) * half:][:half]

            @pl.when((source >= lo) & (source < hi))
            def _():
                for p, j in enumerate(kept):
                    far = (j ^ first) * plan.block
                    away[p][source - lo, :, cols] = product[far:far + plan.block].astype(BF16)
                    keep[p][source - lo, :, cols] = product[j * plan.block:(j + 1) * plan.block]

    streamed(plan.sources * steps, w_buf.shape[0], copies_of, step, 3)

    def add_squares(i, total):
        rows = pl.ds(pl.multiple_of(i * ROW_TILE, ROW_TILE), ROW_TILE)
        value = e_buf[rows, :].astype(F32)
        value = value * value
        value = value[:8] + value[8:]
        for col in range(0, plan.model, 128):
            total = total + value[:, col:col + 128]
        return total

    outs[-1][...] = lax.fori_loop(
        0, plan.chunk_rows // ROW_TILE, add_squares, jnp.zeros((8, 128), F32)
    )


def gradient(plan, index, errors, w_dec):
    depth = pick_tile(plan.width, 512)
    half = plan.groups // 2
    out_shape = []
    for lo, hi in plan.lane_sources:
        shape = (hi - lo, plan.block, plan.width)
        out_shape += [jax.ShapeDtypeStruct(shape, BF16)] * half
        out_shape += [jax.ShapeDtypeStruct(shape, F32)] * half
    outs = call(
        partial(gradient_kernel, plan),
        "gradient",
        [SCALARS] + [ANYWHERE] * len(errors) + [FAR],
        out_shape + [jax.ShapeDtypeStruct((8, 128), F32)],
        [
            pltpu.VMEM((plan.chunk_rows, plan.model), BF16),
            pltpu.VMEM((WEIGHT_SLOTS, depth, plan.model), BF16),
            pltpu.SemaphoreType.DMA((len(errors),)),
            pltpu.SemaphoreType.DMA((WEIGHT_SLOTS,)),
        ],
        (index, *errors, w_dec),
    )
    lanes = [outs[2 * i * half:2 * (i + 1) * half] for i in range(len(plan.lanes))]
    return [(lane[:half], lane[half:]) for lane in lanes], outs[-1]


def finish_kernel(plan, chunk, with_previous, *refs):
    lanes = len(plan.lanes)
    out_ref, stage, sem = refs[-3:]
    for lane, (lo, hi) in enumerate(plan.lane_sources):
        for s in range(lo, hi):
            total = refs[lane][s - lo]
            for got in refs[lanes + lane:lanes * (1 + lanes):lanes]:
                total = total + got[s - lo].astype(F32)
            stage[:, s, :] = total
    copies = [
        pltpu.make_async_copy(
            stage.at[pl.ds(b * plan.piece, plan.piece)],
            out_ref.at[pl.ds((b * plan.chunks + chunk) * plan.piece, plan.piece)],
            sem.at[b],
        )
        for b in range(plan.per_group)
    ]
    for copy in copies:
        copy.start()
    for copy in copies:
        copy.wait()


def finish(plan, chunk, kept, got, previous):
    options = {}
    if previous is not None:
        options["input_output_aliases"] = {len(kept) + len(got): 0}
    previous = [] if previous is None else [previous]
    return call(
        partial(finish_kernel, plan, chunk, bool(previous)),
        "finish",
        [NEAR] * (len(kept) + len(got)) + [FAR] * len(previous),
        jax.ShapeDtypeStruct((plan.rows, plan.sources, plan.width), F32),
        [
            pltpu.VMEM((plan.block, plan.sources, plan.width), F32),
            pltpu.SemaphoreType.DMA((plan.per_group,)),
        ],
        (*kept, *got, *previous),
        out_specs=FAR,
        **options,
    )


def per_device(resid, w_enc, b_enc, w_dec, targets, start_layer):
    plan = Plan(resid, w_dec)
    group = lax.axis_index("grp").astype(jnp.int32)
    feat = lax.axis_index("feat").astype(jnp.int32)
    core, level = feat % 2, feat // 2
    groups, feats, chunks = plan.groups, plan.feats, plan.chunks

    feeds = (group >= start_layer[:, 0]).astype(jnp.int32)
    offsets = [
        ((group ^ j) * plan.pairs + b) ^ level
        for j in range(groups)
        for b in range(plan.pairs)
    ]
    places = []
    for other in range(2):
        for d in range(plan.depth):
            owner = level ^ d
            place = ((owner // plan.pairs) ^ group) * plan.pairs + owner % plan.pairs
            places.append(place * 2 + (core ^ other))
    index = jnp.concatenate([core[None], feeds, jnp.stack(offsets), jnp.stack(places)])

    encoded, batches = [], []
    for lo, hi in plan.lane_sources:
        batches.append(range(lo, hi))
        encoded += encode(plan, lo, hi, resid, w_enc, b_enc)
    active = arrange(plan, encoded)

    pieces, arrived, also, forwarded = [], [], [], []
    for batch in batches:
        before, arrived, before_forward, forwarded = arrived, [], also + forwarded, []
        for s in batch:
            bits = plan.lanes[s % len(plan.lanes)]
            mine, = after([encoded[s]], before)
            held = {0: mine}
            for bit in bits:
                old = dict(held)
                for j, x in old.items():
                    if j:
                        x, = after([x], before_forward)
                    held[j | bit] = swap(x, "grp", groups, bit)
            pieces += [held[j] for j in range(groups)]
            arrived.append(held[bits[0]])
            also += [held[bit] for bit in bits[1:]]
            forwarded += [held[j] for j in range(groups) if j & (j - 1)]

    sends, keeps = decode(plan, index, after(pieces, [active]), w_dec)
    recon_parts, errors, first_errors, earlier = [], [], [], []
    for c in range(chunks):
        other = swap(sends[c], "feat", feats, 1)
        held = {
            d: keeps[c][d * plan.piece:(d + 1) * plan.piece]
            + other[d * plan.piece:(d + 1) * plan.piece].astype(F32)
            for d in range(plan.depth)
        }
        for step, bit in enumerate(plan.level_bits):
            away = {d: held.pop(d).astype(BF16) for d in sorted(held, reverse=True) if d & bit}
            wait = earlier if not step else [e[0] for e in errors]
            away = dict(zip(away, after(away.values(), wait)))
            got = {d: swap(x, "feat", feats, 2 * bit) for d, x in away.items()}
            if not step:
                earlier = list(got.values())[:1]
            for d, x in got.items():
                held[d ^ bit] = held[d ^ bit] + x.astype(F32)
        recon_rows, = after([held[0]], [e[0] for e in errors])

        first = feat * plan.rows_feat + c * plan.piece
        own_targets = lax.dynamic_slice_in_dim(targets[0], first, plan.piece, 0)
        difference = recon_rows - own_targets.astype(F32)
        recon_parts.append(recon_rows.astype(BF16))
        error = difference.astype(BF16)
        held = {0: error}
        if c:
            for d in range(plan.depth - 1, 0, -1):
                held[d] = swap(error, "feat", feats, 2 * d)
        else:
            for bit in reversed(plan.level_bits):
                held.update(
                    {d | bit: swap(x, "feat", feats, 2 * bit) for d, x in list(held.items())}
                )
        first_errors.append([held[d] for d in range(1, plan.depth)])
        errors.append([held[d] for d in range(plan.depth)])

    squares = jnp.zeros((8, 128), F32)
    totals, results = [], []
    for c in range(chunks):
        every = after(errors[c], totals[-1:])
        every += [swap(x, "feat", feats, 1) for x in every]
        ready = after(every, [e[0] for e in errors[c + 1:c + 2]])
        lanes, total = gradient(plan, index, ready, w_dec)
        totals.append(total)
        squares = squares + total
        results.append(lanes)

    unfinished, seconds = [], []
    for c, lanes in enumerate(results):
        earlier = [x for each in first_errors[c + 1:c + 2] for x in each]
        first_step = []
        for bits, (away, kept) in zip(plan.lanes, lanes):
            away = after(away, earlier)
            cut = len(away) // 2
            got = [swap(x, "grp", groups, bits[0]) for x in away[:cut]]
            rest = away[cut:] if c + 1 < chunks else after(away[cut:], got[:1])
            got += [swap(x, "grp", groups, bits[0]) for x in rest]
            first_step.append(got)
        wait = totals[c + 1:c + 2]
        if wait:
            wait = wait + [got[-1] for got in first_step]
        second, kept_all = [], []
        for bits, (away, kept), got in zip(plan.lanes, lanes, first_step):
            kept = [[x, after([y], wait)[0]] for x, y in zip(kept, got)]
            for bit in bits[1:]:
                cut = len(kept) // 2
                away = [sum(x.astype(F32) for x in own).astype(BF16) for own in kept[:cut]]
                second += away
                kept = kept[cut:]
                for own, x in zip(kept, away):
                    own.append(swap(x, "grp", groups, bit))
            kept_all.append(kept[0])
        got_all = [own[i] for i in range(1, len(kept_all[0])) for own in kept_all]
        unfinished.append(([own[0] for own in kept_all], got_all))
        seconds.append(second)

    feat_grad = None
    for c, (kept, got) in enumerate(unfinished):
        before_last = feat_grad
        feat_grad = finish(plan, c, kept, got, feat_grad)

    squares, = after([squares], seconds[0])
    parts = [squares] + [swap(squares, "grp", groups, j) for j in range(1, groups)]
    parts = after(parts, second + ([] if before_last is None else [before_last]))
    while len(parts) > 1:
        parts = [x + y for x, y in zip(parts[::2], parts[1::2])]
    loss = jnp.sum(parts[0])
    entries = targets.shape[0] * groups * plan.tokens * plan.model
    recon_loss = loss / entries
    recon = jnp.concatenate(recon_parts, axis=0)[None]
    return active, recon, recon_loss, feat_grad


def solution(mesh):
    in_specs = (
        P(None, "grp", None),
        P(None, None, "feat"),
        P(None, "feat"),
        P(None, "grp", "feat", None),
        P("grp", None, None),
        P(None, "feat"),
    )
    out_specs = (P("grp", None, "feat"), P("grp", "feat", None), P(), P("grp", None, "feat"))
    return jax.shard_map(
        per_device, mesh=mesh, in_specs=in_specs, out_specs=out_specs, check_vma=False
    )
```
